32 devices in a mesh: seq: 16 (over z, y, core), tp: 2 (over x).
Axes of the slice: x: 2, y: 2, z: 4, core: 2. Of those that a mesh axis runs over, the one named last changes fastest.
Arguments:
- stream: bfloat16 [2048, 8192], P('seq', 'tp'), may hold values from -6 to 6
- hidden: bfloat16 [14336, 2048], P('seq'), may hold values from -6 to 6
- final_gain: bfloat16 [8192], P('tp'), may hold values from 0.099609375 to 1.8984375
- value_head: bfloat16 [8192], P('tp'), may hold values from -0.0625 to 0.0625
- rewards: float32 [2048], P('seq'), may hold values from -3 to 3
- kl_terms: float32 [2048], P('seq'), may hold values from -6 to 6
- resets: int32 [2048], P('seq'), may hold values 0 or 1
Outputs:
- values: float32 [2048], P('seq')
- returns: float32 [2048], P('seq')
- grad_head: float32 [8192], P('tp')
- grad_down: bfloat16 [14336, 8192], P('seq', 'tp')
The draws below stay inside these ranges and needn't reach their ends.
All inputs are finite; a program needn't handle non-finite values. No bound on the sum of `resets` on one device may be relied on, other than what follows from the above.
Results may differ from the reference program's by a relative error of at most 0.0049.
Values may be sent and summed in bfloat16 or wider, within the bound.
No kernel may reach another device: no remote copies, remote signals or barrier semaphores. Data moves between devices by JAX's collectives and lax.ppermute only.
A program may use at most 64 MiB of HBM per device.

```python
import jax
import jax.numpy as jnp
from jax import lax

D = 8192
FF = 14336
TOKENS = 2048


def with_ends(entries, key, smallest, high):
    extent = entries.shape
    index_at = [jax.random.randint(jax.random.fold_in(key, axis), (), 0, extent[axis]) for axis in range(len(extent))]
    entries = entries.at[tuple(index_at)].set(smallest)
    longest = extent.index(max(extent))
    index_at[longest] = (index_at[longest] + 1) % extent[longest]
    return entries.at[tuple(index_at)].set(high)


def block_levels(key, dims, cuts, smallest, top_value):
    def one(dim, parts):
        heights = jax.random.uniform(jax.random.fold_in(jax.random.fold_in(key, 6), dim), (parts,), jnp.float32, smallest / len(cuts), top_value / len(cuts))
        return jnp.repeat(jnp.exp(heights), dims[dim] // parts).reshape((-1,) + (1,) * (len(dims) - dim - 1))

    factor_of = one(*cuts[0])
    for cut in cuts[1:]:
        factor_of = factor_of * one(*cut)
    return factor_of


def bell_draw(stream_key, shape, spread, most, split=(), dtype=jnp.bfloat16):
    drawn = jax.random.normal(stream_key, shape, jnp.float32) * spread
    if len(split) > 0:
        drawn = block_levels(stream_key, shape, split, -0.22, 0.18) * drawn
    return jnp.clip(drawn, min=-most, max=most).astype(dtype)


def setup_inputs(seed: int = 0) -> dict:
    arg_keys = jax.random.split(jax.random.key(seed), 8)
    return {
        "stream": bell_draw(arg_keys[0], (TOKENS, D), 1.0, 6.0, ((0, 16), (1, 2))),
        "hidden": bell_draw(arg_keys[1], (FF, TOKENS), 1.0, 6.0, ((0, 16),)),
        "final_gain": jnp.clip(1.0 + 0.18 * jax.random.normal(arg_keys[2], (D,), jnp.float32), 0.099609375, 1.8984375).astype(jnp.bfloat16),
        "value_head": bell_draw(arg_keys[3], (D,), D ** -0.5, 0.0625, ((0, 2),)),
        "rewards": bell_draw(arg_keys[4], (TOKENS,), 0.2, 3.0, ((0, 16),), jnp.float32),
        "kl_terms": bell_draw(arg_keys[5], (TOKENS,), 0.5, 6.0, ((0, 16),), jnp.float32),
        "resets": with_ends((jax.random.randint(arg_keys[6], (TOKENS,), 0, 128) < 1).astype(jnp.int32), jax.random.fold_in(arg_keys[6], 1), 0, 1),
    }


epsilon = 1e-05

def reference(stream, hidden, final_gain, value_head, rewards, kl_terms, resets):
    stream_f = stream.astype(jnp.float32)
    head_vector = final_gain.astype(jnp.float32) * value_head.astype(jnp.float32)
    inv_rms = lax.rsqrt(lax.optimization_barrier(jnp.mean(stream_f * stream_f, axis=-1)) + epsilon)
    head_dot = lax.optimization_barrier(jnp.sum(stream_f * head_vector, axis=-1))
    values = inv_rms * head_dot
    step_reward = rewards - 0.2 * kl_terms
    carry_keep = 1.0 - resets.astype(jnp.float32)

    def backward_step(carry, step_item):
        step_value = step_item[0] + step_item[1] * carry
        return (step_value, step_value)
    _, returns = lax.scan(backward_step, jnp.zeros((), jnp.float32), (step_reward, carry_keep), reverse=True)
    value_error = values - returns
    grad_head = final_gain.astype(jnp.float32) * lax.optimization_barrier(jnp.sum((value_error * inv_rms)[:, None] * stream_f, axis=0))
    width = stream.shape[1]
    dstream = (value_error[:, None] * (inv_rms[:, None] * head_vector - (inv_rms ** 3 * head_dot / width)[:, None] * stream_f)).astype(jnp.bfloat16)
    grad_down = jnp.dot(hidden, dstream, preferred_element_type=jnp.float32).astype(jnp.bfloat16)
    return (values, returns, grad_head, grad_down)
```

```python
import jax
import jax.numpy as jnp
from jax import lax
from jax.experimental import pallas as pl
from jax.experimental.pallas import tpu as pltpu
from jax.sharding import PartitionSpec as P

EPSILON = 1e-05


def product_kernel(gathered, hidden, coefs, head, gain, grad_down, grad_head):
    stream_f = gathered[...].astype(jnp.float32)
    error = coefs[:, 0:1]
    scale = coefs[:, 1:2]
    pull = coefs[:, 2:3]
    weight = coefs[:, 3:4]
    dstream = (error * (scale * head[...] - pull * stream_f)).astype(jnp.bfloat16)
    grad_head[...] = gain[...] * jnp.sum(weight * stream_f, axis=0, keepdims=True)
    grad_down[...] = jnp.dot(hidden[...], dstream, preferred_element_type=jnp.float32).astype(jnp.bfloat16)


def product(gathered, hidden, coefs, head, gain):
    tokens, width = gathered.shape
    units = hidden.shape[0]
    tile = min(width, max(128, (1 << 20) // tokens))
    steps = width // tile
    return pl.pallas_call(
        product_kernel,
        grid=(steps,),
        in_specs=[
            pl.BlockSpec((tokens, tile), lambda i: (0, i)),
            pl.BlockSpec((units, tokens), lambda i: (0, 0)),
            pl.BlockSpec((tokens, 4), lambda i: (0, 0)),
            pl.BlockSpec((1, tile), lambda i: (0, i)),
            pl.BlockSpec((1, tile), lambda i: (0, i)),
        ],
        out_specs=[
            pl.BlockSpec((units, tile), lambda i: (0, i)),
            pl.BlockSpec((1, tile), lambda i: (0, i)),
        ],
        out_shape=[
            jax.ShapeDtypeStruct((units, width), jnp.bfloat16),
            jax.ShapeDtypeStruct((1, width), jnp.float32),
        ],
        compiler_params=pltpu.CompilerParams(vmem_limit_bytes=48 * 1024 * 1024),
        cost_estimate=pl.CostEstimate(
            flops=2 * units * tokens * width,
            bytes_accessed=2 * (units * tokens + tokens * width + units * width),
            transcendentals=0,
        ),
    )(gathered, hidden, coefs, head, gain)


def all_returns(step_reward, resets):
    shards, tok = step_reward.shape
    position = jnp.arange(tok)
    before = jnp.cumsum(resets, axis=1) - resets
    total = jnp.sum(resets, axis=1, keepdims=True)
    reach = (position[None, :] >= position[:, None])[None] & (before[:, None, :] == before[:, :, None])
    local = jnp.sum(jnp.where(reach, step_reward[:, None, :], 0.0), axis=2)
    passing = before == total
    blocked = jnp.where(passing[:, 0], 0.0, 1.0)
    upto = jnp.cumsum(blocked)
    ids = jnp.arange(shards)
    open_path = (ids[None, :] > ids[:, None]) & ((upto - blocked)[None, :] == upto[:, None])
    incoming = jnp.sum(jnp.where(open_path, local[None, :, 0], 0.0), axis=1)
    return local + jnp.where(passing, incoming[:, None], 0.0)


def make_body(width, shards, halves):
    def body(stream, hidden, final_gain, value_head, rewards, kl_terms, resets):
        tok = stream.shape[0]
        gathered = lax.all_gather(stream, "seq", axis=0, tiled=True)
        stream_f = stream.astype(jnp.float32)
        gain = final_gain.astype(jnp.float32)
        head = gain * value_head.astype(jnp.float32)
        share = jnp.where(lax.axis_index("tp") == 0, 1.0, 0.0)
        own = jnp.stack(
            [
                jnp.sum(stream_f * stream_f, axis=-1),
                jnp.sum(stream_f * head, axis=-1),
                (rewards - 0.2 * kl_terms) * share,
                resets.astype(jnp.float32) * share,
            ]
        )
        me = lax.axis_index("seq")
        mine = jnp.arange(shards)[:, None, None] == me
        facts = lax.psum(jnp.where(mine, own[None], 0.0), ("seq", "tp"))
        sum_squares, along, step_reward, cut = (facts[:, k] for k in range(4))
        scale = lax.rsqrt(sum_squares / width + EPSILON)
        values = scale * along
        returns = all_returns(step_reward, cut)
        error = values - returns
        pull = scale**3 * along / width
        coefs = jnp.stack([error, scale, pull, error * scale], axis=-1).reshape(shards * tok, 4)
        grad_down, grad_head = product(gathered, hidden, coefs, head[None], gain[None])
        pick = lambda a: lax.dynamic_index_in_dim(a, me, 0, keepdims=False)
        return (pick(values), pick(returns), grad_head[0], grad_down)

    return body


def solution(mesh):
    placed = (P("seq", "tp"), P("seq", None), P("tp"), P("tp"), P("seq"), P("seq"), P("seq"))

    def run(stream, *rest):
        body = make_body(stream.shape[1], mesh.shape["seq"], mesh.shape["tp"])
        return jax.shard_map(
            body,
            mesh=mesh,
            in_specs=placed,
            out_specs=(P("seq"), P("seq"), P("tp"), P("seq", "tp")),
            check_vma=False,
        )(stream, *rest)

    return run
```

```python
import functools

import jax
import jax.numpy as jnp
from jax import lax
from jax.experimental import pallas as pl
from jax.experimental.pallas import tpu as pltpu
from jax.sharding import PartitionSpec as P

EPSILON = 1e-05


def butterfly_sum(x, axis):
    count = lax.axis_size(axis)
    step = 1
    while step < count:
        x = x + lax.ppermute(x, axis, [(i, i ^ step) for i in range(count)])
        step *= 2
    return x


def butterfly_gather(x, axis):
    count = lax.axis_size(axis)
    me = lax.axis_index(axis)
    x = x[None]
    step = 1
    while step < count:
        other = lax.ppermute(x, axis, [(i, i ^ step) for i in range(count)])
        low = (me & step) == 0
        x = jnp.concatenate([jnp.where(low, x, other), jnp.where(low, other, x)])
        step *= 2
    return x


class Paths:
    def __init__(self, count):
        self.count = count
        self.m = count // 4
        self.order = list(range(0, self.m, 2)) + list(range(self.m - 1 - self.m % 2, 0, -2))
        self.place = [self.order.index(z) for z in range(self.m)]

    def ring(self, by):
        pairs = []
        for i in range(self.count):
            z, rest = divmod(i, 4)
            pairs.append((i, self.order[(self.place[z] + by) % self.m] * 4 + rest))
        return pairs

    def across(self):
        return [(i, i ^ 2) for i in range(self.count)]

    def core(self):
        return [(i, i ^ 1) for i in range(self.count)]

    def owners(self, me):
        place = jnp.array(self.place, jnp.int32)[me // 4]
        offsets = jnp.arange(self.m, dtype=jnp.int32)
        z = jnp.array(self.order, jnp.int32)[(place - offsets) % self.m]
        rest = (me % 4) ^ jnp.array([0, 1, 2, 3], jnp.int32)
        return (z[:, None] * 4 + rest[None, :]).reshape(-1)


def gather_blocks(stream, paths):
    half = stream.shape[1] // 2
    go = lambda x, pairs: lax.ppermute(x, "seq", pairs)
    m = paths.m
    left = {0: stream[:, :half]}
    right = {0: stream[:, half:]}
    for k in range(1, m):
        left[k] = go(left[k - 1], paths.ring(1))
        right[m - k] = go(right[(m - k + 1) % m], paths.ring(-1))
    over = go(stream, paths.across())
    blocks = [[stream, go(stream, paths.core()), over, go(over, paths.core())]]
    for j in range(1, m):
        pair = [left[j], right[j]]
        over = [go(x, paths.across()) for x in pair]
        blocks.append([pair, [go(x, paths.core()) for x in pair], over, [go(x, paths.core()) for x in over]])
    return blocks


def product_kernel(wide, owners, hidden, coefs, head, gain, *refs):
    blocks, (grad_down, grad_head, dstream) = refs[:-3], refs[-3:]
    tok = blocks[0].shape[0]
    side = pl.program_id(0)

    def fill(picked):
        total = jnp.zeros((8, dstream.shape[1]), jnp.float32)
        for b, ref in enumerate(picked):
            rows = pl.ds(pl.multiple_of(owners[b] * tok, tok), tok)
            stream_f = ref[...].astype(jnp.float32)
            coef = coefs[rows, :]
            error, scale, pull, weight = (coef[:, k : k + 1] for k in range(4))
            dstream[rows, :] = (error * (scale * head[...] - pull * stream_f)).astype(jnp.bfloat16)
            total += jnp.sum((weight * stream_f).reshape(tok // 8, 8, -1), axis=0)
        grad_head[...] = gain[...] * jnp.sum(total, axis=0, keepdims=True)

    for s in range(2):

        @pl.when(side == s)
        def _():
            fill(list(blocks[:wide]) + list(blocks[wide + s :: 2]))

    grad_down[...] = jnp.dot(hidden[...], dstream[...], preferred_element_type=jnp.float32).astype(jnp.bfloat16)


def product(blocks, owners, hidden, coefs, head, gain):
    wide = list(blocks[0])
    halves = [x for row in blocks[1:] for pair in row for x in pair]
    tok, width = wide[0].shape
    units, tokens = hidden.shape
    tile = min(width // 2, max(128, (1 << 20) // tokens))
    steps = width // 2 // tile
    at = lambda s, i, *_: (0, s * steps + i)
    half_at = [
        lambda s, i, *_: (0, jnp.where(s == 0, i, steps - 1)),
        lambda s, i, *_: (0, jnp.where(s == 0, 0, i)),
    ]
    whole = lambda s, i, *_: (0, 0)
    return pl.pallas_call(
        functools.partial(product_kernel, len(wide)),
        grid_spec=pltpu.PrefetchScalarGridSpec(
            num_scalar_prefetch=1,
            grid=(2, steps),
            in_specs=[
                pl.BlockSpec((units, tokens), whole),
                pl.BlockSpec((tokens, 4), whole),
                pl.BlockSpec((1, tile), at),
                pl.BlockSpec((1, tile), at),
            ]
            + [pl.BlockSpec((tok, tile), at)] * len(wide)
            + [pl.BlockSpec((tok, tile), half_at[k % 2]) for k in range(len(halves))],
            out_specs=[pl.BlockSpec((units, tile), at), pl.BlockSpec((1, tile), at)],
            scratch_shapes=[pltpu.VMEM((tokens, tile), jnp.bfloat16)],
        ),
        out_shape=[
            jax.ShapeDtypeStruct((units, width), jnp.bfloat16),
            jax.ShapeDtypeStruct((1, width), jnp.float32),
        ],
        compiler_params=pltpu.CompilerParams(vmem_limit_bytes=44 * 1024 * 1024),
        cost_estimate=pl.CostEstimate(
            flops=2 * units * tokens * width,
            bytes_accessed=2 * (units * tokens + tokens * width + units * width),
            transcendentals=0,
        ),
    )(owners, hidden, coefs, head, gain, *wide, *halves)


def all_returns(step_reward, resets):
    shards, tok = step_reward.shape
    position = jnp.arange(tok)
    before = jnp.cumsum(resets, axis=1) - resets
    total = jnp.sum(resets, axis=1, keepdims=True)
    reach = (position[None, :] >= position[:, None])[None] & (before[:, None, :] == before[:, :, None])
    local = jnp.sum(jnp.where(reach, step_reward[:, None, :], 0.0), axis=2)
    passing = before == total
    blocked = jnp.where(passing[:, 0], 0.0, 1.0)
    upto = jnp.cumsum(blocked)
    ids = jnp.arange(shards)
    open_path = (ids[None, :] > ids[:, None]) & ((upto - blocked)[None, :] == upto[:, None])
    incoming = jnp.sum(jnp.where(open_path, local[None, :, 0], 0.0), axis=1)
    return local + jnp.where(passing, incoming[:, None], 0.0)


def make_body(width, shards):
    paths = Paths(shards)

    def body(stream, hidden, final_gain, value_head, rewards, kl_terms, resets):
        tok = stream.shape[0]
        me = lax.axis_index("seq")
        blocks = gather_blocks(stream, paths)
        stream_f = stream.astype(jnp.float32)
        gain = final_gain.astype(jnp.float32)
        head = gain * value_head.astype(jnp.float32)
        sums = jnp.stack([jnp.sum(stream_f * stream_f, axis=-1), jnp.sum(stream_f * head, axis=-1)])
        sums = butterfly_sum(sums, "tp")
        steps = jnp.stack([rewards - 0.2 * kl_terms, resets.astype(jnp.float32)])
        facts = butterfly_gather(jnp.concatenate([sums, steps]), "seq")
        sum_squares, along, step_reward, cut = (facts[:, k] for k in range(4))
        scale = lax.rsqrt(sum_squares / width + EPSILON)
        values = scale * along
        returns = all_returns(step_reward, cut)
        error = values - returns
        pull = scale**3 * along / width
        coefs = jnp.stack([error, scale, pull, error * scale], axis=-1).reshape(shards * tok, 4)
        grad_down, grad_head = product(blocks, paths.owners(me), hidden, coefs, head[None], gain[None])
        pick = lambda a: lax.dynamic_index_in_dim(a, me, 0, keepdims=False)
        return (pick(values), pick(returns), grad_head[0], grad_down)

    return body


def solution(mesh):
    placed = (P("seq", "tp"), P("seq", None), P("tp"), P("tp"), P("seq"), P("seq"), P("seq"))

    def run(stream, *rest):
        return jax.shard_map(
            make_body(stream.shape[1], mesh.shape["seq"]),
            mesh=mesh,
            in_specs=placed,
            out_specs=(P("seq"), P("seq"), P("tp"), P("seq", "tp")),
            check_vma=False,
        )(stream, *rest)

    return run
```

```python
import functools

import jax
import jax.numpy as jnp
from jax import lax
from jax.experimental import pallas as pl
from jax.experimental.pallas import tpu as pltpu
from jax.sharding import PartitionSpec as P

EPSILON = 1e-05


def butterfly_sum(x, axis):
    count = lax.axis_size(axis)
    step = 1
    while step < count:
        x = x + lax.ppermute(x, axis, [(i, i ^ step) for i in range(count)])
        step *= 2
    return x


def butterfly_gather(x, axis, step, stop):
    count = lax.axis_size(axis)
    me = lax.axis_index(axis)
    while step < min(stop, count):
        other = lax.ppermute(x, axis, [(i, i ^ step) for i in range(count)])
        low = (me & step) == 0
        x = jnp.concatenate([jnp.where(low, x, other), jnp.where(low, other, x)])
        step *= 2
    return x


class Paths:
    def __init__(self, count):
        self.count = count
        self.m = count // 4
        self.order = list(range(0, self.m, 2)) + list(range(self.m - 1 - self.m % 2, 0, -2))
        self.place = [self.order.index(z) for z in range(self.m)]

    def ring(self, by):
        pairs = []
        for i in range(self.count):
            z, rest = divmod(i, 4)
            pairs.append((i, self.order[(self.place[z] + by) % self.m] * 4 + rest))
        return pairs

    def across(self):
        return [(i, i ^ 2) for i in range(self.count)]

    def core(self):
        return [(i, i ^ 1) for i in range(self.count)]

    def owners(self, me):
        place = jnp.array(self.place, jnp.int32)[me // 4]
        offsets = jnp.arange(self.m, dtype=jnp.int32)
        z = jnp.array(self.order, jnp.int32)[(place - offsets) % self.m]
        rest = (me % 4) ^ jnp.array([0, 1, 2, 3], jnp.int32)
        return (z[:, None] * 4 + rest[None, :]).reshape(-1)


def gate(arrays):
    return list(lax.optimization_barrier(tuple(arrays)))


def gather_blocks(stream, own_facts, paths):
    half = stream.shape[1] // 2
    go = lambda x, pairs: lax.ppermute(x, "seq", pairs)
    ring = (paths.ring(1), paths.ring(-1))
    m = paths.m
    near, over = {}, {}
    twin_near, twin_over = {}, {}
    near[0, 0], near[0, 1] = (stream, 0), (stream, 1)

    def unpack(joined, k):
        twin_over[k - 1, 0], twin_over[k - 1, 1] = (joined, 0), (joined, 1)
        if k < m:
            twin_near[k, 0], twin_near[k, 1] = (joined, 2), (joined, 3)

    across = [go(stream, paths.across())]
    core = go(stream, paths.core())
    tips = [go(stream[:, :half], ring[0]), go(stream[:, half:], ring[1])]
    facts = butterfly_gather(own_facts(), "seq", 1, 2)
    *tips, across[0], core, facts = gate([*tips, *across, core, facts])
    over[0, 0], over[0, 1] = (across[0], 0), (across[0], 1)
    twin_near[0, 0], twin_near[0, 1] = (core, 0), (core, 1)
    waiting = []
    for k in range(1, m + 1):
        waiting.append((k, jnp.concatenate(across + (tips if k < m else []), axis=1)))
        flights = []
        if k < m - 1:
            flights += [go(tips[side], ring[side]) for side in range(2)]
        if k < m - 1:
            flights += [go(tips[side], paths.across()) for side in range(2)]
        elif k == m - 1:
            flights += [go(over[k - 1, 0][0], ring[0]), go(tips[1], paths.across())]
        sent = []
        if k > 1:
            limit = 1 if k < m - 1 else len(waiting)
            sent, waiting = waiting[:limit], waiting[limit:]
            flights += [go(x, paths.core()) for _, x in sent]
        stop = 2 << k if k < m else paths.count
        flights.append(butterfly_gather(facts, "seq", 1 << k, stop))
        if k < m:
            near[k, 0], near[k, 1] = (tips[0], 0), (tips[1], 0)
        got = gate(flights)
        facts = got.pop()
        for phase, _ in sent[::-1]:
            unpack(got.pop(), phase)
        if k < m:
            across = got[-2:]
            over[k, 0], over[k, 1] = (across[0], 0), (across[1], 0)
            tips = got[:-2]
    blocks = [[], []]
    for j in range(m):
        for side, steps in ((0, j), (1, (m - j) % m)):
            for kind in (near, twin_near, over, twin_over):
                blocks[side].append(kind[steps, side])
    return blocks, facts


def product_kernel(count, owners, hidden, coefs, head, gain, *refs):
    blocks, (grad_down, grad_head, dstream) = refs[:-3], refs[-3:]
    tok = blocks[0].shape[0]
    side = pl.program_id(0)

    def fill(picked):
        total = jnp.zeros((8, dstream.shape[1]), jnp.float32)
        for b, ref in enumerate(picked):
            rows = pl.ds(pl.multiple_of(owners[b] * tok, tok), tok)
            stream_f = ref[...].astype(jnp.float32)
            coef = coefs[rows, :]
            error, scale, pull, weight = (coef[:, k : k + 1] for k in range(4))
            dstream[rows, :] = (error * (scale * head[...] - pull * stream_f)).astype(jnp.bfloat16)
            total += jnp.sum((weight * stream_f).reshape(tok // 8, 8, -1), axis=0)
        grad_head[...] = gain[...] * jnp.sum(total, axis=0, keepdims=True)

    for s in range(2):

        @pl.when(side == s)
        def _():
            fill(blocks[s * count : (s + 1) * count])

    grad_down[...] = jnp.dot(hidden[...], dstream[...], preferred_element_type=jnp.float32).astype(jnp.bfloat16)


def product(blocks, owners, hidden, coefs, head, gain):
    count = len(blocks[0])
    units, tokens = hidden.shape
    width = head.shape[1]
    tok = tokens // count
    tile = min(width // 2, max(128, (1 << 20) // tokens))
    steps = width // 2 // tile
    at = lambda s, i, *_: (0, s * steps + i)
    whole = lambda s, i, *_: (0, 0)

    def block_at(side, offset):
        if side == 0:
            return lambda s, i, *_: (0, offset * steps + jnp.where(s == 0, i, steps - 1))
        return lambda s, i, *_: (0, offset * steps + jnp.where(s == 0, 0, i))

    return pl.pallas_call(
        functools.partial(product_kernel, count),
        grid_spec=pltpu.PrefetchScalarGridSpec(
            num_scalar_prefetch=1,
            grid=(2, steps),
            in_specs=[
                pl.BlockSpec((units, tokens), whole),
                pl.BlockSpec((tokens, 4), whole),
                pl.BlockSpec((1, tile), at),
                pl.BlockSpec((1, tile), at),
            ]
            + [pl.BlockSpec((tok, tile), block_at(side, offset)) for side in range(2) for _, offset in blocks[side]],
            out_specs=[pl.BlockSpec((units, tile), at), pl.BlockSpec((1, tile), at)],
            scratch_shapes=[pltpu.VMEM((tokens, tile), jnp.bfloat16)],
        ),
        out_shape=[
            jax.ShapeDtypeStruct((units, width), jnp.bfloat16),
            jax.ShapeDtypeStruct((1, width), jnp.float32),
        ],
        compiler_params=pltpu.CompilerParams(vmem_limit_bytes=44 * 1024 * 1024),
        cost_estimate=pl.CostEstimate(
            flops=2 * units * tokens * width,
            bytes_accessed=2 * (units * tokens + tokens * width + units * width),
            transcendentals=0,
        ),
    )(owners, hidden, coefs, head, gain, *[array for side in blocks for array, _ in side])


def all_returns(step_reward, resets):
    shards, tok = step_reward.shape
    position = jnp.arange(tok)
    before = jnp.cumsum(resets, axis=1) - resets
    total = jnp.sum(resets, axis=1, keepdims=True)
    reach = (position[None, :] >= position[:, None])[None] & (before[:, None, :] == before[:, :, None])
    local = jnp.sum(jnp.where(reach, step_reward[:, None, :], 0.0), axis=2)
    passing = before == total
    blocked = jnp.where(passing[:, 0], 0.0, 1.0)
    upto = jnp.cumsum(blocked)
    ids = jnp.arange(shards)
    open_path = (ids[None, :] > ids[:, None]) & ((upto - blocked)[None, :] == upto[:, None])
    incoming = jnp.sum(jnp.where(open_path, local[None, :, 0], 0.0), axis=1)
    return local + jnp.where(passing, incoming[:, None], 0.0)


def make_body(width, shards):
    paths = Paths(shards)

    def body(stream, hidden, final_gain, value_head, rewards, kl_terms, resets):
        tok = stream.shape[0]
        me = lax.axis_index("seq")
        stream_f = stream.astype(jnp.float32)
        gain = final_gain.astype(jnp.float32)
        head = gain * value_head.astype(jnp.float32)
        sums = jnp.stack([jnp.sum(stream_f * stream_f, axis=-1), jnp.sum(stream_f * head, axis=-1)])
        steps = jnp.stack([rewards - 0.2 * kl_terms, resets.astype(jnp.float32)])
        own_facts = lambda: jnp.concatenate([butterfly_sum(sums, "tp"), steps])[None]
        blocks, facts = gather_blocks(stream, own_facts, paths)
        sum_squares, along, step_reward, cut = (facts[:, k] for k in range(4))
        scale = lax.rsqrt(sum_squares / width + EPSILON)
        values = scale * along
        returns = all_returns(step_reward, cut)
        error = values - returns
        pull = scale**3 * along / width
        coefs = jnp.stack([error, scale, pull, error * scale], axis=-1).reshape(shards * tok, 4)
        grad_down, grad_head = product(blocks, paths.owners(me), hidden, coefs, head[None], gain[None])
        pick = lambda a: lax.dynamic_index_in_dim(a, me, 0, keepdims=False)
        return (pick(values), pick(returns), grad_head[0], grad_down)

    return body


def solution(mesh):
    placed = (P("seq", "tp"), P("seq", None), P("tp"), P("tp"), P("seq"), P("seq"), P("seq"))

    def run(stream, *rest):
        return jax.shard_map(
            make_body(stream.shape[1], mesh.shape["seq"]),
            mesh=mesh,
            in_specs=placed,
            out_specs=(P("seq"), P("seq"), P("tp"), P("seq", "tp")),
            check_vma=False,
        )(stream, *rest)

    return run
```

```python
import functools

import jax
import jax.numpy as jnp
from jax import lax
from jax.experimental import pallas as pl
from jax.experimental.pallas import tpu as pltpu
from jax.sharding import PartitionSpec as P

EPSILON = 1e-05


def butterfly_sum(x, axis):
    count = lax.axis_size(axis)
    step = 1
    while step < count:
        x = x + lax.ppermute(x, axis, [(i, i ^ step) for i in range(count)])
        step *= 2
    return x


def butterfly_step(x, axis):
    count = lax.axis_size(axis)
    step = x.shape[0]
    if step >= count:
        return x
    other = lax.ppermute(x, axis, [(i, i ^ step) for i in range(count)])
    low = (lax.axis_index(axis) & step) == 0
    return jnp.concatenate([jnp.where(low, x, other), jnp.where(low, other, x)])


class Paths:
    def __init__(self, count):
        self.count = count
        self.m = count // 4
        self.order = list(range(0, self.m, 2)) + list(range(self.m - 1 - self.m % 2, 0, -2))
        self.place = [self.order.index(z) for z in range(self.m)]
        self.across = [(i, i ^ 2) for i in range(count)]
        self.core = [(i, i ^ 1) for i in range(count)]
        self.ring = [self._ring(1), self._ring(-1)]

    def _ring(self, way):
        pairs = []
        for i in range(self.count):
            z, rest = divmod(i, 4)
            by = way if i % 2 == 0 else -way
            pairs.append((i, self.order[(self.place[z] + by) % self.m] * 4 + rest))
        return pairs

    def owner(self, me, block):
        steps, across, kind = block
        place = jnp.array(self.place, jnp.int32)[me // 4]
        way = jnp.where((me % 2 == 0) == (kind == 0), -1, 1)
        z = jnp.array(self.order, jnp.int32)[(place + way * steps) % self.m]
        return z * 4 + (me % 4 ^ (2 * across + kind))


class Flights:
    def __init__(self, **arrays):
        self.have = arrays

    def event(self, waits, sends=()):
        names = list(dict.fromkeys([*waits, *(source for _, source, _ in sends)]))
        self.have.update(zip(names, lax.optimization_barrier(tuple(self.have[n] for n in names))))
        for name, source, pairs in sends:
            self.have[name] = lax.ppermute(self.have[source], "seq", pairs)


def early_blocks(m):
    return [(k, a, kind) for k in range(m - 1) for a in range(2) for kind in range(2) if k < m - 2 or a == 0]


def late_blocks(m):
    return [(m - 2, 1, 0), (m - 2, 1, 1)] + [(m - 1, a, kind) for a in range(2) for kind in range(2)]


def run_plan(stream, hidden, core_index, own_facts, paths, early_own, early_other):
    half = stream.shape[1] // 2
    m, ring, across, core = paths.m, paths.ring, paths.across, paths.core
    cut = lambda c: lax.dynamic_slice_in_dim(stream, c * half, half, 1)
    f = Flights(hidden=hidden, stream=stream, away=cut(1 - core_index))
    f.have[0, 0, 0] = cut(core_index)
    have = f.have

    def facts_step():
        have["facts"] = butterfly_step(have["facts"], "seq")

    f.event([], [((1, 0, 0), (0, 0, 0), ring[0]), ((0, 1, 0), (0, 0, 0), across), ((0, 0, 1), "away", core), ("other hidden", "hidden", core)])
    f.event(
        [(0, 0, 1), "stream"],
        [((1, 0, 1), (0, 0, 1), ring[1]), ((0, 1, 1), (0, 0, 1), across)],
    )
    have["sums"] = own_facts(have["stream"])
    f.event([(1, 0, 0), (0, 1, 0), "sums", "other hidden"], [((2, 0, 0), (1, 0, 0), ring[0]), ((1, 1, 0), (1, 0, 0), across)])
    have["facts"] = butterfly_sum(have["sums"], "tp")[None]
    facts_step()
    f.event([(1, 0, 1), (0, 1, 1), "facts"], [((2, 0, 1), (1, 0, 1), ring[1]), ((1, 1, 1), (1, 0, 1), across)])
    for k in range(2, m):
        for kind in range(2):
            facts_step()
            if k < m - 1:
                sends = [((k + 1, 0, kind), (k, 0, kind), ring[kind]), ((k, 1, kind), (k, 0, kind), across)]
            elif kind == 0:
                sends = [((k, 1, kind), (k - 1, 1, kind), ring[kind])]
            else:
                sends = [((k, 1, kind), (k, 0, kind), across)]
            waits = [(k, 0, kind), (k - 1, 1, kind), "facts"]
            if k == m - 1 and kind == 1:
                waits.append("early own")
            f.event(waits, sends)
            if k == m - 1 and kind == 0:
                while have["facts"].shape[0] < paths.count:
                    facts_step()
                blocks = early_blocks(m)
                have["early own"], have["early dstream"], have["early parts"] = early_own(
                    have["facts"], blocks, [have[b] for b in blocks]
                )
    have["early other"] = early_other(have["early dstream"], have["other hidden"])
    f.event([(m - 1, 1, 0), (m - 1, 1, 1), "early other"])
    return have


PARAMS = pltpu.CompilerParams(vmem_limit_bytes=56 * 1024 * 1024)


def cost(units, k, width, extra):
    return pl.CostEstimate(
        flops=2 * units * k * width, bytes_accessed=2 * (units * k + k * width) + extra, transcendentals=0
    )


def pick_kernel(owners, hidden, picked):
    picked[...] = hidden[...]


def pick(hidden, owners, tok):
    units = hidden.shape[0]
    count = owners.shape[0]
    return pl.pallas_call(
        pick_kernel,
        grid_spec=pltpu.PrefetchScalarGridSpec(
            num_scalar_prefetch=1,
            grid=(count,),
            in_specs=[pl.BlockSpec((units, tok), lambda b, owners: (0, owners[b]))],
            out_specs=pl.BlockSpec((units, tok), lambda b, owners: (0, b)),
        ),
        out_shape=jax.ShapeDtypeStruct((units, count * tok), hidden.dtype),
        compiler_params=PARAMS,
        cost_estimate=cost(units, 0, 0, 4 * units * count * tok),
    )(owners, hidden)


def form(owners, coefs, head, blocks, dstream, parts):
    tok = blocks[0].shape[0]
    parts[...] = jnp.zeros_like(parts)
    for b, ref in enumerate(blocks):
        owner = owners[b]
        rows = pl.ds(pl.multiple_of(owner * tok, tok), tok)
        stream_f = ref[...].astype(jnp.float32)
        weight = coefs[rows, 0:1]
        pulled = coefs[rows, 1:2] * stream_f
        dstream[b * tok : (b + 1) * tok, :] = (weight * head[...] - pulled).astype(jnp.bfloat16)
        parts[pl.ds(owner, 1), :] = jnp.sum(weight * stream_f, axis=0, keepdims=True)


def form_kernel(count, added, owners, picked, coefs, head, *refs):
    blocks, refs = refs[:count], refs[count:]
    out, dstream, parts = refs[added:]
    form(owners, coefs, head, blocks, dstream, parts)
    total = jnp.dot(picked[...], dstream[...], preferred_element_type=jnp.float32)
    if added:
        total += refs[0][...]
    out[...] = total.astype(out.dtype)


def tile_of(tokens, half):
    return min(half, max(128, (1 << 20) // tokens))


def form_product(blocks, owners, picked, coefs, head, total, out_type):
    count = len(blocks)
    tok, half = blocks[0].shape
    units = picked.shape[0]
    tokens = coefs.shape[0]
    tile = tile_of(tokens, half)
    whole = lambda i, *_: (0, 0)
    at = lambda i, *_: (0, i)
    sums = [] if total is None else [total]
    return pl.pallas_call(
        functools.partial(form_kernel, count, len(sums)),
        grid_spec=pltpu.PrefetchScalarGridSpec(
            num_scalar_prefetch=1,
            grid=(half // tile,),
            in_specs=[
                pl.BlockSpec((units, count * tok), whole, pipeline_mode=pl.Buffered(1)),
                pl.BlockSpec((tokens, 2), whole, pipeline_mode=pl.Buffered(1)),
                pl.BlockSpec((1, tile), at),
            ]
            + [pl.BlockSpec((tok, tile), at)] * count
            + [pl.BlockSpec((units, tile), at)] * len(sums),
            out_specs=[
                pl.BlockSpec((units, tile), at),
                pl.BlockSpec((count * tok, tile), at),
                pl.BlockSpec((tokens // tok, tile), at),
            ],
        ),
        out_shape=[
            jax.ShapeDtypeStruct((units, half), out_type),
            jax.ShapeDtypeStruct((count * tok, half), jnp.bfloat16),
            jax.ShapeDtypeStruct((tokens // tok, half), jnp.float32),
        ],
        compiler_params=PARAMS,
        cost_estimate=cost(units, count * tok, half, 6 * units * half),
    )(owners, picked, coefs, head, *blocks, *sums)


def plain_kernel(added, where, picked, dstream, *refs):
    total = jnp.dot(picked[...], dstream[...], preferred_element_type=jnp.float32)
    if added:
        total += refs[0][...]
    refs[-1][...] = total.astype(refs[-1].dtype)


def plain_product(picked, dstream, total, out_type, where=None):
    units, k = picked.shape
    half = dstream.shape[1]
    tile = min(512, half)
    steps = half // tile
    at = lambda i, *_: (0, i)
    sums = [] if total is None else [total]
    wide = where is not None
    return pl.pallas_call(
        functools.partial(plain_kernel, len(sums)),
        grid_spec=pltpu.PrefetchScalarGridSpec(
            num_scalar_prefetch=1,
            grid=(steps,),
            in_specs=[
                pl.BlockSpec((units, k), lambda i, *_: (0, 0), pipeline_mode=pl.Buffered(1)),
                pl.BlockSpec((k, tile), at),
            ]
            + [pl.BlockSpec((units, tile), at)] * len(sums),
            out_specs=pl.BlockSpec((units, tile), lambda i, w: (0, w[0] * steps + i)),
        ),
        out_shape=jax.ShapeDtypeStruct((units, half * (2 if wide else 1)), out_type),
        compiler_params=PARAMS,
        cost_estimate=cost(units, k, half, 6 * units * half),
    )(where if wide else jnp.zeros((1,), jnp.int32), picked, dstream, *sums)


def put_kernel(where, part, whole, out):
    out[...] = part[...]


def put(whole, part, where):
    units, half = part.shape
    tile = min(512, half)
    steps = half // tile
    return pl.pallas_call(
        put_kernel,
        grid_spec=pltpu.PrefetchScalarGridSpec(
            num_scalar_prefetch=1,
            grid=(steps,),
            in_specs=[pl.BlockSpec((units, tile), lambda i, w: (0, i)), pl.BlockSpec(memory_space=pl.ANY)],
            out_specs=pl.BlockSpec((units, tile), lambda i, w: (0, w[0] * steps + i)),
        ),
        out_shape=jax.ShapeDtypeStruct(whole.shape, whole.dtype),
        input_output_aliases={2: 0},
        compiler_params=PARAMS,
        cost_estimate=cost(0, 0, 0, 4 * units * half),
    )(where, part, whole)


def all_returns(step_reward, resets):
    shards, tok = step_reward.shape
    position = jnp.arange(tok)
    before = jnp.cumsum(resets, axis=1) - resets
    total = jnp.sum(resets, axis=1, keepdims=True)
    reach = (position[None, :] >= position[:, None])[None] & (before[:, None, :] == before[:, :, None])
    local = jnp.sum(jnp.where(reach, step_reward[:, None, :], 0.0), axis=2)
    passing = before == total
    blocked = jnp.where(passing[:, 0], 0.0, 1.0)
    upto = jnp.cumsum(blocked)
    ids = jnp.arange(shards)
    open_path = (ids[None, :] > ids[:, None]) & ((upto - blocked)[None, :] == upto[:, None])
    incoming = jnp.sum(jnp.where(open_path, local[None, :, 0], 0.0), axis=1)
    return local + jnp.where(passing, incoming[:, None], 0.0)


def make_body(width, shards):
    paths = Paths(shards)

    def body(stream, hidden, final_gain, value_head, rewards, kl_terms, resets):
        tok, local = stream.shape
        half = local // 2
        me = lax.axis_index("seq")
        mine = me % 2
        gain = final_gain.astype(jnp.float32)
        head = gain * value_head.astype(jnp.float32)
        head_half = lax.dynamic_slice_in_dim(head, mine * half, half)[None]
        owners = lambda blocks: jnp.stack([paths.owner(me, b) for b in blocks])
        to_core = lambda x: lax.ppermute(x, "seq", paths.core)
        early, late = owners(early_blocks(paths.m)), owners(late_blocks(paths.m))
        made = {}

        def own_facts(stream):
            stream_f = stream.astype(jnp.float32)
            share = jnp.where(lax.axis_index("tp") == 0, 1.0, 0.0)
            return jnp.stack(
                [
                    jnp.sum(stream_f * stream_f, axis=-1),
                    jnp.sum(stream_f * head, axis=-1),
                    (rewards - 0.2 * kl_terms) * share,
                    resets.astype(jnp.float32) * share,
                ]
            )

        def early_own(facts, _, blocks):
            sum_squares, along, step_reward, cut = (facts[:, k] for k in range(4))
            scale = lax.rsqrt(sum_squares / width + EPSILON)
            values = scale * along
            returns = all_returns(step_reward, cut)
            error = values - returns
            pull = scale**3 * along / width
            coefs = jnp.stack([error * scale, error * pull], axis=-1).reshape(shards * tok, 2)
            made.update(values=values, returns=returns, coefs=coefs)
            return form_product(blocks, early, pick(hidden, early, tok), coefs, head_half, None, jnp.float32)

        def early_other(dstream, other_hidden):
            return plain_product(pick(other_hidden, early, tok), dstream, None, jnp.float32)

        have = run_plan(stream, hidden, mine, own_facts, paths, early_own, early_other)
        blocks = [have[b] for b in late_blocks(paths.m)]
        out, dstream, parts = form_product(
            blocks, late, pick(have["other hidden"], late, tok), made["coefs"], head_half, have["early other"], jnp.bfloat16
        )
        out = to_core(out)
        grad_head = jnp.sum(parts + have["early parts"], axis=0)
        other_head = to_core(grad_head)
        grad_head = gain * jnp.where(
            mine == 0, jnp.concatenate([grad_head, other_head]), jnp.concatenate([other_head, grad_head])
        )
        where = mine[None].astype(jnp.int32)
        grad_down = plain_product(pick(hidden, late, tok), dstream, have["early own"], jnp.bfloat16, where)
        grad_down = put(grad_down, out, 1 - where)
        own = lambda a: lax.dynamic_index_in_dim(a, me, 0, keepdims=False)
        return (own(made["values"]), own(made["returns"]), grad_head, grad_down)

    return body


def solution(mesh):
    placed = (P("seq", "tp"), P("seq", None), P("tp"), P("tp"), P("seq"), P("seq"), P("seq"))

    def run(stream, *rest):
        return jax.shard_map(
            make_body(stream.shape[1], mesh.shape["seq"]),
            mesh=mesh,
            in_specs=placed,
            out_specs=(P("seq"), P("seq"), P("tp"), P("seq", "tp")),
            check_vma=False,
        )(stream, *rest)

    return run
```

```python
import functools

import jax
import jax.numpy as jnp
import numpy as np
from jax import lax
from jax.experimental import pallas as pl
from jax.experimental.pallas import tpu as pltpu
from jax.sharding import PartitionSpec as P

EPSILON = 1e-05


def butterfly_sum(x, axis):
    count = lax.axis_size(axis)
    step = 1
    while step < count:
        x = x + lax.ppermute(x, axis, [(i, i ^ step) for i in range(count)])
        step *= 2
    return x


def butterfly_step(x, axis):
    count = lax.axis_size(axis)
    step = x.shape[0]
    if step >= count:
        return x
    other = lax.ppermute(x, axis, [(i, i ^ step) for i in range(count)])
    low = (lax.axis_index(axis) & step) == 0
    return jnp.concatenate([jnp.where(low, x, other), jnp.where(low, other, x)])


class Paths:
    def __init__(self, count):
        self.count = count
        self.m = count // 4
        self.order = list(range(0, self.m, 2)) + list(range(self.m - 1 - self.m % 2, 0, -2))
        self.place = [self.order.index(z) for z in range(self.m)]
        self.across = [(i, i ^ 2) for i in range(count)]
        self.core = [(i, i ^ 1) for i in range(count)]
        self.ring = [self._ring(1), self._ring(-1)]

    def _ring(self, way):
        pairs = []
        for i in range(self.count):
            z, rest = divmod(i, 4)
            by = way if i % 2 == 0 else -way
            pairs.append((i, self.order[(self.place[z] + by) % self.m] * 4 + rest))
        return pairs

    def owners(self, blocks):
        table = np.zeros((self.count, len(blocks)), np.int32)
        for me in range(self.count):
            z, rest = divmod(me, 4)
            for b, (steps, across, kind) in enumerate(blocks):
                way = -1 if (me % 2 == 0) == (kind == 0) else 1
                table[me, b] = self.order[(self.place[z] + way * steps) % self.m] * 4 + (rest ^ (2 * across + kind))
        return table


class Flights:
    def __init__(self, **arrays):
        self.have = arrays

    def event(self, waits, sends=()):
        names = list(dict.fromkeys([*waits, *(source for _, source, _ in sends)]))
        self.have.update(zip(names, lax.optimization_barrier(tuple(self.have[n] for n in names))))
        for name, source, pairs in sends:
            self.have[name] = lax.ppermute(self.have[source], "seq", pairs)


def early_blocks(m):
    return [(k, a, kind) for k in range(m - 1) for a in range(2) for kind in range(2) if k < m - 2 or a == 0]


def late_blocks(m):
    return [(m - 2, 1, 0), (m - 2, 1, 1)] + [(m - 1, a, kind) for a in range(2) for kind in range(2)]


def run_plan(stream, hidden, core_index, own_facts, paths, pick_own, early_own, early_other):
    half = stream.shape[1] // 2
    m, ring, across, core = paths.m, paths.ring, paths.across, paths.core
    cut = lambda c: lax.dynamic_slice_in_dim(stream, c * half, half, 1)
    f = Flights(hidden=hidden, stream=stream, away=cut(1 - core_index))
    f.have[0, 0, 0] = cut(core_index)
    have = f.have

    def facts_step():
        have["facts"] = butterfly_step(have["facts"], "seq")

    f.event([], [((1, 0, 0), (0, 0, 0), ring[0]), ((0, 1, 0), (0, 0, 0), across), ((0, 0, 1), "away", core), ("other hidden", "hidden", core)])
    f.event(
        [(0, 0, 1), "stream"],
        [((1, 0, 1), (0, 0, 1), ring[1]), ((0, 1, 1), (0, 0, 1), across)],
    )
    have["sums"] = own_facts(have["stream"])
    have["own picks"] = pick_own(hidden)
    f.event([(1, 0, 0), (0, 1, 0), "sums", "other hidden", "own picks"], [((2, 0, 0), (1, 0, 0), ring[0]), ((1, 1, 0), (1, 0, 0), across)])
    have["facts"] = butterfly_sum(have["sums"], "tp")[None]
    facts_step()
    f.event([(1, 0, 1), (0, 1, 1), "facts"], [((2, 0, 1), (1, 0, 1), ring[1]), ((1, 1, 1), (1, 0, 1), across)])
    have["other picks"] = pick_own(have["other hidden"])
    for k in range(2, m):
        for kind in range(2):
            facts_step()
            if k < m - 1:
                sends = [((k + 1, 0, kind), (k, 0, kind), ring[kind]), ((k, 1, kind), (k, 0, kind), across)]
            elif kind == 0:
                sends = [((k, 1, kind), (k - 1, 1, kind), ring[kind])]
            else:
                sends = [((k, 1, kind), (k, 0, kind), across)]
            waits = [(k, 0, kind), (k - 1, 1, kind), "facts"]
            if k == 2 and kind == 0:
                waits.append("other picks")
            if k == m - 1 and kind == 1:
                waits.append("early own")
            f.event(waits, sends)
            if k == m - 1 and kind == 0:
                while have["facts"].shape[0] < paths.count:
                    facts_step()
                blocks = early_blocks(m)
                have["early own"], have["early dstream"], have["early parts"] = early_own(
                    have["facts"], have["own picks"][0], [have[b] for b in blocks]
                )
    have["early other"] = early_other(have["early dstream"], have["other picks"][0])
    f.event([(m - 1, 1, 0), (m - 1, 1, 1), "early other"])
    return have


PARAMS = pltpu.CompilerParams(vmem_limit_bytes=24 * 1024 * 1024)


def cost(units, k, width, extra):
    return pl.CostEstimate(
        flops=2 * units * k * width, bytes_accessed=2 * (units * k + k * width) + extra, transcendentals=0
    )


def pick_kernel(tok, owners, hidden, *picked):
    b = 0
    for out in picked:
        for at in range(0, out.shape[1], tok):
            out[:, at : at + tok] = hidden[:, pl.ds(pl.multiple_of(owners[b] * tok, tok), tok)]
            b += 1


def pick(hidden, owners, counts, tok):
    units, tokens = hidden.shape
    rows = next(r for r in range(128, 0, -16) if units % r == 0)
    at = lambda i, *_: (i, 0)
    return pl.pallas_call(
        functools.partial(pick_kernel, tok),
        grid_spec=pltpu.PrefetchScalarGridSpec(
            num_scalar_prefetch=1,
            grid=(units // rows,),
            in_specs=[pl.BlockSpec((rows, tokens), at)],
            out_specs=[pl.BlockSpec((rows, count * tok), at) for count in counts],
        ),
        out_shape=[jax.ShapeDtypeStruct((units, count * tok), hidden.dtype) for count in counts],
        compiler_params=PARAMS,
        cost_estimate=cost(units, 0, 0, 4 * units * tokens),
    )(owners, hidden)


def form(owners, first, coefs, head, blocks, dstream, parts):
    tok = blocks[0].shape[0]
    parts[...] = jnp.zeros_like(parts)
    for b, ref in enumerate(blocks):
        owner = owners[first + b]
        coef = coefs[:, pl.ds(pl.multiple_of(owner * tok, tok), tok)].T
        stream_f = ref[...].astype(jnp.float32)
        weight = coef[:, 0:1]
        pulled = coef[:, 1:2] * stream_f
        dstream[b * tok : (b + 1) * tok, :] = (weight * head[...] - pulled).astype(jnp.bfloat16)
        parts[pl.ds(owner, 1), :] = jnp.sum(weight * stream_f, axis=0, keepdims=True)


def form_kernel(count, first, added, owners, picked, coefs, head, *refs):
    blocks, refs = refs[:count], refs[count:]
    out, dstream, parts = refs[added:]
    form(owners, first, coefs, head, blocks, dstream, parts)
    total = jnp.dot(picked[...], dstream[...], preferred_element_type=jnp.float32)
    if added:
        total += refs[0][...]
    out[...] = total.astype(out.dtype)


def tile_of(units, width):
    return next(t for t in (256, 128, width) if width % t == 0)


def form_product(blocks, owners, first, picked, coefs, head, total, out_type, part=0, parts=1):
    count = len(blocks)
    tok, half = blocks[0].shape
    units = picked.shape[0]
    tokens = coefs.shape[1]
    width = half // parts
    tile = tile_of(units, width)
    steps = width // tile
    whole = lambda i, *_: (0, 0)
    at = lambda i, *_: (0, i)
    from_part = lambda i, *_: (0, part * steps + i)
    sums = [] if total is None else [total]
    return pl.pallas_call(
        functools.partial(form_kernel, count, first, len(sums)),
        grid_spec=pltpu.PrefetchScalarGridSpec(
            num_scalar_prefetch=1,
            grid=(steps,),
            in_specs=[
                pl.BlockSpec((units, count * tok), whole, pipeline_mode=pl.Buffered(1)),
                pl.BlockSpec(coefs.shape, whole, pipeline_mode=pl.Buffered(1)),
                pl.BlockSpec((1, tile), from_part),
            ]
            + [pl.BlockSpec((tok, tile), from_part)] * count
            + [pl.BlockSpec((units, tile), from_part)] * len(sums),
            out_specs=[
                pl.BlockSpec((units, tile), at),
                pl.BlockSpec((count * tok, tile), at),
                pl.BlockSpec((tokens // tok, tile), at),
            ],
        ),
        out_shape=[
            jax.ShapeDtypeStruct((units, width), out_type),
            jax.ShapeDtypeStruct((count * tok, width), jnp.bfloat16),
            jax.ShapeDtypeStruct((tokens // tok, width), jnp.float32),
        ],
        compiler_params=PARAMS,
        cost_estimate=cost(units, count * tok, width, 6 * units * width),
    )(owners, picked, coefs, head, *blocks, *sums)


def plain_kernel(parts, steps, added, where, picked, *refs):
    for part in range(parts):

        @pl.when(pl.program_id(0) // steps == part)
        def _():
            total = jnp.dot(picked[...], refs[part][...], preferred_element_type=jnp.float32)
            if added:
                total += refs[parts][...]
            refs[-1][...] = total.astype(refs[-1].dtype)


def plain_product(picked, dstreams, total, out_type, where=None):
    units, k = picked.shape
    parts = len(dstreams)
    width = dstreams[0].shape[1]
    tile = tile_of(units, width)
    steps = width // tile
    sums = [] if total is None else [total]
    wide = where is not None

    def part_at(part):
        return lambda i, *_: (0, jnp.clip(i - part * steps, 0, steps - 1))

    return pl.pallas_call(
        functools.partial(plain_kernel, parts, steps, len(sums)),
        grid_spec=pltpu.PrefetchScalarGridSpec(
            num_scalar_prefetch=1,
            grid=(parts * steps,),
            in_specs=[pl.BlockSpec((units, k), lambda i, *_: (0, 0), pipeline_mode=pl.Buffered(1))]
            + [pl.BlockSpec((k, tile), part_at(part)) for part in range(parts)]
            + [pl.BlockSpec((units, tile), lambda i, *_: (0, i))] * len(sums),
            out_specs=pl.BlockSpec((units, tile), lambda i, w: (0, w[0] * parts * steps + i)),
        ),
        out_shape=jax.ShapeDtypeStruct((units, parts * width * (2 if wide else 1)), out_type),
        compiler_params=PARAMS,
        cost_estimate=cost(units, k, parts * width, 6 * units * parts * width),
    )(where if wide else jnp.zeros((1,), jnp.int32), picked, *dstreams, *sums)


def put_kernel(pieces, where, part, whole, out, sems):
    units, width = part.shape
    rows = units // pieces
    start = pl.multiple_of(where[0] * width, width)
    copies = [
        pltpu.make_async_copy(
            part.at[pl.ds(n * rows, rows), :], out.at[pl.ds(n * rows, rows), pl.ds(start, width)], sems.at[n]
        )
        for n in range(pieces)
    ]
    for copy in copies:
        copy.start()
    for copy in copies:
        copy.wait()


def put(whole, part, where):
    units, width = part.shape
    pieces = next(n for n in (7, 4, 2, 1) if units % (16 * n) == 0)
    return pl.pallas_call(
        functools.partial(put_kernel, pieces),
        grid_spec=pltpu.PrefetchScalarGridSpec(
            num_scalar_prefetch=1,
            grid=(),
            in_specs=[pl.BlockSpec(memory_space=pl.ANY)] * 2,
            out_specs=pl.BlockSpec(memory_space=pl.ANY),
            scratch_shapes=[pltpu.SemaphoreType.DMA((pieces,))],
        ),
        out_shape=jax.ShapeDtypeStruct(whole.shape, whole.dtype),
        input_output_aliases={2: 0},
        compiler_params=PARAMS,
        cost_estimate=cost(0, 0, 0, 4 * units * width),
    )(where, part, whole)


def all_returns(step_reward, resets):
    shards, tok = step_reward.shape
    position = jnp.arange(tok)
    before = jnp.cumsum(resets, axis=1) - resets
    total = jnp.sum(resets, axis=1, keepdims=True)
    reach = (position[None, :] >= position[:, None])[None] & (before[:, None, :] == before[:, :, None])
    local = jnp.sum(jnp.where(reach, step_reward[:, None, :], 0.0), axis=2)
    passing = before == total
    blocked = jnp.where(passing[:, 0], 0.0, 1.0)
    upto = jnp.cumsum(blocked)
    ids = jnp.arange(shards)
    open_path = (ids[None, :] > ids[:, None]) & ((upto - blocked)[None, :] == upto[:, None])
    incoming = jnp.sum(jnp.where(open_path, local[None, :, 0], 0.0), axis=1)
    return local + jnp.where(passing, incoming[:, None], 0.0)


def make_body(width, shards):
    paths = Paths(shards)

    def body(stream, hidden, final_gain, value_head, rewards, kl_terms, resets):
        tok, local = stream.shape
        half = local // 2
        me = lax.axis_index("seq")
        mine = me % 2
        gain = final_gain.astype(jnp.float32)
        head = gain * value_head.astype(jnp.float32)
        head_half = lax.dynamic_slice_in_dim(head, mine * half, half)[None]
        to_core = lambda x: lax.ppermute(x, "seq", paths.core)
        early, late = early_blocks(paths.m), late_blocks(paths.m)
        owners = lax.dynamic_index_in_dim(jnp.asarray(paths.owners(early + late)), me, 0, keepdims=False)
        pick_own = lambda hidden: pick(hidden, owners, (len(early), len(late)), tok)
        made = {}

        def own_facts(stream):
            stream_f = stream.astype(jnp.float32)
            share = jnp.where(lax.axis_index("tp") == 0, 1.0, 0.0)
            return jnp.stack(
                [
                    jnp.sum(stream_f * stream_f, axis=-1),
                    jnp.sum(stream_f * head, axis=-1),
                    (rewards - 0.2 * kl_terms) * share,
                    resets.astype(jnp.float32) * share,
                ]
            )

        def early_own(facts, picked, blocks):
            sum_squares, along, step_reward, cut = (facts[:, k] for k in range(4))
            scale = lax.rsqrt(sum_squares / width + EPSILON)
            values = scale * along
            returns = all_returns(step_reward, cut)
            error = values - returns
            pull = scale**3 * along / width
            coefs = jnp.stack([error * scale, error * pull]).reshape(2, shards * tok)
            coefs = jnp.pad(coefs, ((0, 6), (0, 0)))
            made.update(values=values, returns=returns, coefs=coefs)
            return form_product(blocks, owners, 0, picked, coefs, head_half, None, jnp.float32)

        def early_other(dstream, picked):
            return plain_product(picked, [dstream], None, jnp.float32)

        have = run_plan(stream, hidden, mine, own_facts, paths, pick_own, early_own, early_other)
        blocks = [have[b] for b in late]
        swaps = 2
        swapped, dstreams, heads = [], [], []
        for n in range(swaps):
            out, dstream, parts = form_product(
                blocks,
                owners,
                len(early),
                have["other picks"][1],
                made["coefs"],
                head_half,
                have["early other"],
                jnp.bfloat16,
                n,
                swaps,
            )
            swapped.append(to_core(out))
            dstreams.append(dstream)
            heads.append(parts)
        grad_head = jnp.sum(jnp.concatenate(heads, axis=1) + have["early parts"], axis=0)
        other_head = to_core(grad_head)
        grad_head = gain * jnp.where(
            mine == 0, jnp.concatenate([grad_head, other_head]), jnp.concatenate([other_head, grad_head])
        )
        where = mine[None].astype(jnp.int32)
        grad_down = plain_product(have["own picks"][1], dstreams, have["early own"], jnp.bfloat16, where)
        for n in range(swaps):
            grad_down = put(grad_down, swapped[n], (1 - where) * swaps + n)
        own = lambda a: lax.dynamic_index_in_dim(a, me, 0, keepdims=False)
        return (own(made["values"]), own(made["returns"]), grad_head, grad_down)

    return body


def solution(mesh):
    placed = (P("seq", "tp"), P("seq", None), P("tp"), P("tp"), P("seq"), P("seq"), P("seq"))

    def run(stream, *rest):
        return jax.shard_map(
            make_body(stream.shape[1], mesh.shape["seq"]),
            mesh=mesh,
            in_specs=placed,
            out_specs=(P("seq"), P("seq"), P("tp"), P("seq", "tp")),
            check_vma=False,
        )(stream, *rest)

    return run
```

```python
import functools

import jax
import jax.numpy as jnp
import numpy as np
from jax import lax
from jax.experimental import pallas as pl
from jax.experimental.pallas import tpu as pltpu
from jax.sharding import PartitionSpec as P

EPSILON = 1e-05


def butterfly_sum(x, axis):
    count = lax.axis_size(axis)
    step = 1
    while step < count:
        x = x + lax.ppermute(x, axis, [(i, i ^ step) for i in range(count)])
        step *= 2
    return x


def butterfly_step(x, axis):
    count = lax.axis_size(axis)
    step = x.shape[0]
    if step >= count:
        return x
    other = lax.ppermute(x, axis, [(i, i ^ step) for i in range(count)])
    low = (lax.axis_index(axis) & step) == 0
    return jnp.concatenate([jnp.where(low, x, other), jnp.where(low, other, x)])


class Paths:
    def __init__(self, count):
        self.count = count
        self.m = count // 4
        self.order = list(range(0, self.m, 2)) + list(range(self.m - 1 - self.m % 2, 0, -2))
        self.place = [self.order.index(z) for z in range(self.m)]
        self.across = [(i, i ^ 2) for i in range(count)]
        self.core = [(i, i ^ 1) for i in range(count)]
        self.ring = [self._ring(1), self._ring(-1)]

    def _ring(self, way):
        pairs = []
        for i in range(self.count):
            z, rest = divmod(i, 4)
            by = way if i % 2 == 0 else -way
            pairs.append((i, self.order[(self.place[z] + by) % self.m] * 4 + rest))
        return pairs

    def owners(self, blocks):
        table = np.zeros((self.count, len(blocks)), np.int32)
        for me in range(self.count):
            z, rest = divmod(me, 4)
            for b, (steps, across, kind) in enumerate(blocks):
                way = -1 if (me % 2 == 0) == (kind == 0) else 1
                table[me, b] = self.order[(self.place[z] + way * steps) % self.m] * 4 + (rest ^ (2 * across + kind))
        return table


class Flights:
    def __init__(self, **arrays):
        self.have = arrays

    def event(self, waits, sends=()):
        names = list(dict.fromkeys([*waits, *(source for _, source, _ in sends)]))
        self.have.update(zip(names, lax.optimization_barrier(tuple(self.have[n] for n in names))))
        for name, source, pairs in sends:
            self.have[name] = lax.ppermute(self.have[source], "seq", pairs)


def early_blocks(m):
    return [(k, a, kind) for k in range(m - 1) for a in range(2) for kind in range(2) if k < m - 2 or a == 0]


def late_blocks(m):
    return [(m - 2, 1, 0), (m - 2, 1, 1)] + [(m - 1, a, kind) for a in range(2) for kind in range(2)]


def run_plan(stream, core_index, own_facts, paths, pick_both, early_own, early_other):
    half = stream.shape[1] // 2
    m, ring, across, core = paths.m, paths.ring, paths.across, paths.core
    cut = lambda c: lax.dynamic_slice_in_dim(stream, c * half, half, 1)
    f = Flights(stream=stream, away=cut(1 - core_index))
    f.have[0, 0, 0] = cut(core_index)
    have = f.have

    def facts_step():
        have["facts"] = butterfly_step(have["facts"], "seq")

    f.event([], [((1, 0, 0), (0, 0, 0), ring[0]), ((0, 1, 0), (0, 0, 0), across), ((0, 0, 1), "away", core)])
    f.event(
        [(0, 0, 1), "stream"],
        [((1, 0, 1), (0, 0, 1), ring[1]), ((0, 1, 1), (0, 0, 1), across)],
    )
    have["sums"] = own_facts(have["stream"])
    have["own picks"], have["away picks"] = pick_both()
    f.event([(1, 0, 0), (0, 1, 0), "sums", "own picks", "away picks"], [((2, 0, 0), (1, 0, 0), ring[0]), ((1, 1, 0), (1, 0, 0), across)])
    have["facts"] = butterfly_sum(have["sums"], "tp")[None]
    facts_step()
    f.event([(1, 0, 1), (0, 1, 1), "facts"], [((2, 0, 1), (1, 0, 1), ring[1]), ((1, 1, 1), (1, 0, 1), across)])
    for k in range(2, m):
        for kind in range(2):
            facts_step()
            if k < m - 1:
                sends = [((k + 1, 0, kind), (k, 0, kind), ring[kind]), ((k, 1, kind), (k, 0, kind), across)]
            elif kind == 0:
                sends = [((k, 1, kind), (k - 1, 1, kind), ring[kind])]
            else:
                sends = [((k, 1, kind), (k, 0, kind), across)]
            waits = [(k, 0, kind), (k - 1, 1, kind), "facts"]
            if k == m - 2 and kind == 1:
                sends.append(("other picks", "away picks", core))
            if k == m - 1 and kind == 1:
                waits += ["other picks", "early own"]
            f.event(waits, sends)
            if k == m - 1 and kind == 0:
                while have["facts"].shape[0] < paths.count:
                    facts_step()
                blocks = early_blocks(m)
                have["early own"], have["early dstream"], have["early parts"] = early_own(
                    have["facts"], have["own picks"], [have[b] for b in blocks]
                )
    have["early other"] = early_other(have["early dstream"], have["other picks"])
    f.event([(m - 1, 1, 0), (m - 1, 1, 1), "early other"])
    return have


PARAMS = pltpu.CompilerParams(vmem_limit_bytes=60 * 1024 * 1024)


def cost(units, k, width, extra):
    return pl.CostEstimate(
        flops=2 * units * k * width, bytes_accessed=2 * (units * k + k * width) + extra, transcendentals=0
    )


def pick_kernel(tok, owners, hidden, *picked):
    count = hidden.shape[1] // tok
    for n, out in enumerate(picked):
        for b in range(count):
            columns = pl.ds(pl.multiple_of(owners[n * count + b] * tok, tok), tok)
            out[:, b * tok : (b + 1) * tok] = hidden[:, columns]


def pick(hidden, owners, orders, tok):
    units, tokens = hidden.shape
    rows = next(r for r in range(128, 0, -16) if units % r == 0)
    spec = pl.BlockSpec((rows, tokens), lambda i, *_: (i, 0))
    return pl.pallas_call(
        functools.partial(pick_kernel, tok),
        grid_spec=pltpu.PrefetchScalarGridSpec(
            num_scalar_prefetch=1, grid=(units // rows,), in_specs=[spec], out_specs=[spec] * orders
        ),
        out_shape=[jax.ShapeDtypeStruct(hidden.shape, hidden.dtype)] * orders,
        compiler_params=PARAMS,
        cost_estimate=cost(units, 0, 0, 2 * (1 + orders) * units * tokens),
    )(owners, hidden)


def spread(tok, owners, first, coefs, weights, pulls):
    for b in range(weights.shape[0] // tok):
        coef = coefs[:, pl.ds(pl.multiple_of(owners[first + b] * tok, tok), tok)].T
        rows = slice(b * tok, (b + 1) * tok)
        weights[rows, :] = jnp.broadcast_to(coef[:, 0:1], (tok, 128))
        pulls[rows, :] = jnp.broadcast_to(coef[:, 1:2], (tok, 128))


def form(owners, first, weights, pulls, head, blocks, dstream, parts):
    tok, tile = blocks[0].shape
    parts[...] = jnp.zeros_like(parts)
    for b, ref in enumerate(blocks):
        rows = slice(b * tok, (b + 1) * tok)
        sums = []
        for at in range(0, tile, 128):
            lanes = slice(at, at + 128)
            stream_f = ref[:, lanes].astype(jnp.float32)
            weight = weights[rows, :]
            dstream[rows, lanes] = (weight * head[:, lanes] - pulls[rows, :] * stream_f).astype(jnp.bfloat16)
            sums.append(jnp.sum(weight * stream_f, axis=0, keepdims=True))
        parts[pl.ds(owners[first + b], 1), :] = jnp.concatenate(sums, axis=1)


def form_kernel(count, first, start, added, owners, picked, coefs, head, *refs):
    blocks, refs = refs[:count], refs[count:]
    out, dstream, parts, weights, pulls = refs[added:]

    @pl.when(pl.program_id(0) == 0)
    def _():
        spread(blocks[0].shape[0], owners, first, coefs, weights, pulls)

    form(owners, first, weights, pulls, head, blocks, dstream, parts)
    total = jnp.dot(picked[:, start : start + dstream.shape[0]], dstream[...], preferred_element_type=jnp.float32)
    if added:
        total += refs[0][...]
    out[...] = total.astype(out.dtype)


def tile_of(tokens, width):
    return next(t for t in (512 if tokens <= 4096 else 256, 128, width) if width % t == 0)


def picked_spec(units, start, k):
    return pl.BlockSpec((units, start + k), lambda i, *_: (0, 0), pipeline_mode=pl.Buffered(1))


def form_product(blocks, owners, first, picked, coefs, head, total, out_type):
    count = len(blocks)
    tok, half = blocks[0].shape
    units, tokens = picked.shape
    k = count * tok
    tile = tile_of(tokens, half)
    at = lambda i, *_: (0, i)
    sums = [] if total is None else [total]
    return pl.pallas_call(
        functools.partial(form_kernel, count, first, first * tok, len(sums)),
        grid_spec=pltpu.PrefetchScalarGridSpec(
            num_scalar_prefetch=1,
            grid=(half // tile,),
            in_specs=[
                picked_spec(units, first * tok, k),
                pl.BlockSpec(coefs.shape, lambda i, *_: (0, 0), pipeline_mode=pl.Buffered(1)),
                pl.BlockSpec((1, tile), at),
            ]
            + [pl.BlockSpec((tok, tile), at)] * count
            + [pl.BlockSpec((units, tile), at)] * len(sums),
            out_specs=[
                pl.BlockSpec((units, tile), at),
                pl.BlockSpec((k, tile), at),
                pl.BlockSpec((tokens // tok, tile), at),
            ],
            scratch_shapes=[pltpu.VMEM((k, 128), jnp.float32)] * 2,
        ),
        out_shape=[
            jax.ShapeDtypeStruct((units, half), out_type),
            jax.ShapeDtypeStruct((k, half), jnp.bfloat16),
            jax.ShapeDtypeStruct((tokens // tok, half), jnp.float32),
        ],
        compiler_params=PARAMS,
        cost_estimate=cost(units, k * (1 if sums else 10), half, 6 * units * half),
    )(owners, picked, coefs, head, *blocks, *sums)


def plain_kernel(start, added, where, picked, dstream, *refs):
    total = jnp.dot(picked[:, start : start + dstream.shape[0]], dstream[...], preferred_element_type=jnp.float32)
    if added:
        total += refs[0][...]
    refs[-1][...] = total.astype(refs[-1].dtype)


def plain_product(picked, start, dstream, total, out_type, where=None):
    units, tokens = picked.shape
    k, half = dstream.shape
    tile = tile_of(tokens, half)
    steps = half // tile
    at = lambda i, *_: (0, i)
    sums = [] if total is None else [total]
    wide = where is not None
    return pl.pallas_call(
        functools.partial(plain_kernel, start, len(sums)),
        grid_spec=pltpu.PrefetchScalarGridSpec(
            num_scalar_prefetch=1,
            grid=(steps,),
            in_specs=[picked_spec(units, start, k), pl.BlockSpec((k, tile), at)]
            + [pl.BlockSpec((units, tile), at)] * len(sums),
            out_specs=pl.BlockSpec((units, tile), lambda i, w: (0, w[0] * steps + i)),
        ),
        out_shape=jax.ShapeDtypeStruct((units, half * (2 if wide else 1)), out_type),
        compiler_params=PARAMS,
        cost_estimate=cost(units, k, half, 6 * units * half),
    )(where if wide else jnp.zeros((1,), jnp.int32), picked, dstream, *sums)


def put_kernel(pieces, where, part, whole, out, held, sems_in, sems_out):
    units, width = part.shape
    start = pl.multiple_of(where[0] * width, width)
    rows = [pl.ds(n * (units // pieces), units // pieces) for n in range(pieces)]
    fetch = [pltpu.make_async_copy(part.at[r, :], held.at[r, :], sems_in.at[n]) for n, r in enumerate(rows)]
    place = [
        pltpu.make_async_copy(held.at[r, :], out.at[r, pl.ds(start, width)], sems_out.at[n]) for n, r in enumerate(rows)
    ]
    for copy in fetch:
        copy.start()
    for n in range(pieces):
        fetch[n].wait()
        place[n].start()
    for copy in place:
        copy.wait()


def put(whole, part, where):
    units, width = part.shape
    pieces = next(n for n in (7, 4, 2, 1) if units % (16 * n) == 0)
    return pl.pallas_call(
        functools.partial(put_kernel, pieces),
        grid_spec=pltpu.PrefetchScalarGridSpec(
            num_scalar_prefetch=1,
            grid=(),
            in_specs=[pl.BlockSpec(memory_space=pl.ANY)] * 2,
            out_specs=pl.BlockSpec(memory_space=pl.ANY),
            scratch_shapes=[
                pltpu.VMEM(part.shape, part.dtype),
                pltpu.SemaphoreType.DMA((pieces,)),
                pltpu.SemaphoreType.DMA((pieces,)),
            ],
        ),
        out_shape=jax.ShapeDtypeStruct(whole.shape, whole.dtype),
        input_output_aliases={2: 0},
        compiler_params=PARAMS,
        cost_estimate=cost(0, 0, 0, 4 * units * width),
    )(where, part, whole)


def all_returns(step_reward, resets):
    shards, tok = step_reward.shape
    position = jnp.arange(tok)
    before = jnp.cumsum(resets, axis=1) - resets
    total = jnp.sum(resets, axis=1, keepdims=True)
    reach = (position[None, :] >= position[:, None])[None] & (before[:, None, :] == before[:, :, None])
    local = jnp.sum(jnp.where(reach, step_reward[:, None, :], 0.0), axis=2)
    passing = before == total
    blocked = jnp.where(passing[:, 0], 0.0, 1.0)
    upto = jnp.cumsum(blocked)
    ids = jnp.arange(shards)
    open_path = (ids[None, :] > ids[:, None]) & ((upto - blocked)[None, :] == upto[:, None])
    incoming = jnp.sum(jnp.where(open_path, local[None, :, 0], 0.0), axis=1)
    return local + jnp.where(passing, incoming[:, None], 0.0)


def make_body(width, shards):
    paths = Paths(shards)

    def body(stream, hidden, final_gain, value_head, rewards, kl_terms, resets):
        tok, local = stream.shape
        half = local // 2
        me = lax.axis_index("seq")
        mine = me % 2
        gain = final_gain.astype(jnp.float32)
        head = gain * value_head.astype(jnp.float32)
        head_half = lax.dynamic_slice_in_dim(head, mine * half, half)[None]
        to_core = lambda x: lax.ppermute(x, "seq", paths.core)
        early, late = early_blocks(paths.m), late_blocks(paths.m)
        table = paths.owners(late + early)
        both = np.concatenate([table, table[np.arange(shards) ^ 1]], axis=1)
        owners = lax.dynamic_index_in_dim(jnp.asarray(both), me, 0, keepdims=False)
        pick_both = lambda: pick(hidden, owners, 2, tok)
        early_start = len(late) * tok
        made = {}

        def own_facts(stream):
            stream_f = stream.astype(jnp.float32)
            share = jnp.where(lax.axis_index("tp") == 0, 1.0, 0.0)
            return jnp.stack(
                [
                    jnp.sum(stream_f * stream_f, axis=-1),
                    jnp.sum(stream_f * head, axis=-1),
                    (rewards - 0.2 * kl_terms) * share,
                    resets.astype(jnp.float32) * share,
                ]
            )

        def early_own(facts, picked, blocks):
            sum_squares, along, step_reward, cut = (facts[:, k] for k in range(4))
            scale = lax.rsqrt(sum_squares / width + EPSILON)
            values = scale * along
            returns = all_returns(step_reward, cut)
            error = values - returns
            pull = scale**3 * along / width
            coefs = jnp.stack([error * scale, error * pull]).reshape(2, shards * tok)
            coefs = jnp.pad(coefs, ((0, 6), (0, 0)))
            made.update(values=values, returns=returns, coefs=coefs)
            return form_product(blocks, owners, len(late), picked, coefs, head_half, None, jnp.float32)

        def early_other(dstream, picked):
            return plain_product(picked, early_start, dstream, None, jnp.float32)

        have = run_plan(stream, mine, own_facts, paths, pick_both, early_own, early_other)
        blocks = [have[b] for b in late]
        out, dstream, parts = form_product(
            blocks, owners, 0, have["other picks"], made["coefs"], head_half, have["early other"], jnp.bfloat16
        )
        swapped = to_core(out)
        grad_head = jnp.sum(parts + have["early parts"], axis=0)
        other_head = to_core(grad_head)
        grad_head = gain * jnp.where(
            mine == 0, jnp.concatenate([grad_head, other_head]), jnp.concatenate([other_head, grad_head])
        )
        where = mine[None].astype(jnp.int32)
        grad_down = plain_product(have["own picks"], 0, dstream, have["early own"], jnp.bfloat16, where)
        grad_down = put(grad_down, swapped, 1 - where)
        own = lambda a: lax.dynamic_index_in_dim(a, me, 0, keepdims=False)
        return (own(made["values"]), own(made["returns"]), grad_head, grad_down)

    return body


def solution(mesh):
    placed = (P("seq", "tp"), P("seq", None), P("tp"), P("tp"), P("seq"), P("seq"), P("seq"))

    def run(stream, *rest):
        return jax.shard_map(
            make_body(stream.shape[1], mesh.shape["seq"]),
            mesh=mesh,
            in_specs=placed,
            out_specs=(P("seq"), P("seq"), P("tp"), P("seq", "tp")),
            check_vma=False,
        )(stream, *rest)

    return run
```

```python
import functools

import jax
import jax.numpy as jnp
import numpy as np
from jax import lax
from jax.experimental import pallas as pl
from jax.experimental.pallas import tpu as pltpu
from jax.sharding import PartitionSpec as P

EPSILON = 1e-05


def butterfly_sum(x, axis):
    count = lax.axis_size(axis)
    step = 1
    while step < count:
        x = x + lax.ppermute(x, axis, [(i, i ^ step) for i in range(count)])
        step *= 2
    return x


def butterfly_step(x, axis):
    count = lax.axis_size(axis)
    step = x.shape[0]
    if step >= count:
        return x
    other = lax.ppermute(x, axis, [(i, i ^ step) for i in range(count)])
    low = (lax.axis_index(axis) & step) == 0
    return jnp.concatenate([jnp.where(low, x, other), jnp.where(low, other, x)])


class Paths:
    def __init__(self, count):
        self.count = count
        self.m = count // 4
        self.order = list(range(0, self.m, 2)) + list(range(self.m - 1 - self.m % 2, 0, -2))
        self.place = [self.order.index(z) for z in range(self.m)]
        self.across = [(i, i ^ 2) for i in range(count)]
        self.core = [(i, i ^ 1) for i in range(count)]
        self.ring = [self._ring(1), self._ring(-1)]

    def _ring(self, way):
        pairs = []
        for i in range(self.count):
            z, rest = divmod(i, 4)
            by = way if i % 2 == 0 else -way
            pairs.append((i, self.order[(self.place[z] + by) % self.m] * 4 + rest))
        return pairs

    def owners(self, blocks):
        table = np.zeros((self.count, len(blocks)), np.int32)
        for me in range(self.count):
            z, rest = divmod(me, 4)
            for b, (steps, across, kind) in enumerate(blocks):
                way = -1 if (me % 2 == 0) == (kind == 0) else 1
                table[me, b] = self.order[(self.place[z] + way * steps) % self.m] * 4 + (rest ^ (2 * across + kind))
        return table


class Flights:
    def __init__(self, **arrays):
        self.have = arrays

    def event(self, waits, sends=()):
        names = list(dict.fromkeys([*waits, *(source for _, source, _ in sends)]))
        self.have.update(zip(names, lax.optimization_barrier(tuple(self.have[n] for n in names))))
        for name, source, pairs in sends:
            self.have[name] = lax.ppermute(self.have[source], "seq", pairs)


def block_groups(m):
    last = [(m - 1, 1, 0), (m - 1, 1, 1)]
    middle = [(m - 2, 1, 0), (m - 2, 1, 1), (m - 1, 0, 0), (m - 1, 0, 1)]
    early = [(k, a, kind) for k in range(m - 1) for a in range(2) for kind in range(2) if k < m - 2 or a == 0]
    return last, middle, early


def run_plan(stream, core_index, own_facts, paths, pick_both, early_own, early_other):
    half = stream.shape[1] // 2
    m, ring, across, core = paths.m, paths.ring, paths.across, paths.core
    cut = lambda c: lax.dynamic_slice_in_dim(stream, c * half, half, 1)
    f = Flights(stream=stream, away=cut(1 - core_index))
    f.have[0, 0, 0] = cut(core_index)
    have = f.have

    def facts_step():
        have["facts"] = butterfly_step(have["facts"], "seq")

    f.event([], [((1, 0, 0), (0, 0, 0), ring[0]), ((0, 1, 0), (0, 0, 0), across), ((0, 0, 1), "away", core)])
    f.event(
        [(0, 0, 1), "stream"],
        [((1, 0, 1), (0, 0, 1), ring[1]), ((0, 1, 1), (0, 0, 1), across)],
    )
    have["sums"] = own_facts(have["stream"])
    have["own picks"], have["away picks"] = pick_both()
    f.event(
        [(1, 0, 0), (0, 1, 0), "sums", "own picks", "away picks"],
        [((2, 0, 0), (1, 0, 0), ring[0]), ((1, 1, 0), (1, 0, 0), across)],
    )
    have["facts"] = butterfly_sum(have["sums"], "tp")[None]
    facts_step()
    f.event([(1, 0, 1), (0, 1, 1), "facts"], [((2, 0, 1), (1, 0, 1), ring[1]), ((1, 1, 1), (1, 0, 1), across)])
    for k in range(2, m):
        for kind in range(2):
            facts_step()
            if k < m - 1:
                sends = [((k + 1, 0, kind), (k, 0, kind), ring[kind]), ((k, 1, kind), (k, 0, kind), across)]
            elif kind == 0:
                sends = [((k, 1, kind), (k - 1, 1, kind), ring[kind])]
            else:
                sends = [((k, 1, kind), (k, 0, kind), across)]
            waits = [(k, 0, kind), (k - 1, 1, kind), "facts"]
            if k == m - 2 and kind == 1:
                sends.append(("other picks", "away picks", core))
            if k == m - 1 and kind == 1:
                waits += ["other picks", "early own", "values", "returns"]
            f.event(waits, sends)
            if k == m - 1 and kind == 0:
                while have["facts"].shape[0] < paths.count:
                    facts_step()
                early_own(have)
    early_other(have)
    f.event([(m - 1, 1, 0), (m - 1, 1, 1), "other sum"])
    return have


PARAMS = pltpu.CompilerParams(vmem_limit_bytes=60 * 1024 * 1024)


def cost(units, k, width, extra):
    return pl.CostEstimate(
        flops=2 * units * k * width, bytes_accessed=2 * (units * k + k * width) + extra, transcendentals=0
    )


def pick_kernel(tok, owners, hidden, *picked):
    count = hidden.shape[1] // tok
    for n, out in enumerate(picked):
        for b in range(count):
            columns = pl.ds(pl.multiple_of(owners[n * count + b] * tok, tok), tok)
            out[:, b * tok : (b + 1) * tok] = hidden[:, columns]


def pick(hidden, owners, orders, tok):
    units, tokens = hidden.shape
    rows = next(r for r in range(128, 0, -16) if units % r == 0)
    spec = pl.BlockSpec((rows, tokens), lambda i, *_: (i, 0))
    return pl.pallas_call(
        functools.partial(pick_kernel, tok),
        grid_spec=pltpu.PrefetchScalarGridSpec(
            num_scalar_prefetch=1, grid=(units // rows,), in_specs=[spec], out_specs=[spec] * orders
        ),
        out_shape=[jax.ShapeDtypeStruct(hidden.shape, hidden.dtype)] * orders,
        compiler_params=PARAMS,
        cost_estimate=cost(units, 0, 0, 2 * (1 + orders) * units * tokens),
    )(owners, hidden)


def spread(tok, owners, first, coefs, weights, pulls):
    for b in range(weights.shape[0] // tok):
        coef = coefs[:, pl.ds(pl.multiple_of(owners[first + b] * tok, tok), tok)].T
        rows = slice(b * tok, (b + 1) * tok)
        weights[rows, :] = jnp.broadcast_to(coef[:, 0:1], (tok, 128))
        pulls[rows, :] = jnp.broadcast_to(coef[:, 1:2], (tok, 128))


def form(tok, owners, first, weights, pulls, head, blocks, dstream, parts, start, chunk):
    for b in range(blocks.shape[0] // tok):
        rows = slice(b * tok, (b + 1) * tok)
        for at in range(0, chunk, 128):
            lanes = pl.ds(pl.multiple_of(start + at, 128), 128)
            stream_f = blocks[rows, lanes].astype(jnp.float32)
            weight = weights[rows, :]
            dstream[rows, lanes] = (weight * head[:, lanes] - pulls[rows, :] * stream_f).astype(jnp.bfloat16)
            parts[owners[first + b], :, lanes] = jnp.sum(weight * stream_f, axis=0, keepdims=True)


def product_kernel(tok, count, first, given_count, added, chunk, owners, where, *refs):
    refs = list(refs)
    take = lambda n: [refs.pop(0) for _ in range(n)]
    (picked,) = take(1)
    coefs, head = take(2) if count else (None, None)
    blocks, given, total = take(count), take(given_count), take(added)
    (out,) = take(1)
    dstream, parts = take(2) if count else (None, None)
    picked_v, dstream_v, sum_v = take(3)
    blocks_v, weights, pulls = take(3) if count else (None, None, None)
    out_v = take(1)[0] if added else sum_v
    sem_picked, sem_blocks, sem_given, sem_total, sem_out, sem_dstream = take(6)
    half = sum_v.shape[1]
    steps = half // chunk
    k = picked_v.shape[1]
    formed = count * tok
    base = pl.multiple_of(where[0] * half, half)

    columns = lambda c: pl.ds(pl.multiple_of(c * chunk, chunk), chunk)
    get_picked = pltpu.make_async_copy(picked.at[:, pl.ds(first * tok, k)], picked_v, sem_picked)
    get_blocks = [
        pltpu.make_async_copy(ref, blocks_v.at[pl.ds(b * tok, tok), :], sem_blocks.at[b]) for b, ref in enumerate(blocks)
    ]

    def get_given(g, c):
        row = formed + sum(ref.shape[0] for ref in given[:g])
        rows = pl.ds(row, given[g].shape[0])
        return pltpu.make_async_copy(given[g].at[:, columns(c)], dstream_v.at[rows, columns(c)], sem_given.at[g, c])

    def get_total(c):
        return pltpu.make_async_copy(total[0].at[:, columns(c)], sum_v.at[:, columns(c)], sem_total.at[c])

    def put_out(c):
        there = pl.ds(pl.multiple_of(base + c * chunk, chunk), chunk)
        return pltpu.make_async_copy(out_v.at[:, columns(c)], out.at[:, there], sem_out.at[c])

    def put_dstream(c):
        rows = pl.ds(0, formed)
        return pltpu.make_async_copy(dstream_v.at[rows, columns(c)], dstream.at[:, columns(c)], sem_dstream.at[c])

    for copy in get_blocks:
        copy.start()
    get_picked.start()
    for c in range(steps):
        for g in range(given_count):
            get_given(g, c).start()
        if added:
            get_total(c).start()
    if count:
        parts[...] = jnp.zeros_like(parts)
        spread(tok, owners, first, coefs, weights, pulls)
    for copy in get_blocks:
        copy.wait()
    get_picked.wait()

    def step(c, carry):
        if count:
            form(tok, owners, first, weights, pulls, head, blocks_v, dstream_v, parts, c * chunk, chunk)
            put_dstream(c).start()
        for g in range(given_count):
            get_given(g, c).wait()
        here = jnp.dot(picked_v[...], dstream_v[:, columns(c)], preferred_element_type=jnp.float32)
        if added:
            get_total(c).wait()
            here += sum_v[:, columns(c)]
        out_v[:, columns(c)] = here.astype(out_v.dtype)
        put_out(c).start()
        return carry

    lax.fori_loop(0, steps, step, 0)
    for c in range(steps):
        put_out(c).wait()
        if count:
            put_dstream(c).wait()


def product(owners, first, picked, formed=None, given=(), total=None, where=None):
    units, tokens = picked.shape
    coefs, head, blocks = formed or (None, None, [])
    half = blocks[0].shape[1] if blocks else given[0].shape[1]
    count = len(blocks)
    tok = tokens // owners.shape[0] * 2
    k = count * tok + sum(g.shape[0] for g in given)
    chunk = next(t for t in (512 if tokens <= 4096 else 256, 128, half) if half % t == 0)
    steps = half // chunk
    added = total is not None
    anywhere = pl.BlockSpec(memory_space=pl.ANY)
    inside = pl.BlockSpec(memory_space=pltpu.VMEM)
    out_type = jnp.bfloat16 if added else jnp.float32
    out_specs = [anywhere]
    out_shape = [jax.ShapeDtypeStruct((units, half if where is None else 2 * half), out_type)]
    scratch = [pltpu.VMEM((units, k), picked.dtype), pltpu.VMEM((k, half), jnp.bfloat16), pltpu.VMEM((units, half), jnp.float32)]
    if count:
        out_specs += [anywhere, inside]
        out_shape += [
            jax.ShapeDtypeStruct((count * tok, half), jnp.bfloat16),
            jax.ShapeDtypeStruct((tokens // tok, 1, half), jnp.float32),
        ]
        scratch += [pltpu.VMEM((count * tok, half), jnp.bfloat16)] + [pltpu.VMEM((count * tok, 128), jnp.float32)] * 2
    if added:
        scratch += [pltpu.VMEM((units, half), out_type)]
    sems = [(), (max(count, 1),), (max(len(given), 1), steps), (steps,), (steps,), (steps,)]
    return pl.pallas_call(
        functools.partial(product_kernel, tok, count, first, len(given), int(added), chunk),
        grid_spec=pltpu.PrefetchScalarGridSpec(
            num_scalar_prefetch=2,
            grid=(),
            in_specs=[anywhere] + [inside] * 2 * bool(count) + [anywhere] * (count + len(given) + added),
            out_specs=out_specs,
            scratch_shapes=scratch + [pltpu.SemaphoreType.DMA(shape) for shape in sems],
        ),
        out_shape=out_shape,
        compiler_params=PARAMS,
        cost_estimate=cost(units, k * (1 if added or given else 10), half, 6 * units * half),
    )(
        owners,
        jnp.zeros((1,), jnp.int32) if where is None else where,
        picked,
        *([coefs, head] if count else []),
        *blocks,
        *given,
        *([total] if added else []),
    )


def put_kernel(pieces, where, part, whole, out, held, sems_in, sems_out):
    units, width = part.shape
    start = pl.multiple_of(where[0] * width, width)
    rows = [pl.ds(n * (units // pieces), units // pieces) for n in range(pieces)]
    fetch = [pltpu.make_async_copy(part.at[r, :], held.at[r, :], sems_in.at[n]) for n, r in enumerate(rows)]
    place = [
        pltpu.make_async_copy(held.at[r, :], out.at[r, pl.ds(start, width)], sems_out.at[n]) for n, r in enumerate(rows)
    ]
    for copy in fetch:
        copy.start()
    for n in range(pieces):
        fetch[n].wait()
        place[n].start()
    for copy in place:
        copy.wait()


def put(whole, part, where):
    units, width = part.shape
    pieces = next(n for n in (7, 4, 2, 1) if units % (16 * n) == 0)
    return pl.pallas_call(
        functools.partial(put_kernel, pieces),
        grid_spec=pltpu.PrefetchScalarGridSpec(
            num_scalar_prefetch=1,
            grid=(),
            in_specs=[pl.BlockSpec(memory_space=pl.ANY)] * 2,
            out_specs=pl.BlockSpec(memory_space=pl.ANY),
            scratch_shapes=[
                pltpu.VMEM(part.shape, part.dtype),
                pltpu.SemaphoreType.DMA((pieces,)),
                pltpu.SemaphoreType.DMA((pieces,)),
            ],
        ),
        out_shape=jax.ShapeDtypeStruct(whole.shape, whole.dtype),
        input_output_aliases={2: 0},
        compiler_params=PARAMS,
        cost_estimate=cost(0, 0, 0, 4 * units * width),
    )(where, part, whole)


def all_returns(step_reward, resets):
    shards, tok = step_reward.shape
    position = jnp.arange(tok)
    before = jnp.cumsum(resets, axis=1) - resets
    total = jnp.sum(resets, axis=1, keepdims=True)
    reach = (position[None, :] >= position[:, None])[None] & (before[:, None, :] == before[:, :, None])
    local = jnp.sum(jnp.where(reach, step_reward[:, None, :], 0.0), axis=2)
    passing = before == total
    blocked = jnp.where(passing[:, 0], 0.0, 1.0)
    upto = jnp.cumsum(blocked)
    ids = jnp.arange(shards)
    open_path = (ids[None, :] > ids[:, None]) & ((upto - blocked)[None, :] == upto[:, None])
    incoming = jnp.sum(jnp.where(open_path, local[None, :, 0], 0.0), axis=1)
    return local + jnp.where(passing, incoming[:, None], 0.0)


def make_body(width, shards):
    paths = Paths(shards)

    def body(stream, hidden, final_gain, value_head, rewards, kl_terms, resets):
        tok, local = stream.shape
        half = local // 2
        me = lax.axis_index("seq")
        mine = me % 2
        gain = final_gain.astype(jnp.float32)
        head = gain * value_head.astype(jnp.float32)
        head_half = lax.dynamic_slice_in_dim(head, mine * half, half)[None]
        to_core = lambda x: lax.ppermute(x, "seq", paths.core)
        own = lambda a: lax.dynamic_index_in_dim(a, me, 0, keepdims=False)
        last, middle, early = block_groups(paths.m)
        table = paths.owners(last + middle + early)
        both = np.concatenate([table, table[np.arange(shards) ^ 1]], axis=1)
        owners = own(jnp.asarray(both))
        early_at = len(last + middle)

        def own_facts(stream):
            stream_f = stream.astype(jnp.float32)
            share = jnp.where(lax.axis_index("tp") == 0, 1.0, 0.0)
            return jnp.stack(
                [
                    jnp.sum(stream_f * stream_f, axis=-1),
                    jnp.sum(stream_f * head, axis=-1),
                    (rewards - 0.2 * kl_terms) * share,
                    resets.astype(jnp.float32) * share,
                ]
            )

        def early_own(have):
            sum_squares, along, step_reward, cut = (have["facts"][:, k] for k in range(4))
            scale = lax.rsqrt(sum_squares / width + EPSILON)
            values = scale * along
            returns = all_returns(step_reward, cut)
            error = values - returns
            pull = scale**3 * along / width
            coefs = jnp.stack([error * scale, error * pull]).reshape(2, shards * tok)
            coefs = jnp.pad(coefs, ((0, 6), (0, 0)))
            have.update(values=own(values), returns=own(returns), coefs=coefs)
            have["early own"], have["early dstream"], have["early parts"] = product(
                owners, early_at, have["own picks"], (coefs, head_half, [have[b] for b in early])
            )

        def early_other(have):
            have["other sum"], have["middle dstream"], have["middle parts"] = product(
                owners,
                len(last),
                have["other picks"],
                (have["coefs"], head_half, [have[b] for b in middle]),
                [have["early dstream"]],
            )

        have = run_plan(stream, mine, own_facts, paths, lambda: pick(hidden, owners, 2, tok), early_own, early_other)
        out, dstream, parts = product(
            owners, 0, have["other picks"], (have["coefs"], head_half, [have[b] for b in last]), (), have["other sum"]
        )
        swapped = to_core(out)
        grad_head = jnp.sum(parts + have["middle parts"] + have["early parts"], axis=(0, 1))
        other_head = to_core(grad_head)
        grad_head = gain * jnp.where(
            mine == 0, jnp.concatenate([grad_head, other_head]), jnp.concatenate([other_head, grad_head])
        )
        where = mine[None].astype(jnp.int32)
        (grad_down,) = product(
            owners, 0, have["own picks"], None, [dstream, have["middle dstream"]], have["early own"], where
        )
        grad_down = put(grad_down, swapped, 1 - where)
        return (have["values"], have["returns"], grad_head, grad_down)

    return body


def solution(mesh):
    placed = (P("seq", "tp"), P("seq", None), P("tp"), P("tp"), P("seq"), P("seq"), P("seq"))

    def run(stream, *rest):
        return jax.shard_map(
            make_body(stream.shape[1], mesh.shape["seq"]),
            mesh=mesh,
            in_specs=placed,
            out_specs=(P("seq"), P("seq"), P("tp"), P("seq", "tp")),
            check_vma=False,
        )(stream, *rest)

    return run
```

```python
import functools

import jax
import jax.numpy as jnp
import numpy as np
from jax import lax
from jax.experimental import pallas as pl
from jax.experimental.pallas import tpu as pltpu
from jax.sharding import PartitionSpec as P

EPSILON = 1e-05


def butterfly_sum(x, axis):
    count = lax.axis_size(axis)
    step = 1
    while step < count:
        x = x + lax.ppermute(x, axis, [(i, i ^ step) for i in range(count)])
        step *= 2
    return x


def butterfly_step(x, axis):
    count = lax.axis_size(axis)
    step = x.shape[0]
    if step >= count:
        return x
    other = lax.ppermute(x, axis, [(i, i ^ step) for i in range(count)])
    low = (lax.axis_index(axis) & step) == 0
    return jnp.concatenate([jnp.where(low, x, other), jnp.where(low, other, x)])


class Paths:
    def __init__(self, count):
        self.count = count
        self.m = count // 4
        self.order = list(range(0, self.m, 2)) + list(range(self.m - 1 - self.m % 2, 0, -2))
        self.place = [self.order.index(z) for z in range(self.m)]
        self.across = [(i, i ^ 2) for i in range(count)]
        self.core = [(i, i ^ 1) for i in range(count)]
        self.ring = [self._ring(1), self._ring(-1)]

    def _ring(self, way):
        pairs = []
        for i in range(self.count):
            z, rest = divmod(i, 4)
            by = way if i % 2 == 0 else -way
            pairs.append((i, self.order[(self.place[z] + by) % self.m] * 4 + rest))
        return pairs

    def owners(self, blocks):
        table = np.zeros((self.count, len(blocks)), np.int32)
        for me in range(self.count):
            z, rest = divmod(me, 4)
            for b, (steps, across, kind) in enumerate(blocks):
                way = -1 if (me % 2 == 0) == (kind == 0) else 1
                table[me, b] = self.order[(self.place[z] + way * steps) % self.m] * 4 + (rest ^ (2 * across + kind))
        return table


class Flights:
    def __init__(self, **arrays):
        self.have = arrays

    def event(self, waits, sends=()):
        names = list(dict.fromkeys([*waits, *(source for _, source, _ in sends)]))
        self.have.update(zip(names, lax.optimization_barrier(tuple(self.have[n] for n in names))))
        for name, source, pairs in sends:
            self.have[name] = lax.ppermute(self.have[source], "seq", pairs)


def block_groups(m):
    last = [(m - 1, 1, 0), (m - 1, 1, 1)]
    middle = [(m - 2, 1, 0), (m - 2, 1, 1), (m - 1, 0, 0), (m - 1, 0, 1)]
    early = [(k, a, kind) for k in range(m - 1) for a in range(2) for kind in range(2) if k < m - 2 or a == 0]
    return last, middle, early


def run_plan(stream, core_index, own_facts, paths, pick_both, early_own, early_other):
    half = stream.shape[1] // 2
    m, ring, across, core = paths.m, paths.ring, paths.across, paths.core
    cut = lambda c: lax.dynamic_slice_in_dim(stream, c * half, half, 1)
    f = Flights(stream=stream, away=cut(1 - core_index))
    f.have[0, 0, 0] = cut(core_index)
    have = f.have

    def facts_step():
        have["facts"] = butterfly_step(have["facts"], "seq")

    f.event([], [((1, 0, 0), (0, 0, 0), ring[0]), ((0, 1, 0), (0, 0, 0), across), ((0, 0, 1), "away", core)])
    f.event(
        [(0, 0, 1), "stream"],
        [((1, 0, 1), (0, 0, 1), ring[1]), ((0, 1, 1), (0, 0, 1), across)],
    )
    have["sums"] = own_facts(have["stream"])
    have["own picks"], have["away picks"] = pick_both()
    f.event(
        [(1, 0, 0), (0, 1, 0), "sums", "own picks", "away picks"],
        [((2, 0, 0), (1, 0, 0), ring[0]), ((1, 1, 0), (1, 0, 0), across)],
    )
    have["facts"] = butterfly_sum(have["sums"], "tp")[None]
    facts_step()
    f.event([(1, 0, 1), (0, 1, 1), "facts"], [((2, 0, 1), (1, 0, 1), ring[1]), ((1, 1, 1), (1, 0, 1), across)])
    for k in range(2, m):
        for kind in range(2):
            facts_step()
            if k < m - 1:
                sends = [((k + 1, 0, kind), (k, 0, kind), ring[kind]), ((k, 1, kind), (k, 0, kind), across)]
            elif kind == 0:
                sends = [((k, 1, kind), (k - 1, 1, kind), ring[kind])]
            else:
                sends = [((k, 1, kind), (k, 0, kind), across)]
            waits = [(k, 0, kind), (k - 1, 1, kind), "facts"]
            if k == m - 2 and kind == 1:
                sends.append(("other picks", "away picks", core))
            if k == m - 1 and kind == 1:
                waits += ["other picks", "early own", "values", "returns"]
            f.event(waits, sends)
            if k == m - 1 and kind == 0:
                while have["facts"].shape[0] < paths.count:
                    facts_step()
                early_own(have)
    early_other(have)
    f.event([(m - 1, 1, 0), (m - 1, 1, 1), "other sum"])
    return have


PARAMS = pltpu.CompilerParams(vmem_limit_bytes=16 * 1024 * 1024)


def cost(units, k, width, extra):
    return pl.CostEstimate(
        flops=2 * units * k * width, bytes_accessed=2 * (units * k + k * width) + extra, transcendentals=0
    )


def pick_kernel(tok, owners, hidden, *picked):
    count = hidden.shape[1] // tok
    for n, out in enumerate(picked):
        for b in range(count):
            columns = pl.ds(pl.multiple_of(owners[n * count + b] * tok, tok), tok)
            out[:, b * tok : (b + 1) * tok] = hidden[:, columns]


def pick(hidden, owners, orders, tok):
    units, tokens = hidden.shape
    rows = next(r for r in range(128, 0, -16) if units % r == 0)
    spec = pl.BlockSpec((rows, tokens), lambda i, *_: (i, 0))
    return pl.pallas_call(
        functools.partial(pick_kernel, tok),
        grid_spec=pltpu.PrefetchScalarGridSpec(
            num_scalar_prefetch=1, grid=(units // rows,), in_specs=[spec], out_specs=[spec] * orders
        ),
        out_shape=[jax.ShapeDtypeStruct(hidden.shape, hidden.dtype)] * orders,
        compiler_params=PARAMS,
        cost_estimate=cost(units, 0, 0, 2 * (1 + orders) * units * tokens),
    )(owners, hidden)


def spread(tok, owners, first, coefs, weights, pulls):
    for b in range(weights.shape[0] // tok):
        coef = coefs[:, pl.ds(pl.multiple_of(owners[first + b] * tok, tok), tok)].T
        rows = slice(b * tok, (b + 1) * tok)
        weights[rows, :] = jnp.broadcast_to(coef[:, 0:1], (tok, 128))
        pulls[rows, :] = jnp.broadcast_to(coef[:, 1:2], (tok, 128))


def form(tok, owners, first, weights, pulls, head, blocks, dstream, parts, start, chunk):
    for b in range(len(blocks)):
        rows = slice(b * tok, (b + 1) * tok)
        for at in range(0, chunk, 128):
            lanes = pl.ds(pl.multiple_of(start + at, 128), 128)
            stream_f = blocks[b][:, lanes].astype(jnp.float32)
            weight = weights[rows, :]
            dstream[rows, lanes] = (weight * head[:, lanes] - pulls[rows, :] * stream_f).astype(jnp.bfloat16)
            parts[owners[first + b], :, lanes] = jnp.sum(weight * stream_f, axis=0, keepdims=True)


def pieces_of(units):
    return next(n for n in (7, 4, 2, 1) if units % (16 * n) == 0)


def product_kernel(tok, count, first, given_count, added, parts_count, wide, chunk, owners, where, *refs):
    refs = list(refs)
    take = lambda n: [refs.pop(0) for _ in range(n)]
    (picked,) = take(1)
    coefs, head = take(2) if count else (None, None)
    blocks, given, total, other_parts = take(count), take(given_count), take(added), take(parts_count)
    (out,) = take(1)
    dstream, parts_out = take(2) if count else (None, None)
    weights, pulls, parts = take(3) if count else (None, None, None)
    out_v = take(1)[0] if wide else out
    (sem_out,) = take(1)
    half = out_v.shape[1]
    steps = half // chunk
    base = pl.multiple_of(where[0] * half, half)

    columns = lambda c: pl.ds(pl.multiple_of(c * chunk, chunk), chunk)

    def put_out(c):
        there = pl.ds(pl.multiple_of(base + c * chunk, chunk), chunk)
        return pltpu.make_async_copy(out_v.at[:, columns(c)], out.at[:, there], sem_out.at[c])

    if count:
        parts[...] = jnp.zeros_like(parts)
        spread(tok, owners, first, coefs, weights, pulls)

    def step(c, carry):
        if count:
            form(tok, owners, first, weights, pulls, head, blocks, dstream, parts, c * chunk, chunk)

        factors = ([dstream] if count else []) + given
        here = total[0][:, columns(c)] if added else None
        at = first * tok
        for factor in factors:
            depth = factor.shape[0]
            term = jnp.dot(picked[:, at : at + depth], factor[:, columns(c)], preferred_element_type=jnp.float32)
            here = term if here is None else here + term
            at += depth
        out_v[:, columns(c)] = here.astype(out_v.dtype)
        if wide:
            put_out(c).start()
        return carry

    lax.fori_loop(0, steps, step, 0)
    if count:
        if other_parts:
            parts_out[...] = sum([p[...] for p in other_parts], parts[...]).sum(axis=0)
        else:
            parts_out[...] = parts[...]
    if wide:
        for c in range(steps):
            put_out(c).wait()


def product(owners, first, picked, formed=None, given=(), total=None, parts=(), where=None):
    units, tokens = picked.shape
    coefs, head, blocks = formed or (None, None, [])
    half = blocks[0].shape[1] if blocks else given[0].shape[1]
    count = len(blocks)
    tok = tokens // owners.shape[0] * 2
    k = count * tok + sum(g.shape[0] for g in given)
    chunk = next(t for t in (512 if tokens <= 4096 else 256, 128, half) if half % t == 0)
    steps = half // chunk
    added, wide = total is not None, where is not None
    anywhere = pl.BlockSpec(memory_space=pl.ANY)
    inside = pl.BlockSpec(memory_space=pltpu.VMEM)
    in_vmem = lambda x: pltpu.with_memory_space_constraint(x, pltpu.VMEM)
    out_type = jnp.bfloat16 if added else jnp.float32
    if wide:
        out_specs = [anywhere]
        out_shape = [jax.ShapeDtypeStruct((units, 2 * half), out_type)]
    else:
        out_specs = [inside]
        out_shape = [pltpu.VMEM((units, half), out_type)]
    scratch = []
    parts_shape = (tokens // tok, 1, half)
    if count:
        out_specs += [inside, inside]
        out_shape += [
            pltpu.VMEM((count * tok, half), jnp.bfloat16),
            jax.ShapeDtypeStruct(parts_shape[1:] if parts else parts_shape, jnp.float32),
        ]
        scratch += [pltpu.VMEM((count * tok, 128), jnp.float32)] * 2 + [pltpu.VMEM(parts_shape, jnp.float32)]
    if wide:
        scratch += [pltpu.VMEM((units, half), out_type)]
    sems = [(steps,)]
    return pl.pallas_call(
        functools.partial(product_kernel, tok, count, first, len(given), int(added), len(parts), wide, chunk),
        grid_spec=pltpu.PrefetchScalarGridSpec(
            num_scalar_prefetch=2,
            grid=(),
            in_specs=[inside] * (1 + 2 * bool(count) + count + len(given) + added + len(parts)),
            out_specs=out_specs,
            scratch_shapes=scratch + [pltpu.SemaphoreType.DMA(shape) for shape in sems],
        ),
        out_shape=out_shape,
        compiler_params=PARAMS,
        cost_estimate=cost(units, k * (1 if added or given else 10), half, 6 * units * half),
    )(
        owners,
        where if wide else jnp.zeros((1,), jnp.int32),
        in_vmem(picked),
        *([coefs, head] if count else []),
        *[in_vmem(x) for x in blocks],
        *[in_vmem(x) for x in given],
        *([in_vmem(total)] if added else []),
        *parts,
    )


def put_kernel(pieces, where, part, whole, out, held, sems_in, sems_out):
    units, width = part.shape
    start = pl.multiple_of(where[0] * width, width)
    rows = [pl.ds(n * (units // pieces), units // pieces) for n in range(pieces)]
    fetch = [pltpu.make_async_copy(part.at[r, :], held.at[r, :], sems_in.at[n]) for n, r in enumerate(rows)]
    place = [
        pltpu.make_async_copy(held.at[r, :], out.at[r, pl.ds(start, width)], sems_out.at[n]) for n, r in enumerate(rows)
    ]
    for copy in fetch:
        copy.start()
    for n in range(pieces):
        fetch[n].wait()
        place[n].start()
    for copy in place:
        copy.wait()


def put(whole, part, where):
    units, width = part.shape
    pieces = pieces_of(units)
    return pl.pallas_call(
        functools.partial(put_kernel, pieces),
        grid_spec=pltpu.PrefetchScalarGridSpec(
            num_scalar_prefetch=1,
            grid=(),
            in_specs=[pl.BlockSpec(memory_space=pl.ANY)] * 2,
            out_specs=pl.BlockSpec(memory_space=pl.ANY),
            scratch_shapes=[
                pltpu.VMEM(part.shape, part.dtype),
                pltpu.SemaphoreType.DMA((pieces,)),
                pltpu.SemaphoreType.DMA((pieces,)),
            ],
        ),
        out_shape=jax.ShapeDtypeStruct(whole.shape, whole.dtype),
        input_output_aliases={2: 0},
        compiler_params=PARAMS,
        cost_estimate=cost(0, 0, 0, 4 * units * width),
    )(where, part, whole)


def all_returns(step_reward, resets):
    shards, tok = step_reward.shape
    position = jnp.arange(tok)
    before = jnp.cumsum(resets, axis=1) - resets
    total = jnp.sum(resets, axis=1, keepdims=True)
    reach = (position[None, :] >= position[:, None])[None] & (before[:, None, :] == before[:, :, None])
    local = jnp.sum(jnp.where(reach, step_reward[:, None, :], 0.0), axis=2)
    passing = before == total
    blocked = jnp.where(passing[:, 0], 0.0, 1.0)
    upto = jnp.cumsum(blocked)
    ids = jnp.arange(shards)
    open_path = (ids[None, :] > ids[:, None]) & ((upto - blocked)[None, :] == upto[:, None])
    incoming = jnp.sum(jnp.where(open_path, local[None, :, 0], 0.0), axis=1)
    return local + jnp.where(passing, incoming[:, None], 0.0)


def make_body(width, shards):
    paths = Paths(shards)

    def body(stream, hidden, final_gain, value_head, rewards, kl_terms, resets):
        tok, local = stream.shape
        half = local // 2
        me = lax.axis_index("seq")
        mine = me % 2
        gain = final_gain.astype(jnp.float32)
        head = gain * value_head.astype(jnp.float32)
        head_half = lax.dynamic_slice_in_dim(head, mine * half, half)[None]
        to_core = lambda x: lax.ppermute(x, "seq", paths.core)
        own = lambda a: lax.dynamic_index_in_dim(a, me, 0, keepdims=False)
        last, middle, early = block_groups(paths.m)
        table = paths.owners(last + middle + early)
        both = np.concatenate([table, table[np.arange(shards) ^ 1]], axis=1)
        owners = own(jnp.asarray(both))
        early_at = len(last + middle)

        def own_facts(stream):
            stream_f = stream.astype(jnp.float32)
            share = jnp.where(lax.axis_index("tp") == 0, 1.0, 0.0)
            return jnp.stack(
                [
                    jnp.sum(stream_f * stream_f, axis=-1),
                    jnp.sum(stream_f * head, axis=-1),
                    (rewards - 0.2 * kl_terms) * share,
                    resets.astype(jnp.float32) * share,
                ]
            )

        def early_own(have):
            sum_squares, along, step_reward, cut = (have["facts"][:, k] for k in range(4))
            scale = lax.rsqrt(sum_squares / width + EPSILON)
            values = scale * along
            returns = all_returns(step_reward, cut)
            error = values - returns
            pull = scale**3 * along / width
            coefs = jnp.stack([error * scale, error * pull]).reshape(2, shards * tok)
            coefs = jnp.pad(coefs, ((0, 6), (0, 0)))
            have.update(values=own(values), returns=own(returns), coefs=coefs)
            have["early own"], have["early dstream"], have["early parts"] = product(
                owners, early_at, have["own picks"], (coefs, head_half, [have[b] for b in early])
            )

        def early_other(have):
            have["other sum"], have["middle dstream"], have["middle parts"] = product(
                owners,
                len(last),
                have["other picks"],
                (have["coefs"], head_half, [have[b] for b in middle]),
                [have["early dstream"]],
            )

        have = run_plan(stream, mine, own_facts, paths, lambda: pick(hidden, owners, 2, tok), early_own, early_other)
        out, dstream, grad_head = product(
            owners,
            0,
            have["other picks"],
            (have["coefs"], head_half, [have[b] for b in last]),
            (),
            have["other sum"],
            [have["early parts"], have["middle parts"]],
        )
        swapped = to_core(out)
        grad_head = grad_head[0]
        other_head = to_core(grad_head)
        grad_head = gain * jnp.where(
            mine == 0, jnp.concatenate([grad_head, other_head]), jnp.concatenate([other_head, grad_head])
        )
        where = mine[None].astype(jnp.int32)
        (grad_down,) = product(
            owners, 0, have["own picks"], None, [dstream, have["middle dstream"]], have["early own"], (), where
        )
        grad_down = put(grad_down, swapped, 1 - where)
        return (have["values"], have["returns"], grad_head, grad_down)

    return body


def solution(mesh):
    placed = (P("seq", "tp"), P("seq", None), P("tp"), P("tp"), P("seq"), P("seq"), P("seq"))

    def run(stream, *rest):
        return jax.shard_map(
            make_body(stream.shape[1], mesh.shape["seq"]),
            mesh=mesh,
            in_specs=placed,
            out_specs=(P("seq"), P("seq"), P("tp"), P("seq", "tp")),
            check_vma=False,
        )(stream, *rest)

    return run
```

```python
import functools

import jax
import jax.numpy as jnp
import numpy as np
from jax import lax
from jax.experimental import pallas as pl
from jax.experimental.pallas import tpu as pltpu
from jax.sharding import PartitionSpec as P

EPSILON = 1e-05


def butterfly_sum(x, axis):
    count = lax.axis_size(axis)
    step = 1
    while step < count:
        x = x + lax.ppermute(x, axis, [(i, i ^ step) for i in range(count)])
        step *= 2
    return x


def butterfly_step(x, axis, low):
    count = lax.axis_size(axis)
    step = x.shape[0]
    if step >= count:
        return x
    other = lax.ppermute(x, axis, [(i, i ^ step) for i in range(count)])
    if step > 1:
        return jnp.concatenate([jnp.where(low[step], x, other), jnp.where(low[step], other, x)])
    first = lax.broadcasted_iota(jnp.int32, (2, *x.shape), 0) == 0
    return jnp.where(first == low[step], x[None], other[None]).reshape(2 * step, *x.shape[1:])


class Paths:
    def __init__(self, count):
        self.count = count
        self.m = count // 4
        self.order = list(range(0, self.m, 2)) + list(range(self.m - 1 - self.m % 2, 0, -2))
        self.place = [self.order.index(z) for z in range(self.m)]
        self.across = [(i, i ^ 2) for i in range(count)]
        self.core = [(i, i ^ 1) for i in range(count)]
        self.ring = [self._ring(1), self._ring(-1)]

    def _ring(self, way):
        pairs = []
        for i in range(self.count):
            z, rest = divmod(i, 4)
            by = way if i % 2 == 0 else -way
            pairs.append((i, self.order[(self.place[z] + by) % self.m] * 4 + rest))
        return pairs

    def owners(self, blocks):
        table = np.zeros((self.count, len(blocks)), np.int32)
        for me in range(self.count):
            z, rest = divmod(me, 4)
            for b, (steps, across, kind) in enumerate(blocks):
                way = -1 if (me % 2 == 0) == (kind == 0) else 1
                table[me, b] = self.order[(self.place[z] + way * steps) % self.m] * 4 + (rest ^ (2 * across + kind))
        return table


class Flights:
    def __init__(self, **arrays):
        self.have = arrays

    def event(self, waits, sends=()):
        names = list(dict.fromkeys([*waits, *(source for _, source, _ in sends)]))
        self.have.update(zip(names, lax.optimization_barrier(tuple(self.have[n] for n in names))))
        for name, source, pairs in sends:
            self.have[name] = lax.ppermute(self.have[source], "seq", pairs)


def block_groups(m):
    last = [(m - 1, 1, 0), (m - 1, 1, 1)]
    middle = [(m - 2, 1, 0), (m - 2, 1, 1), (m - 1, 0, 0), (m - 1, 0, 1)]
    early = [(k, a, kind) for k in range(m - 1) for a in range(2) for kind in range(2) if k < m - 2 or a == 0]
    return last, middle, early


def run_plan(stream, scalars, own_facts, paths, pick_both, early_own, early_other):
    half = stream.shape[1] // 2
    m, ring, across, core = paths.m, paths.ring, paths.across, paths.core
    cut = lambda c: lax.dynamic_slice_in_dim(stream, c * half, half, 1)
    core_index = scalars["core"]
    f = Flights(stream=stream, away=cut(1 - core_index), **scalars)
    f.have[0, 0, 0] = cut(core_index)
    have = f.have
    names = list(scalars)
    low = lambda: {1 << n: have["low %d" % n] for n in range(paths.count.bit_length() - 1)}

    def facts_step():
        have["facts"] = butterfly_step(have["facts"], "seq", low())

    f.event([], [((1, 0, 0), (0, 0, 0), ring[0]), ((0, 1, 0), (0, 0, 0), across), ((0, 0, 1), "away", core)])
    f.event(
        [(0, 0, 1), "stream", *names],
        [((1, 0, 1), (0, 0, 1), ring[1]), ((0, 1, 1), (0, 0, 1), across)],
    )
    have["sums"] = own_facts(have["stream"])
    have["own picks"], have["away picks"] = pick_both()
    f.event(
        [(1, 0, 0), (0, 1, 0), "sums", "own picks", "away picks"],
        [((2, 0, 0), (1, 0, 0), ring[0]), ((1, 1, 0), (1, 0, 0), across)],
    )
    have["facts"] = butterfly_sum(have["sums"], "tp")[None]
    facts_step()
    f.event([(1, 0, 1), (0, 1, 1), "facts"], [((2, 0, 1), (1, 0, 1), ring[1]), ((1, 1, 1), (1, 0, 1), across)])
    for k in range(2, m):
        for kind in range(2):
            facts_step()
            if k < m - 1:
                sends = [((k + 1, 0, kind), (k, 0, kind), ring[kind]), ((k, 1, kind), (k, 0, kind), across)]
            elif kind == 0:
                sends = [((k, 1, kind), (k - 1, 1, kind), ring[kind])]
            else:
                sends = [((k, 1, kind), (k, 0, kind), across)]
            waits = [(k, 0, kind), (k - 1, 1, kind), "facts"]
            if k == m - 2 and kind == 1:
                sends.append(("other picks", "away picks", core))
            if k == m - 1 and kind == 1:
                waits += ["other picks", "early own", "values", "returns"]
            f.event(waits, sends)
            if k == m - 1 and kind == 0:
                while have["facts"].shape[0] < paths.count:
                    facts_step()
                early_own(have)
    early_other(have)
    f.event([(m - 1, 1, 0), (m - 1, 1, 1), "other sum"])
    return have


PARAMS = pltpu.CompilerParams(vmem_limit_bytes=16 * 1024 * 1024)


def cost(units, k, width, extra):
    return pl.CostEstimate(
        flops=2 * units * k * width, bytes_accessed=2 * (units * k + k * width) + extra, transcendentals=0
    )


def pick_kernel(tok, owners, hidden, *picked):
    count = hidden.shape[1] // tok
    for n, out in enumerate(picked):
        for b in range(count):
            columns = pl.ds(pl.multiple_of(owners[n * count + b] * tok, tok), tok)
            out[:, b * tok : (b + 1) * tok] = hidden[:, columns]


def pick(hidden, owners, orders, tok):
    units, tokens = hidden.shape
    rows = next(r for r in range(128, 0, -16) if units % r == 0)
    spec = pl.BlockSpec((rows, tokens), lambda i, *_: (i, 0))
    return pl.pallas_call(
        functools.partial(pick_kernel, tok),
        grid_spec=pltpu.PrefetchScalarGridSpec(
            num_scalar_prefetch=1, grid=(units // rows,), in_specs=[spec], out_specs=[spec] * orders
        ),
        out_shape=[jax.ShapeDtypeStruct(hidden.shape, hidden.dtype)] * orders,
        compiler_params=PARAMS,
        cost_estimate=cost(units, 0, 0, 2 * (1 + orders) * units * tokens),
    )(owners, hidden)


def spread(tok, owners, first, coefs, weights, pulls):
    for b in range(weights.shape[0] // tok):
        coef = coefs[:, pl.ds(pl.multiple_of(owners[first + b] * tok, tok), tok)].T
        rows = slice(b * tok, (b + 1) * tok)
        weights[rows, :] = jnp.broadcast_to(coef[:, 0:1], (tok, 128))
        pulls[rows, :] = jnp.broadcast_to(coef[:, 1:2], (tok, 128))


def form(tok, owners, first, weights, pulls, head, blocks, dstream, parts, start, chunk):
    for b in range(len(blocks)):
        rows = slice(b * tok, (b + 1) * tok)
        for at in range(0, chunk, 128):
            lanes = pl.ds(pl.multiple_of(start + at, 128), 128)
            stream_f = blocks[b][:, lanes].astype(jnp.float32)
            weight = weights[rows, :]
            dstream[rows, lanes] = (weight * head[:, lanes] - pulls[rows, :] * stream_f).astype(jnp.bfloat16)
            parts[owners[first + b], :, lanes] = jnp.sum(weight * stream_f, axis=0, keepdims=True)


def pieces_of(units):
    return next(n for n in (7, 4, 2, 1) if units % (16 * n) == 0)


def product_kernel(tok, count, first, given_count, added, parts_count, wide, chunk, owners, where, *refs):
    refs = list(refs)
    take = lambda n: [refs.pop(0) for _ in range(n)]
    (picked,) = take(1)
    coefs, head = take(2) if count else (None, None)
    blocks, given, total, other_parts = take(count), take(given_count), take(added), take(parts_count)
    (out,) = take(1)
    dstream, parts_out = take(2) if count else (None, None)
    weights, pulls, parts = take(3) if count else (None, None, None)
    out_v = take(1)[0] if wide else out
    (sem_out,) = take(1)
    half = out_v.shape[1]
    steps = half // chunk
    base = pl.multiple_of(where[0] * half, half)

    columns = lambda c: pl.ds(pl.multiple_of(c * chunk, chunk), chunk)

    def put_out(c):
        there = pl.ds(pl.multiple_of(base + c * chunk, chunk), chunk)
        return pltpu.make_async_copy(out_v.at[:, columns(c)], out.at[:, there], sem_out.at[c])

    if count:
        parts[...] = jnp.zeros_like(parts)
        spread(tok, owners, first, coefs, weights, pulls)

    def step(c, carry):
        if count:
            form(tok, owners, first, weights, pulls, head, blocks, dstream, parts, c * chunk, chunk)

        factors = ([dstream] if count else []) + given
        here = total[0][:, columns(c)] if added else None
        at = first * tok
        for factor in factors:
            depth = factor.shape[0]
            term = jnp.dot(picked[:, at : at + depth], factor[:, columns(c)], preferred_element_type=jnp.float32)
            here = term if here is None else here + term
            at += depth
        out_v[:, columns(c)] = here.astype(out_v.dtype)
        if wide:
            put_out(c).start()
        return carry

    lax.fori_loop(0, steps, step, 0)
    if count:
        if other_parts:
            parts_out[...] = sum([p[...] for p in other_parts], parts[...]).sum(axis=0)
        else:
            parts_out[...] = parts[...]
    if wide:
        for c in range(steps):
            put_out(c).wait()


def product(owners, first, picked, formed=None, given=(), total=None, parts=(), where=None):
    units, tokens = picked.shape
    coefs, head, blocks = formed or (None, None, [])
    half = blocks[0].shape[1] if blocks else given[0].shape[1]
    count = len(blocks)
    tok = tokens // owners.shape[0] * 2
    k = count * tok + sum(g.shape[0] for g in given)
    chunk = next(t for t in (512 if tokens <= 4096 else 256, 128, half) if half % t == 0)
    steps = half // chunk
    added, wide = total is not None, where is not None
    anywhere = pl.BlockSpec(memory_space=pl.ANY)
    inside = pl.BlockSpec(memory_space=pltpu.VMEM)
    in_vmem = lambda x: pltpu.with_memory_space_constraint(x, pltpu.VMEM)
    out_type = jnp.bfloat16 if added else jnp.float32
    if wide:
        out_specs = [anywhere]
        out_shape = [jax.ShapeDtypeStruct((units, 2 * half), out_type)]
    else:
        out_specs = [inside]
        out_shape = [pltpu.VMEM((units, half), out_type)]
    scratch = []
    parts_shape = (tokens // tok, 1, half)
    if count:
        out_specs += [inside, inside]
        out_shape += [
            pltpu.VMEM((count * tok, half), jnp.bfloat16),
            jax.ShapeDtypeStruct(parts_shape[1:] if parts else parts_shape, jnp.float32),
        ]
        scratch += [pltpu.VMEM((count * tok, 128), jnp.float32)] * 2 + [pltpu.VMEM(parts_shape, jnp.float32)]
    if wide:
        scratch += [pltpu.VMEM((units, half), out_type)]
    sems = [(steps,)]
    return pl.pallas_call(
        functools.partial(product_kernel, tok, count, first, len(given), int(added), len(parts), wide, chunk),
        grid_spec=pltpu.PrefetchScalarGridSpec(
            num_scalar_prefetch=2,
            grid=(),
            in_specs=[inside] * (1 + 2 * bool(count) + count + len(given) + added + len(parts)),
            out_specs=out_specs,
            scratch_shapes=scratch + [pltpu.SemaphoreType.DMA(shape) for shape in sems],
        ),
        out_shape=out_shape,
        compiler_params=PARAMS,
        cost_estimate=cost(units, k * (1 if added or given else 10), half, 6 * units * half),
    )(
        owners,
        where if wide else jnp.zeros((1,), jnp.int32),
        in_vmem(picked),
        *([coefs, head] if count else []),
        *[in_vmem(x) for x in blocks],
        *[in_vmem(x) for x in given],
        *([in_vmem(total)] if added else []),
        *parts,
    )


def put_kernel(pieces, where, part, whole, out, held, sems_in, sems_out):
    units, width = part.shape
    start = pl.multiple_of(where[0] * width, width)
    rows = [pl.ds(n * (units // pieces), units // pieces) for n in range(pieces)]
    fetch = [pltpu.make_async_copy(part.at[r, :], held.at[r, :], sems_in.at[n]) for n, r in enumerate(rows)]
    place = [
        pltpu.make_async_copy(held.at[r, :], out.at[r, pl.ds(start, width)], sems_out.at[n]) for n, r in enumerate(rows)
    ]
    for copy in fetch:
        copy.start()
    for n in range(pieces):
        fetch[n].wait()
        place[n].start()
    for copy in place:
        copy.wait()


def put(whole, part, where):
    units, width = part.shape
    pieces = pieces_of(units)
    return pl.pallas_call(
        functools.partial(put_kernel, pieces),
        grid_spec=pltpu.PrefetchScalarGridSpec(
            num_scalar_prefetch=1,
            grid=(),
            in_specs=[pl.BlockSpec(memory_space=pl.ANY)] * 2,
            out_specs=pl.BlockSpec(memory_space=pl.ANY),
            scratch_shapes=[
                pltpu.VMEM(part.shape, part.dtype),
                pltpu.SemaphoreType.DMA((pieces,)),
                pltpu.SemaphoreType.DMA((pieces,)),
            ],
        ),
        out_shape=jax.ShapeDtypeStruct(whole.shape, whole.dtype),
        input_output_aliases={2: 0},
        compiler_params=PARAMS,
        cost_estimate=cost(0, 0, 0, 4 * units * width),
    )(where, part, whole)


def all_returns(step_reward, resets):
    shards, tok = step_reward.shape
    position = jnp.arange(tok)
    earlier = position[None, :] < position[:, None]
    before = jnp.sum(jnp.where(earlier[None], resets[:, None, :], 0.0), axis=2)
    total = jnp.sum(resets, axis=1, keepdims=True)
    reach = (position[None, :] >= position[:, None])[None] & (before[:, None, :] == before[:, :, None])
    local = jnp.sum(jnp.where(reach, step_reward[:, None, :], 0.0), axis=2)
    passing = before == total
    blocked = jnp.where(passing[:, 0], 0.0, 1.0)
    ids = jnp.arange(shards)
    later = ids[None, :] > ids[:, None]
    between = later[:, None, :] & (ids[None, :] < ids[:, None])[None]
    open_path = later & (jnp.sum(jnp.where(between, blocked[None, None, :], 0.0), axis=2) == 0.0)
    incoming = jnp.sum(jnp.where(open_path, local[None, :, 0], 0.0), axis=1)
    return local + jnp.where(passing, incoming[:, None], 0.0)


def make_body(width, shards):
    paths = Paths(shards)

    def body(stream, hidden, final_gain, value_head, rewards, kl_terms, resets):
        tok, local = stream.shape
        half = local // 2
        me = lax.axis_index("seq")
        mine = me % 2
        gain = final_gain.astype(jnp.float32)
        head = gain * value_head.astype(jnp.float32)
        head_half = lax.dynamic_slice_in_dim(head, mine * half, half)[None]
        to_core = lambda x: lax.ppermute(x, "seq", paths.core)
        own = lambda a, me=me: lax.dynamic_index_in_dim(a, me, 0, keepdims=False)
        last, middle, early = block_groups(paths.m)
        table = paths.owners(last + middle + early)
        both = np.concatenate([table, table[np.arange(shards) ^ 1]], axis=1)
        owners = own(jnp.asarray(both))
        early_at = len(last + middle)

        def own_facts(stream):
            stream_f = stream.astype(jnp.float32)
            share = jnp.where(lax.axis_index("tp") == 0, 1.0, 0.0)
            return jnp.stack(
                [
                    jnp.sum(stream_f * stream_f, axis=-1),
                    jnp.sum(stream_f * head, axis=-1),
                    (rewards - 0.2 * kl_terms) * share,
                    resets.astype(jnp.float32) * share,
                ]
            )

        def early_own(have):
            sum_squares, along, step_reward, cut = (have["facts"][:, k] for k in range(4))
            scale = lax.rsqrt(sum_squares / width + EPSILON)
            values = scale * along
            returns = all_returns(step_reward, cut)
            error = values - returns
            pull = scale**3 * along / width
            coefs = jnp.stack([error * scale, error * pull]).reshape(2, shards * tok)
            coefs = jnp.pad(coefs, ((0, 6), (0, 0)))
            have.update(values=own(values, have["me"]), returns=own(returns, have["me"]), coefs=coefs)
            have["early own"], have["early dstream"], have["early parts"] = product(
                have["owners"], early_at, have["own picks"], (coefs, head_half, [have[b] for b in early])
            )

        def early_other(have):
            have["other sum"], have["middle dstream"], have["middle parts"] = product(
                have["owners"],
                len(last),
                have["other picks"],
                (have["coefs"], head_half, [have[b] for b in middle]),
                [have["early dstream"]],
            )

        where = mine[None].astype(jnp.int32)
        scalars = {"core": mine, "me": me, "first core": mine == 0, "where": where, "elsewhere": 1 - where}
        scalars.update({"low %d" % n: (me >> n) % 2 == 0 for n in range(shards.bit_length() - 1)})
        scalars["owners"] = owners
        have = run_plan(stream, scalars, own_facts, paths, lambda: pick(hidden, owners, 2, tok), early_own, early_other)
        out, dstream, grad_head = product(
            have["owners"],
            0,
            have["other picks"],
            (have["coefs"], head_half, [have[b] for b in last]),
            (),
            have["other sum"],
            [have["early parts"], have["middle parts"]],
        )
        swapped = to_core(out)
        grad_head = grad_head[0]
        other_head = to_core(grad_head)
        grad_head = gain * jnp.where(
            have["first core"], jnp.concatenate([grad_head, other_head]), jnp.concatenate([other_head, grad_head])
        )
        (grad_down,) = product(
            have["owners"], 0, have["own picks"], None, [dstream, have["middle dstream"]], have["early own"], (), have["where"]
        )
        grad_down = put(grad_down, swapped, have["elsewhere"])
        return (have["values"], have["returns"], grad_head, grad_down)

    return body


def solution(mesh):
    placed = (P("seq", "tp"), P("seq", None), P("tp"), P("tp"), P("seq"), P("seq"), P("seq"))

    def run(stream, *rest):
        return jax.shard_map(
            make_body(stream.shape[1], mesh.shape["seq"]),
            mesh=mesh,
            in_specs=placed,
            out_specs=(P("seq"), P("seq"), P("tp"), P("seq", "tp")),
            check_vma=False,
        )(stream, *rest)

    return run
```

```python
import functools

import jax
import jax.numpy as jnp
import numpy as np
from jax import lax
from jax.experimental import pallas as pl
from jax.experimental.pallas import tpu as pltpu
from jax.sharding import PartitionSpec as P

EPSILON = 1e-05


def butterfly_sum(x, axis):
    count = lax.axis_size(axis)
    step = 1
    while step < count:
        x = x + lax.ppermute(x, axis, [(i, i ^ step) for i in range(count)])
        step *= 2
    return x


def butterfly_step(x, axis, low):
    count = lax.axis_size(axis)
    step = x.shape[0]
    if step >= count:
        return x
    other = lax.ppermute(x, axis, [(i, i ^ step) for i in range(count)])
    if step > 2:
        return jnp.concatenate([jnp.where(low[step], x, other), jnp.where(low[step], other, x)])
    first = lax.broadcasted_iota(jnp.int32, (2, *x.shape), 0) == 0
    return jnp.where(first == low[step], x[None], other[None]).reshape(2 * step, *x.shape[1:])


class Paths:
    def __init__(self, count):
        self.count = count
        self.m = count // 4
        self.order = list(range(0, self.m, 2)) + list(range(self.m - 1 - self.m % 2, 0, -2))
        self.place = [self.order.index(z) for z in range(self.m)]
        self.across = [(i, i ^ 2) for i in range(count)]
        self.core = [(i, i ^ 1) for i in range(count)]
        self.ring = [self._ring(1), self._ring(-1)]

    def _ring(self, way):
        pairs = []
        for i in range(self.count):
            z, rest = divmod(i, 4)
            by = way if i % 2 == 0 else -way
            pairs.append((i, self.order[(self.place[z] + by) % self.m] * 4 + rest))
        return pairs

    def owners(self, blocks):
        table = np.zeros((self.count, len(blocks)), np.int32)
        for me in range(self.count):
            z, rest = divmod(me, 4)
            for b, (steps, across, kind) in enumerate(blocks):
                way = -1 if (me % 2 == 0) == (kind == 0) else 1
                table[me, b] = self.order[(self.place[z] + way * steps) % self.m] * 4 + (rest ^ (2 * across + kind))
        return table


class Flights:
    def __init__(self, **arrays):
        self.have = arrays

    def event(self, waits, sends=()):
        names = list(dict.fromkeys([*waits, *(source for _, source, _ in sends)]))
        self.have.update(zip(names, lax.optimization_barrier(tuple(self.have[n] for n in names))))
        for name, source, pairs in sends:
            self.have[name] = lax.ppermute(self.have[source], "seq", pairs)


def block_groups(m):
    last = [(m - 1, 1, 0), (m - 1, 1, 1)]
    middle = [(m - 2, 1, 0), (m - 2, 1, 1), (m - 1, 0, 0), (m - 1, 0, 1)]
    early = [(k, a, kind) for k in range(m - 1) for a in range(2) for kind in range(2) if k < m - 2 or a == 0]
    return last, middle, early


def run_plan(stream, scalars, own_facts, paths, pick_both, early_own, early_other):
    half = stream.shape[1] // 2
    m, ring, across, core = paths.m, paths.ring, paths.across, paths.core
    cut = lambda c: lax.dynamic_slice_in_dim(stream, c * half, half, 1)
    core_index = scalars["core"]
    f = Flights(stream=stream, away=cut(1 - core_index), **scalars)
    f.have[0, 0, 0] = cut(core_index)
    have = f.have
    names = list(scalars)
    low = lambda: {1 << n: have["low %d" % n] for n in range(paths.count.bit_length() - 1)}

    def facts_step():
        have["facts"] = butterfly_step(have["facts"], "seq", low())

    f.event([], [((1, 0, 0), (0, 0, 0), ring[0]), ((0, 1, 0), (0, 0, 0), across), ((0, 0, 1), "away", core)])
    f.event(
        [(0, 0, 1), "stream", *names],
        [((1, 0, 1), (0, 0, 1), ring[1]), ((0, 1, 1), (0, 0, 1), across)],
    )
    have["facts"] = butterfly_sum(own_facts(have["stream"]), "tp")[None]
    have["own picks"], have["away picks"] = pick_both()
    f.event(
        [(1, 0, 0), (0, 1, 0), "facts", "own picks", "away picks"],
        [((2, 0, 0), (1, 0, 0), ring[0]), ((1, 1, 0), (1, 0, 0), across)],
    )
    facts_step()
    facts_step()
    f.event([(1, 0, 1), (0, 1, 1), "facts"], [((2, 0, 1), (1, 0, 1), ring[1]), ((1, 1, 1), (1, 0, 1), across)])
    for k in range(2, m):
        for kind in range(2):
            facts_step()
            if k < m - 1:
                sends = [((k + 1, 0, kind), (k, 0, kind), ring[kind]), ((k, 1, kind), (k, 0, kind), across)]
            elif kind == 0:
                sends = [((k, 1, kind), (k - 1, 1, kind), ring[kind])]
            else:
                sends = [((k, 1, kind), (k, 0, kind), across)]
            waits = [(k, 0, kind), (k - 1, 1, kind), "facts"]
            if k == m - 2 and kind == 1:
                sends.append(("other picks", "away picks", core))
            if k == m - 1 and kind == 1:
                waits += ["other picks", "early own", "values", "returns"]
            f.event(waits, sends)
            if k == m - 2 and kind == 1:
                while have["facts"].shape[0] < paths.count:
                    facts_step()
                early_own(have)
    early_other(have)
    f.event([(m - 1, 1, 0), (m - 1, 1, 1), "other sum"])
    return have


PARAMS = pltpu.CompilerParams(vmem_limit_bytes=16 * 1024 * 1024)


def cost(units, k, width, extra):
    return pl.CostEstimate(
        flops=2 * units * k * width, bytes_accessed=2 * (units * k + k * width) + extra, transcendentals=0
    )


def pick_kernel(tok, owners, hidden, *picked):
    count = hidden.shape[1] // tok
    for n, out in enumerate(picked):
        for b in range(count):
            columns = pl.ds(pl.multiple_of(owners[n * count + b] * tok, tok), tok)
            out[:, b * tok : (b + 1) * tok] = hidden[:, columns]


def pick(hidden, owners, orders, tok):
    units, tokens = hidden.shape
    rows = next(r for r in range(128, 0, -16) if units % r == 0)
    spec = pl.BlockSpec((rows, tokens), lambda i, *_: (i, 0))
    return pl.pallas_call(
        functools.partial(pick_kernel, tok),
        grid_spec=pltpu.PrefetchScalarGridSpec(
            num_scalar_prefetch=1, grid=(units // rows,), in_specs=[spec], out_specs=[spec] * orders
        ),
        out_shape=[jax.ShapeDtypeStruct(hidden.shape, hidden.dtype)] * orders,
        compiler_params=PARAMS,
        cost_estimate=cost(units, 0, 0, 2 * (1 + orders) * units * tokens),
    )(owners, hidden)


def spread(tok, owners, first, coefs, weights, pulls):
    for b in range(weights.shape[0] // tok):
        coef = coefs[:, pl.ds(pl.multiple_of(owners[first + b] * tok, tok), tok)].T
        rows = slice(b * tok, (b + 1) * tok)
        weights[rows, :] = jnp.broadcast_to(coef[:, 0:1], (tok, 128))
        pulls[rows, :] = jnp.broadcast_to(coef[:, 1:2], (tok, 128))


def form(tok, owners, first, weights, pulls, head, blocks, dstream, parts, start, chunk):
    for b in range(len(blocks)):
        rows = slice(b * tok, (b + 1) * tok)
        for at in range(0, chunk, 128):
            lanes = pl.ds(pl.multiple_of(start + at, 128), 128)
            stream_f = blocks[b][:, lanes].astype(jnp.float32)
            weight = weights[rows, :]
            dstream[rows, lanes] = (weight * head[:, lanes] - pulls[rows, :] * stream_f).astype(jnp.bfloat16)
            parts[owners[first + b], :, lanes] = jnp.sum(weight * stream_f, axis=0, keepdims=True)


def pieces_of(units):
    return next(n for n in (7, 4, 2, 1) if units % (16 * n) == 0)


def product_kernel(tok, count, first, given_count, added, parts_count, wide, chunk, owners, where, *refs):
    refs = list(refs)
    take = lambda n: [refs.pop(0) for _ in range(n)]
    (picked,) = take(1)
    coefs, head = take(2) if count else (None, None)
    blocks, given, total, other_parts = take(count), take(given_count), take(added), take(parts_count)
    (out,) = take(1)
    dstream, parts_out = take(2) if count else (None, None)
    weights, pulls, parts = take(3) if count else (None, None, None)
    out_v = take(1)[0] if wide else out
    (sem_out,) = take(1)
    half = out_v.shape[1]
    steps = half // chunk
    base = pl.multiple_of(where[0] * half, half)

    columns = lambda c: pl.ds(pl.multiple_of(c * chunk, chunk), chunk)

    def put_out(c):
        there = pl.ds(pl.multiple_of(base + c * chunk, chunk), chunk)
        return pltpu.make_async_copy(out_v.at[:, columns(c)], out.at[:, there], sem_out.at[c])

    if count:
        parts[...] = jnp.zeros_like(parts)
        spread(tok, owners, first, coefs, weights, pulls)

    def step(c, carry):
        if count:
            form(tok, owners, first, weights, pulls, head, blocks, dstream, parts, c * chunk, chunk)

        factors = ([dstream] if count else []) + given
        here = total[0][:, columns(c)] if added else None
        at = first * tok
        for factor in factors:
            depth = factor.shape[0]
            term = jnp.dot(picked[:, at : at + depth], factor[:, columns(c)], preferred_element_type=jnp.float32)
            here = term if here is None else here + term
            at += depth
        out_v[:, columns(c)] = here.astype(out_v.dtype)
        if wide:
            put_out(c).start()
        return carry

    lax.fori_loop(0, steps, step, 0)
    if count:
        if other_parts:
            parts_out[...] = sum([p[...] for p in other_parts], parts[...]).sum(axis=0)
        else:
            parts_out[...] = parts[...]
    if wide:
        for c in range(steps):
            put_out(c).wait()


def product(owners, first, picked, formed=None, given=(), total=None, parts=(), where=None):
    units, tokens = picked.shape
    coefs, head, blocks = formed or (None, None, [])
    half = blocks[0].shape[1] if blocks else given[0].shape[1]
    count = len(blocks)
    tok = tokens // owners.shape[0] * 2
    k = count * tok + sum(g.shape[0] for g in given)
    chunk = next(t for t in (512 if tokens <= 4096 else 256, 128, half) if half % t == 0)
    steps = half // chunk
    added, wide = total is not None, where is not None
    anywhere = pl.BlockSpec(memory_space=pl.ANY)
    inside = pl.BlockSpec(memory_space=pltpu.VMEM)
    in_vmem = lambda x: pltpu.with_memory_space_constraint(x, pltpu.VMEM)
    out_type = jnp.bfloat16 if added else jnp.float32
    if wide:
        out_specs = [anywhere]
        out_shape = [jax.ShapeDtypeStruct((units, 2 * half), out_type)]
    else:
        out_specs = [inside]
        out_shape = [pltpu.VMEM((units, half), out_type)]
    scratch = []
    parts_shape = (tokens // tok, 1, half)
    if count:
        out_specs += [inside, inside]
        out_shape += [
            pltpu.VMEM((count * tok, half), jnp.bfloat16),
            jax.ShapeDtypeStruct(parts_shape[1:] if parts else parts_shape, jnp.float32),
        ]
        scratch += [pltpu.VMEM((count * tok, 128), jnp.float32)] * 2 + [pltpu.VMEM(parts_shape, jnp.float32)]
    if wide:
        scratch += [pltpu.VMEM((units, half), out_type)]
    sems = [(steps,)]
    return pl.pallas_call(
        functools.partial(product_kernel, tok, count, first, len(given), int(added), len(parts), wide, chunk),
        grid_spec=pltpu.PrefetchScalarGridSpec(
            num_scalar_prefetch=2,
            grid=(),
            in_specs=[inside] * (1 + 2 * bool(count) + count + len(given) + added + len(parts)),
            out_specs=out_specs,
            scratch_shapes=scratch + [pltpu.SemaphoreType.DMA(shape) for shape in sems],
        ),
        out_shape=out_shape,
        compiler_params=PARAMS,
        cost_estimate=cost(units, k * (1 if added or given else 10), half, 6 * units * half),
    )(
        owners,
        where if wide else jnp.zeros((1,), jnp.int32),
        in_vmem(picked),
        *([coefs, head] if count else []),
        *[in_vmem(x) for x in blocks],
        *[in_vmem(x) for x in given],
        *([in_vmem(total)] if added else []),
        *parts,
    )


def put_kernel(pieces, where, part, whole, out, held, sems_in, sems_out):
    units, width = part.shape
    start = pl.multiple_of(where[0] * width, width)
    rows = [pl.ds(n * (units // pieces), units // pieces) for n in range(pieces)]
    fetch = [pltpu.make_async_copy(part.at[r, :], held.at[r, :], sems_in.at[n]) for n, r in enumerate(rows)]
    place = [
        pltpu.make_async_copy(held.at[r, :], out.at[r, pl.ds(start, width)], sems_out.at[n]) for n, r in enumerate(rows)
    ]
    for copy in fetch:
        copy.start()
    for n in range(pieces):
        fetch[n].wait()
        place[n].start()
    for copy in place:
        copy.wait()


def put(whole, part, where):
    units, width = part.shape
    pieces = pieces_of(units)
    return pl.pallas_call(
        functools.partial(put_kernel, pieces),
        grid_spec=pltpu.PrefetchScalarGridSpec(
            num_scalar_prefetch=1,
            grid=(),
            in_specs=[pl.BlockSpec(memory_space=pl.ANY)] * 2,
            out_specs=pl.BlockSpec(memory_space=pl.ANY),
            scratch_shapes=[
                pltpu.VMEM(part.shape, part.dtype),
                pltpu.SemaphoreType.DMA((pieces,)),
                pltpu.SemaphoreType.DMA((pieces,)),
            ],
        ),
        out_shape=jax.ShapeDtypeStruct(whole.shape, whole.dtype),
        input_output_aliases={2: 0},
        compiler_params=PARAMS,
        cost_estimate=cost(0, 0, 0, 4 * units * width),
    )(where, part, whole)


def all_returns(step_reward, resets):
    shards, tok = step_reward.shape
    position = jnp.arange(tok)
    earlier = position[None, :] < position[:, None]
    before = jnp.sum(jnp.where(earlier[None], resets[:, None, :], 0.0), axis=2)
    total = jnp.sum(resets, axis=1, keepdims=True)
    reach = (position[None, :] >= position[:, None])[None] & (before[:, None, :] == before[:, :, None])
    local = jnp.sum(jnp.where(reach, step_reward[:, None, :], 0.0), axis=2)
    passing = before == total
    blocked = jnp.where(passing[:, 0], 0.0, 1.0)
    ids = jnp.arange(shards)
    later = ids[None, :] > ids[:, None]
    between = later[:, None, :] & (ids[None, :] < ids[:, None])[None]
    open_path = later & (jnp.sum(jnp.where(between, blocked[None, None, :], 0.0), axis=2) == 0.0)
    incoming = jnp.sum(jnp.where(open_path, local[None, :, 0], 0.0), axis=1)
    return local + jnp.where(passing, incoming[:, None], 0.0)


def make_body(width, shards):
    paths = Paths(shards)

    def body(stream, hidden, final_gain, value_head, rewards, kl_terms, resets):
        tok, local = stream.shape
        half = local // 2
        me = lax.axis_index("seq")
        mine = me % 2
        gain = final_gain.astype(jnp.float32)
        head = gain * value_head.astype(jnp.float32)
        head_half = lax.dynamic_slice_in_dim(head, mine * half, half)[None]
        to_core = lambda x: lax.ppermute(x, "seq", paths.core)
        own = lambda a: lax.dynamic_index_in_dim(a, me, 0, keepdims=False)
        last, middle, early = block_groups(paths.m)
        table = paths.owners(last + middle + early)
        both = np.concatenate([table, table[np.arange(shards) ^ 1]], axis=1)
        owners = own(jnp.asarray(both))
        early_at = len(last + middle)

        def own_facts(stream):
            stream_f = stream.astype(jnp.float32)
            share = jnp.where(lax.axis_index("tp") == 0, 1.0, 0.0)
            return jnp.stack(
                [
                    jnp.sum(stream_f * stream_f, axis=-1),
                    jnp.sum(stream_f * head, axis=-1),
                    (rewards - 0.2 * kl_terms) * share,
                    resets.astype(jnp.float32) * share,
                ]
            )

        def early_own(have):
            sum_squares, along, step_reward, cut = (have["facts"][:, k] for k in range(4))
            scale = lax.rsqrt(sum_squares / width + EPSILON)
            values = scale * along
            returns = all_returns(step_reward, cut)
            error = values - returns
            pull = scale**3 * along / width
            coefs = jnp.stack([error * scale, error * pull]).reshape(2, shards * tok)
            coefs = jnp.pad(coefs, ((0, 6), (0, 0)))
            mask = jnp.arange(shards)[:, None] == have["me"]
            row = lambda a: jnp.sum(jnp.where(mask, a, 0.0), axis=0)
            have.update(values=row(values), returns=row(returns), coefs=coefs)
            have["early own"], have["early dstream"], have["early parts"] = product(
                have["owners"], early_at, have["own picks"], (coefs, head_half, [have[b] for b in early])
            )

        def early_other(have):
            have["other sum"], have["middle dstream"], have["middle parts"] = product(
                have["owners"],
                len(last),
                have["other picks"],
                (have["coefs"], head_half, [have[b] for b in middle]),
                [have["early dstream"]],
            )

        where = mine[None].astype(jnp.int32)
        scalars = {"core": mine, "me": me, "first core": mine == 0, "where": where, "elsewhere": 1 - where}
        scalars.update({"low %d" % n: (me >> n) % 2 == 0 for n in range(shards.bit_length() - 1)})
        scalars["owners"] = owners
        have = run_plan(stream, scalars, own_facts, paths, lambda: pick(hidden, owners, 2, tok), early_own, early_other)
        out, dstream, grad_head = product(
            have["owners"],
            0,
            have["other picks"],
            (have["coefs"], head_half, [have[b] for b in last]),
            (),
            have["other sum"],
            [have["early parts"], have["middle parts"]],
        )
        swapped = to_core(out)
        grad_head = grad_head[0]
        other_head = to_core(grad_head)
        grad_head = gain * jnp.where(
            have["first core"], jnp.concatenate([grad_head, other_head]), jnp.concatenate([other_head, grad_head])
        )
        (grad_down,) = product(
            have["owners"], 0, have["own picks"], None, [dstream, have["middle dstream"]], have["early own"], (), have["where"]
        )
        grad_down = put(grad_down, swapped, have["elsewhere"])
        return (have["values"], have["returns"], grad_head, grad_down)

    return body


def solution(mesh):
    placed = (P("seq", "tp"), P("seq", None), P("tp"), P("tp"), P("seq"), P("seq"), P("seq"))

    def run(stream, *rest):
        return jax.shard_map(
            make_body(stream.shape[1], mesh.shape["seq"]),
            mesh=mesh,
            in_specs=placed,
            out_specs=(P("seq"), P("seq"), P("tp"), P("seq", "tp")),
            check_vma=False,
        )(stream, *rest)

    return run
```

```python
import functools

import jax
import jax.numpy as jnp
import numpy as np
from jax import lax
from jax.experimental import pallas as pl
from jax.experimental.pallas import tpu as pltpu
from jax.sharding import PartitionSpec as P

EPSILON = 1e-05


def butterfly_sum(x, axis):
    count = lax.axis_size(axis)
    step = 1
    while step < count:
        x = x + lax.ppermute(x, axis, [(i, i ^ step) for i in range(count)])
        step *= 2
    return x


def butterfly_send(x, axis):
    return lax.ppermute(x, axis, [(i, i ^ x.shape[0]) for i in range(lax.axis_size(axis))])


def butterfly_merge(x, other, low):
    low = low[x.shape[0]]
    if low.ndim:
        return jnp.where(low[:, None, None], jnp.concatenate([x, x]), jnp.concatenate([other, other]))
    return jnp.concatenate([jnp.where(low, x, other), jnp.where(low, other, x)])


class Paths:
    def __init__(self, count):
        self.count = count
        self.m = count // 4
        self.order = list(range(0, self.m, 2)) + list(range(self.m - 1 - self.m % 2, 0, -2))
        self.place = [self.order.index(z) for z in range(self.m)]
        self.across = [(i, i ^ 2) for i in range(count)]
        self.core = [(i, i ^ 1) for i in range(count)]
        self.ring = [self._ring(1), self._ring(-1)]

    def _ring(self, way):
        pairs = []
        for i in range(self.count):
            z, rest = divmod(i, 4)
            by = way if i % 2 == 0 else -way
            pairs.append((i, self.order[(self.place[z] + by) % self.m] * 4 + rest))
        return pairs

    def owners(self, blocks):
        table = np.zeros((self.count, len(blocks)), np.int32)
        for me in range(self.count):
            z, rest = divmod(me, 4)
            for b, (steps, across, kind) in enumerate(blocks):
                way = -1 if (me % 2 == 0) == (kind == 0) else 1
                table[me, b] = self.order[(self.place[z] + way * steps) % self.m] * 4 + (rest ^ (2 * across + kind))
        return table


class Flights:
    def __init__(self, **arrays):
        self.have = arrays

    def event(self, waits, sends=()):
        names = list(dict.fromkeys([*waits, *(source for _, source, _ in sends)]))
        self.have.update(zip(names, lax.optimization_barrier(tuple(self.have[n] for n in names))))
        for name, source, pairs in sends:
            self.have[name] = lax.ppermute(self.have[source], "seq", pairs)


def block_groups(m):
    last = [(m - 1, 1, 0), (m - 1, 1, 1)]
    middle = [(m - 2, 1, 0), (m - 2, 1, 1), (m - 1, 0, 0), (m - 1, 0, 1)]
    early = [(k, a, kind) for k in range(m - 1) for a in range(2) for kind in range(2) if k < m - 2 or a == 0]
    return last, middle, early


def run_plan(stream, scalars, own_facts, paths, pick_both, early_own, early_other):
    half = stream.shape[1] // 2
    m, ring, across, core = paths.m, paths.ring, paths.across, paths.core
    cut = lambda c: lax.dynamic_slice_in_dim(stream, c * half, half, 1)
    core_index = scalars["core"]
    f = Flights(stream=stream, away=cut(1 - core_index), **scalars)
    f.have[0, 0, 0] = cut(core_index)
    have = f.have
    names = list(scalars)
    low = lambda: {1 << n: have["low %d" % n] for n in range(paths.count.bit_length() - 1)}

    def facts_send():
        have["other facts"] = butterfly_send(have["facts"], "seq")

    def facts_merge():
        have["facts"] = butterfly_merge(have["facts"], have["other facts"], low())

    def facts_step():
        if have["facts"].shape[0] < paths.count:
            facts_send()
            facts_merge()

    f.event([], [((1, 0, 0), (0, 0, 0), ring[0]), ((0, 1, 0), (0, 0, 0), across), ((0, 0, 1), "away", core)])
    f.event(
        [(0, 0, 1), "stream", *names],
        [((1, 0, 1), (0, 0, 1), ring[1]), ((0, 1, 1), (0, 0, 1), across)],
    )
    have["facts"] = butterfly_sum(own_facts(have["stream"]), "tp")[None]
    f.event(
        [(1, 0, 0), (0, 1, 0), "facts"],
        [((2, 0, 0), (1, 0, 0), ring[0]), ((1, 1, 0), (1, 0, 0), across)],
    )
    have["own picks"], have["away picks"] = pick_both()
    facts_step()
    facts_send()
    f.event([(1, 0, 1), (0, 1, 1), "facts", "other facts", "own picks", "away picks"], [((2, 0, 1), (1, 0, 1), ring[1]), ((1, 1, 1), (1, 0, 1), across)])
    facts_merge()
    for k in range(2, m):
        for kind in range(2):
            facts_step()
            if k < m - 1:
                sends = [((k + 1, 0, kind), (k, 0, kind), ring[kind]), ((k, 1, kind), (k, 0, kind), across)]
            elif kind == 0:
                sends = []
            else:
                sends = [((k, 1, 0), (k - 1, 1, 0), ring[0]), ((k, 1, 1), (k, 0, 1), across)]
            waits = [(k, 0, kind), (k - 1, 1, kind), "facts"]
            if k == m - 2 and kind == 1:
                sends.append(("other picks", "away picks", core))
            if k == m - 1 and kind == 1:
                waits += ["other picks", "early own", "values", "returns"]
            f.event(waits, sends)
            if k == m - 2 and kind == 1:
                while have["facts"].shape[0] < paths.count:
                    facts_step()
                early_own(have)
    early_other(have)
    f.event([(m - 1, 1, 0), (m - 1, 1, 1), "other sum"])
    return have


def params(tokens):
    return pltpu.CompilerParams(vmem_limit_bytes=(16 if tokens <= 4096 else 40) * 1024 * 1024)


def cost(units, k, width, extra):
    return pl.CostEstimate(
        flops=2 * units * k * width, bytes_accessed=2 * (units * k + k * width) + extra, transcendentals=0
    )


def pick_kernel(tok, owners, hidden, *picked):
    count = hidden.shape[1] // tok
    for n, out in enumerate(picked):
        for b in range(count):
            columns = pl.ds(pl.multiple_of(owners[n * count + b] * tok, tok), tok)
            out[:, b * tok : (b + 1) * tok] = hidden[:, columns]


def pick(hidden, owners, tok):
    orders = 2
    units, tokens = hidden.shape
    rows = next(r for r in range(128, 0, -16) if units % r == 0)
    spec = pl.BlockSpec((rows, tokens), lambda i, *_: (i, 0))
    return pl.pallas_call(
        functools.partial(pick_kernel, tok),
        grid_spec=pltpu.PrefetchScalarGridSpec(
            num_scalar_prefetch=1, grid=(units // rows,), in_specs=[spec], out_specs=[spec] * orders
        ),
        out_shape=[pltpu.VMEM(hidden.shape, hidden.dtype), pltpu.HBM(hidden.shape, hidden.dtype)],
        compiler_params=params(tokens),
        cost_estimate=cost(0, 0, 0, 1),
    )(owners, pltpu.with_memory_space_constraint(hidden, pltpu.HBM))


def spread(tok, owners, first, coefs, weights, pulls):
    for b in range(weights.shape[0] // tok):
        coef = coefs[:, pl.ds(pl.multiple_of(owners[first + b] * tok, tok), tok)].T
        rows = slice(b * tok, (b + 1) * tok)
        weights[rows, :] = jnp.broadcast_to(coef[:, 0:1], (tok, 128))
        pulls[rows, :] = jnp.broadcast_to(coef[:, 1:2], (tok, 128))


def form(tok, owners, first, weights, pulls, head, blocks, dstream, parts, start, chunk):
    for b in range(len(blocks)):
        rows = slice(b * tok, (b + 1) * tok)
        for at in range(0, chunk, 128):
            lanes = slice(start + at, start + at + 128)
            stream_f = blocks[b][:, lanes].astype(jnp.float32)
            weight = weights[rows, :]
            dstream[rows, lanes] = (weight * head[:, lanes] - pulls[rows, :] * stream_f).astype(jnp.bfloat16)
            parts[owners[first + b], :, lanes] = jnp.sum(weight * stream_f, axis=0, keepdims=True)


def pieces_of(units):
    return next(n for n in (7, 4, 2, 1) if units % (16 * n) == 0)


def product_kernel(tok, count, first, given_count, added, parts_count, wide, chunk, owners, where, *refs):
    refs = list(refs)
    take = lambda n: [refs.pop(0) for _ in range(n)]
    (picked,) = take(1)
    coefs, head = take(2) if count else (None, None)
    blocks, given, total, other_parts = take(count), take(given_count), take(added), take(parts_count)
    (out,) = take(1)
    dstream, parts_out = take(2) if count else (None, None)
    weights, pulls, parts = take(3) if count else (None, None, None)
    out_v = take(1)[0] if wide else out
    (sem_out,) = take(1)
    half = out_v.shape[1]
    steps = half // chunk
    base = pl.multiple_of(where[0] * half, half)

    columns = lambda c: pl.ds(c * chunk, chunk)

    def put_out(c):
        there = pl.ds(pl.multiple_of(base + c * chunk, chunk), chunk)
        return pltpu.make_async_copy(out_v.at[:, columns(c)], out.at[:, there], sem_out.at[c])

    if count:
        parts[...] = jnp.zeros_like(parts)
        spread(tok, owners, first, coefs, weights, pulls)

    def form_chunk(c):
        if count and c < steps:
            form(tok, owners, first, weights, pulls, head, blocks, dstream, parts, c * chunk, chunk)

    factors = ([dstream] if count else []) + given
    form_chunk(0)
    for c in range(steps):
        form_chunk(c + 1)
        here = total[0][:, columns(c)] if added else None
        at = first * tok
        for factor in factors:
            depth = factor.shape[0]
            term = jnp.dot(picked[:, at : at + depth], factor[:, columns(c)], preferred_element_type=jnp.float32)
            here = term if here is None else here + term
            at += depth
        out_v[:, columns(c)] = here.astype(out_v.dtype)
        if wide:
            put_out(c).start()
    if count:
        if other_parts:
            parts_out[...] = sum([p[...] for p in other_parts], parts[...]).sum(axis=0)
        else:
            parts_out[...] = parts[...]
    if wide:
        for c in range(steps):
            put_out(c).wait()


def product(owners, first, picked, formed=None, given=(), total=None, parts=(), where=None):
    units, tokens = picked.shape
    coefs, head, blocks = formed or (None, None, [])
    half = blocks[0].shape[1] if blocks else given[0].shape[1]
    count = len(blocks)
    tok = tokens // owners.shape[0] * 2
    k = count * tok + sum(g.shape[0] for g in given)
    chunk = next(t for t in (512 if tokens <= 4096 else 256, 128, half) if half % t == 0)
    steps = half // chunk
    added, wide = total is not None, where is not None
    anywhere = pl.BlockSpec(memory_space=pl.ANY)
    inside = pl.BlockSpec(memory_space=pltpu.VMEM)
    in_vmem = lambda x: pltpu.with_memory_space_constraint(x, pltpu.VMEM)
    out_type = jnp.bfloat16 if added else jnp.float32
    if wide:
        out_specs = [anywhere]
        out_shape = [jax.ShapeDtypeStruct((units, 2 * half), out_type)]
    else:
        out_specs = [inside]
        out_shape = [pltpu.VMEM((units, half), out_type)]
    scratch = []
    parts_shape = (tokens // tok, 1, half)
    if count:
        out_specs += [inside, inside]
        out_shape += [
            pltpu.VMEM((count * tok, half), jnp.bfloat16),
            jax.ShapeDtypeStruct(parts_shape[1:] if parts else parts_shape, jnp.float32),
        ]
        scratch += [pltpu.VMEM((count * tok, 128), jnp.float32)] * 2 + [pltpu.VMEM(parts_shape, jnp.float32)]
    if wide:
        scratch += [pltpu.VMEM((units, half), out_type)]
    sems = [(steps,)]
    return pl.pallas_call(
        functools.partial(product_kernel, tok, count, first, len(given), int(added), len(parts), wide, chunk),
        grid_spec=pltpu.PrefetchScalarGridSpec(
            num_scalar_prefetch=2,
            grid=(),
            in_specs=[inside] * (1 + 2 * bool(count) + count + len(given) + added + len(parts)),
            out_specs=out_specs,
            scratch_shapes=scratch + [pltpu.SemaphoreType.DMA(shape) for shape in sems],
        ),
        out_shape=out_shape,
        compiler_params=params(tokens),
        cost_estimate=cost(units, k * (1 if added or given else 10), half, 6 * units * half),
    )(
        owners,
        where if wide else jnp.zeros((1,), jnp.int32),
        in_vmem(picked),
        *([coefs, head] if count else []),
        *[in_vmem(x) for x in blocks],
        *[in_vmem(x) for x in given],
        *([in_vmem(total)] if added else []),
        *parts,
    )


def put_kernel(pieces, where, part, whole, out, held, sems_in, sems_out):
    units, width = part.shape
    start = pl.multiple_of(where[0] * width, width)
    rows = [pl.ds(n * (units // pieces), units // pieces) for n in range(pieces)]
    fetch = [pltpu.make_async_copy(part.at[r, :], held.at[r, :], sems_in.at[n]) for n, r in enumerate(rows)]
    place = [
        pltpu.make_async_copy(held.at[r, :], out.at[r, pl.ds(start, width)], sems_out.at[n]) for n, r in enumerate(rows)
    ]
    for copy in fetch:
        copy.start()
    for n in range(pieces):
        fetch[n].wait()
        place[n].start()
    for copy in place:
        copy.wait()


def put(whole, part, where):
    units, width = part.shape
    pieces = pieces_of(units)
    return pl.pallas_call(
        functools.partial(put_kernel, pieces),
        grid_spec=pltpu.PrefetchScalarGridSpec(
            num_scalar_prefetch=1,
            grid=(),
            in_specs=[pl.BlockSpec(memory_space=pl.ANY)] * 2,
            out_specs=pl.BlockSpec(memory_space=pl.ANY),
            scratch_shapes=[
                pltpu.VMEM(part.shape, part.dtype),
                pltpu.SemaphoreType.DMA((pieces,)),
                pltpu.SemaphoreType.DMA((pieces,)),
            ],
        ),
        out_shape=jax.ShapeDtypeStruct(whole.shape, whole.dtype),
        input_output_aliases={2: 0},
        compiler_params=params(0),
        cost_estimate=cost(0, 0, 0, 4 * units * width),
    )(where, part, whole)


def all_returns(step_reward, resets):
    shards, tok = step_reward.shape
    position = jnp.arange(tok)
    earlier = position[None, :] < position[:, None]
    before = jnp.sum(jnp.where(earlier[None], resets[:, None, :], 0.0), axis=2)
    total = jnp.sum(resets, axis=1, keepdims=True)
    reach = (position[None, :] >= position[:, None])[None] & (before[:, None, :] == before[:, :, None])
    local = jnp.sum(jnp.where(reach, step_reward[:, None, :], 0.0), axis=2)
    passing = before == total
    blocked = jnp.where(passing[:, 0], 0.0, 1.0)
    ids = jnp.arange(shards)
    later = ids[None, :] > ids[:, None]
    between = later[:, None, :] & (ids[None, :] < ids[:, None])[None]
    open_path = later & (jnp.sum(jnp.where(between, blocked[None, None, :], 0.0), axis=2) == 0.0)
    incoming = jnp.sum(jnp.where(open_path, local[None, :, 0], 0.0), axis=1)
    return local + jnp.where(passing, incoming[:, None], 0.0)


def make_body(width, shards):
    paths = Paths(shards)

    def body(stream, hidden, final_gain, value_head, rewards, kl_terms, resets):
        tok, local = stream.shape
        half = local // 2
        me = lax.axis_index("seq")
        mine = me % 2
        gain = final_gain.astype(jnp.float32)
        head = gain * value_head.astype(jnp.float32)
        head_half = lax.dynamic_slice_in_dim(head, mine * half, half)[None]
        to_core = lambda x: lax.ppermute(x, "seq", paths.core)
        own = lambda a: lax.dynamic_index_in_dim(a, me, 0, keepdims=False)
        last, middle, early = block_groups(paths.m)
        table = paths.owners(last + middle + early)
        both = np.concatenate([table, table[np.arange(shards) ^ 1]], axis=1)
        owners = own(jnp.asarray(both))
        early_at = len(last + middle)

        def own_facts(stream):
            stream_f = stream.astype(jnp.float32)
            share = jnp.where(lax.axis_index("tp") == 0, 1.0, 0.0)
            return jnp.stack(
                [
                    jnp.sum(stream_f * stream_f, axis=-1),
                    jnp.sum(stream_f * head, axis=-1),
                    (rewards - 0.2 * kl_terms) * share,
                    resets.astype(jnp.float32) * share,
                ]
            )

        def early_own(have):
            sum_squares, along, step_reward, cut = (have["facts"][:, k] for k in range(4))
            scale = lax.rsqrt(sum_squares / width + EPSILON)
            values = scale * along
            returns = all_returns(step_reward, cut)
            error = values - returns
            pull = scale**3 * along / width
            coefs = jnp.stack([error * scale, error * pull]).reshape(2, shards * tok)
            coefs = jnp.pad(coefs, ((0, 6), (0, 0)))
            mask = jnp.arange(shards)[:, None] == have["me"]
            row = lambda a: jnp.sum(jnp.where(mask, a, 0.0), axis=0)
            have.update(values=row(values), returns=row(returns), coefs=coefs)
            have["early own"], have["early dstream"], have["early parts"] = product(
                have["owners"], early_at, have["own picks"], (coefs, head_half, [have[b] for b in early])
            )

        def early_other(have):
            have["other sum"], have["middle dstream"], have["middle parts"] = product(
                have["owners"],
                len(last),
                have["other picks"],
                (have["coefs"], head_half, [have[b] for b in middle]),
                [have["early dstream"]],
            )

        where = mine[None].astype(jnp.int32)
        scalars = {"core": mine, "me": me, "first core": mine == 0, "where": where, "elsewhere": 1 - where}
        for n in range(shards.bit_length() - 1):
            low = (me >> n) % 2 == 0
            scalars["low %d" % n] = low if n > 1 else (jnp.arange(2 << n) < 1 << n) == low
        scalars["owners"] = owners
        have = run_plan(stream, scalars, own_facts, paths, lambda: pick(hidden, owners, tok), early_own, early_other)
        out, dstream, grad_head = product(
            have["owners"],
            0,
            have["other picks"],
            (have["coefs"], head_half, [have[b] for b in last]),
            (),
            have["other sum"],
            [have["early parts"], have["middle parts"]],
        )
        swapped = to_core(out)
        grad_head = grad_head[0]
        other_head = to_core(grad_head)
        grad_head = gain * jnp.where(
            have["first core"], jnp.concatenate([grad_head, other_head]), jnp.concatenate([other_head, grad_head])
        )
        (grad_down,) = product(
            have["owners"], 0, have["own picks"], None, [dstream, have["middle dstream"]], have["early own"], (), have["where"]
        )
        grad_down = put(grad_down, swapped, have["elsewhere"])
        return (have["values"], have["returns"], grad_head, grad_down)

    return body


def solution(mesh):
    placed = (P("seq", "tp"), P("seq", None), P("tp"), P("tp"), P("seq"), P("seq"), P("seq"))

    def run(stream, *rest):
        return jax.shard_map(
            make_body(stream.shape[1], mesh.shape["seq"]),
            mesh=mesh,
            in_specs=placed,
            out_specs=(P("seq"), P("seq"), P("tp"), P("seq", "tp")),
            check_vma=False,
        )(stream, *rest)

    return run
```

```python
import functools

import jax
import jax.numpy as jnp
import numpy as np
from jax import lax
from jax.experimental import pallas as pl
from jax.experimental.pallas import tpu as pltpu
from jax.sharding import PartitionSpec as P

EPSILON = 1e-05


def butterfly_sum(x, axis):
    count = lax.axis_size(axis)
    step = 1
    while step < count:
        x = x + lax.ppermute(x, axis, [(i, i ^ step) for i in range(count)])
        step *= 2
    return x


def butterfly_send(x, axis):
    return lax.ppermute(x, axis, [(i, i ^ x.shape[0]) for i in range(lax.axis_size(axis))])


def butterfly_merge(x, other, low):
    low = low[x.shape[0]]
    if low.ndim:
        return jnp.where(low[:, None, None], jnp.concatenate([x, x]), jnp.concatenate([other, other]))
    return jnp.concatenate([jnp.where(low, x, other), jnp.where(low, other, x)])


class Paths:
    def __init__(self, count):
        self.count = count
        self.m = count // 4
        self.order = list(range(0, self.m, 2)) + list(range(self.m - 1 - self.m % 2, 0, -2))
        self.place = [self.order.index(z) for z in range(self.m)]
        self.across = [(i, i ^ 2) for i in range(count)]
        self.core = [(i, i ^ 1) for i in range(count)]
        self.ring = [self._ring(1), self._ring(-1)]

    def _ring(self, way):
        pairs = []
        for i in range(self.count):
            z, rest = divmod(i, 4)
            by = way if i % 2 == 0 else -way
            pairs.append((i, self.order[(self.place[z] + by) % self.m] * 4 + rest))
        return pairs

    def owners(self, blocks):
        table = np.zeros((self.count, len(blocks)), np.int32)
        for me in range(self.count):
            z, rest = divmod(me, 4)
            for b, (steps, across, kind) in enumerate(blocks):
                way = -1 if (me % 2 == 0) == (kind == 0) else 1
                table[me, b] = self.order[(self.place[z] + way * steps) % self.m] * 4 + (rest ^ (2 * across + kind))
        return table


class Flights:
    def __init__(self, **arrays):
        self.have = arrays

    def event(self, waits, sends=()):
        names = list(dict.fromkeys([*waits, *(source for _, source, _ in sends)]))
        self.have.update(zip(names, lax.optimization_barrier(tuple(self.have[n] for n in names))))
        for name, source, pairs in sends:
            self.have[name] = lax.ppermute(self.have[source], "seq", pairs)


def block_groups(m):
    last = [(m - 1, 1, 0), (m - 1, 1, 1)]
    middle = [(m - 2, 1, 0), (m - 2, 1, 1), (m - 1, 0, 0), (m - 1, 0, 1)]
    early = [(k, a, kind) for k in range(m - 1) for a in range(2) for kind in range(2) if k < m - 2 or a == 0]
    return last, middle, early


def run_plan(stream, hidden, scalars, own_facts, paths, pick_both, early_own, early_other):
    half = stream.shape[1] // 2
    m, ring, across, core = paths.m, paths.ring, paths.across, paths.core
    cut = lambda c: lax.dynamic_slice_in_dim(stream, c * half, half, 1)
    core_index = scalars["core"]
    f = Flights(stream=stream, hidden=hidden, away=cut(1 - core_index), **scalars)
    f.have[0, 0, 0] = cut(core_index)
    have = f.have
    names = list(scalars)
    low = lambda: {1 << n: have["low %d" % n] for n in range(paths.count.bit_length() - 1)}

    def facts_send():
        have["other facts"] = butterfly_send(have["facts"], "seq")

    def facts_merge():
        have["facts"] = butterfly_merge(have["facts"], have["other facts"], low())

    def facts_step():
        if have["facts"].shape[0] < paths.count:
            facts_send()
            facts_merge()

    f.event([], [((1, 0, 0), (0, 0, 0), ring[0]), ((0, 1, 0), (0, 0, 0), across), ((0, 0, 1), "away", core)])
    f.event(
        [(0, 0, 1), "stream", *names],
        [((1, 0, 1), (0, 0, 1), ring[1]), ((0, 1, 1), (0, 0, 1), across)],
    )
    have["facts"] = butterfly_sum(own_facts(have["stream"]), "tp")[None]
    f.event(["facts", "hidden"])
    have["own picks"], have["away picks"] = pick_both(have["hidden"])
    f.event(
        [(1, 0, 0), (0, 1, 0), "facts", "own picks", "away picks"],
        [((2, 0, 0), (1, 0, 0), ring[0]), ((1, 1, 0), (1, 0, 0), across)],
    )
    facts_step()
    facts_send()
    f.event([(1, 0, 1), (0, 1, 1), "facts", "other facts"], [((2, 0, 1), (1, 0, 1), ring[1]), ((1, 1, 1), (1, 0, 1), across)])
    facts_merge()
    for k in range(2, m):
        for kind in range(2):
            facts_step()
            if k < m - 1:
                sends = [((k + 1, 0, kind), (k, 0, kind), ring[kind]), ((k, 1, kind), (k, 0, kind), across)]
            elif kind == 0:
                sends = []
            else:
                sends = [((k, 1, 0), (k - 1, 1, 0), ring[0]), ((k, 1, 1), (k, 0, 1), across)]
            waits = [(k, 0, kind), (k - 1, 1, kind), "facts"]
            if k == m - 2 and kind == 1:
                sends.append(("other picks", "away picks", core))
            if k == m - 1 and kind == 1:
                waits += ["other picks", "early own", "values", "returns"]
            f.event(waits, sends)
            if k == m - 2 and kind == 1:
                while have["facts"].shape[0] < paths.count:
                    facts_step()
                early_own(have)
    early_other(have)
    f.event([(m - 1, 1, 0), (m - 1, 1, 1), "other sum"])
    return have


def params(tokens):
    return pltpu.CompilerParams(vmem_limit_bytes=(9 if tokens <= 4096 else 40) * 1024 * 1024)


def cost(units, k, width, extra):
    return pl.CostEstimate(
        flops=2 * units * k * width, bytes_accessed=2 * (units * k + k * width) + extra, transcendentals=0
    )


def pieces_of(units):
    return next(n for n in (7, 4, 2, 1) if units % (16 * n) == 0)


def pick_kernel(tok, owners, hidden, own, away, held, turned, sems_in, sems_out):
    units, tokens = hidden.shape
    count = tokens // tok
    pieces = pieces_of(units)
    size = units // pieces
    rows = [pl.ds(n * size, size) for n in range(pieces)]
    fetch = [pltpu.make_async_copy(hidden.at[r, :], held.at[r, :], sems_in.at[n]) for n, r in enumerate(rows)]
    place = [pltpu.make_async_copy(turned.at[r, :], away.at[r, :], sems_out.at[n]) for n, r in enumerate(rows)]
    for copy in fetch:
        copy.start()
    for n, r in enumerate(rows):
        fetch[n].wait()
        for m, out in enumerate((own, turned)):
            for b in range(count):
                columns = pl.ds(pl.multiple_of(owners[m * count + b] * tok, tok), tok)
                out[r, b * tok : (b + 1) * tok] = held[r, columns]
        place[n].start()
    for copy in place:
        copy.wait()


def pick(hidden, owners, tok):
    inside = pl.BlockSpec(memory_space=pltpu.VMEM)
    anywhere = pl.BlockSpec(memory_space=pl.ANY)
    pieces = pieces_of(hidden.shape[0])
    return pl.pallas_call(
        functools.partial(pick_kernel, tok),
        grid_spec=pltpu.PrefetchScalarGridSpec(
            num_scalar_prefetch=1,
            grid=(),
            in_specs=[anywhere],
            out_specs=[inside, anywhere],
            scratch_shapes=[pltpu.VMEM(hidden.shape, hidden.dtype)] * 2 + [pltpu.SemaphoreType.DMA((pieces,))] * 2,
        ),
        out_shape=[pltpu.VMEM(hidden.shape, hidden.dtype), pltpu.HBM(hidden.shape, hidden.dtype)],
        compiler_params=params(hidden.shape[1]),
        cost_estimate=cost(0, 0, 0, 1),
    )(owners, pltpu.with_memory_space_constraint(hidden, pltpu.HBM))


def spread(tok, owners, first, coefs, weights, pulls):
    for b in range(weights.shape[0] // tok):
        coef = coefs[:, pl.ds(pl.multiple_of(owners[first + b] * tok, tok), tok)].T
        rows = slice(b * tok, (b + 1) * tok)
        weights[rows, :] = jnp.broadcast_to(coef[:, 0:1], (tok, 128))
        pulls[rows, :] = jnp.broadcast_to(coef[:, 1:2], (tok, 128))


def form(tok, owners, first, weights, pulls, head, blocks, dstream, parts, start, chunk):
    for b in range(len(blocks)):
        rows = slice(b * tok, (b + 1) * tok)
        for at in range(0, chunk, 128):
            lanes = slice(start + at, start + at + 128)
            stream_f = blocks[b][:, lanes].astype(jnp.float32)
            weight = weights[rows, :]
            dstream[rows, lanes] = (weight * head[:, lanes] - pulls[rows, :] * stream_f).astype(jnp.bfloat16)
            parts[owners[first + b], :, lanes] = jnp.sum(weight * stream_f, axis=0, keepdims=True)


def product_kernel(tok, count, first, given_count, added, parts_count, wide, chunk, owners, where, *refs):
    refs = list(refs)
    take = lambda n: [refs.pop(0) for _ in range(n)]
    (picked,) = take(1)
    coefs, head = take(2) if count else (None, None)
    blocks, given, total, other_parts = take(count), take(given_count), take(added), take(parts_count)
    (out,) = take(1)
    dstream, parts_out = take(2) if count else (None, None)
    weights, pulls, parts = take(3) if count else (None, None, None)
    out_v = take(1)[0] if wide else out
    (sem_out,) = take(1)
    half = out_v.shape[1]
    steps = half // chunk
    base = pl.multiple_of(where[0] * half, half)

    columns = lambda c: pl.ds(c * chunk, chunk)

    def put_out(c):
        there = pl.ds(pl.multiple_of(base + c * chunk, chunk), chunk)
        return pltpu.make_async_copy(out_v.at[:, columns(c)], out.at[:, there], sem_out.at[c])

    if count:
        parts[...] = jnp.zeros_like(parts)
        spread(tok, owners, first, coefs, weights, pulls)

    def form_chunk(c):
        if count and c < steps:
            form(tok, owners, first, weights, pulls, head, blocks, dstream, parts, c * chunk, chunk)

    factors = ([dstream] if count else []) + given
    form_chunk(0)
    for c in range(steps):
        form_chunk(c + 1)
        here = total[0][:, columns(c)] if added else None
        at = first * tok
        for factor in factors:
            depth = factor.shape[0]
            term = jnp.dot(picked[:, at : at + depth], factor[:, columns(c)], preferred_element_type=jnp.float32)
            here = term if here is None else here + term
            at += depth
        out_v[:, columns(c)] = here.astype(out_v.dtype)
        if wide:
            put_out(c).start()
    if count:
        if other_parts:
            parts_out[...] = sum([p[...] for p in other_parts], parts[...]).sum(axis=0)
        else:
            parts_out[...] = parts[...]
    if wide:
        for c in range(steps):
            put_out(c).wait()


def product(owners, first, picked, formed=None, given=(), total=None, parts=(), where=None):
    units, tokens = picked.shape
    coefs, head, blocks = formed or (None, None, [])
    half = blocks[0].shape[1] if blocks else given[0].shape[1]
    count = len(blocks)
    tok = tokens // owners.shape[0] * 2
    k = count * tok + sum(g.shape[0] for g in given)
    chunk = next(t for t in (512 if tokens <= 4096 else 256, 128, half) if half % t == 0)
    steps = half // chunk
    added, wide = total is not None, where is not None
    anywhere = pl.BlockSpec(memory_space=pl.ANY)
    inside = pl.BlockSpec(memory_space=pltpu.VMEM)
    in_vmem = lambda x: pltpu.with_memory_space_constraint(x, pltpu.VMEM)
    out_type = jnp.bfloat16 if added else jnp.float32
    if wide:
        out_specs = [anywhere]
        out_shape = [jax.ShapeDtypeStruct((units, 2 * half), out_type)]
    else:
        out_specs = [inside]
        out_shape = [pltpu.VMEM((units, half), out_type)]
    scratch = []
    parts_shape = (tokens // tok, 1, half)
    if count:
        out_specs += [inside, inside]
        out_shape += [
            pltpu.VMEM((count * tok, half), jnp.bfloat16),
            jax.ShapeDtypeStruct(parts_shape[1:] if parts else parts_shape, jnp.float32),
        ]
        scratch += [pltpu.VMEM((count * tok, 128), jnp.float32)] * 2 + [pltpu.VMEM(parts_shape, jnp.float32)]
    if wide:
        scratch += [pltpu.VMEM((units, half), out_type)]
    sems = [(steps,)]
    return pl.pallas_call(
        functools.partial(product_kernel, tok, count, first, len(given), int(added), len(parts), wide, chunk),
        grid_spec=pltpu.PrefetchScalarGridSpec(
            num_scalar_prefetch=2,
            grid=(),
            in_specs=[inside] * (1 + 2 * bool(count) + count + len(given) + added + len(parts)),
            out_specs=out_specs,
            scratch_shapes=scratch + [pltpu.SemaphoreType.DMA(shape) for shape in sems],
        ),
        out_shape=out_shape,
        compiler_params=params(tokens),
        cost_estimate=cost(units, k * (1 if added or given else 10), half, 6 * units * half),
    )(
        owners,
        where if wide else jnp.zeros((1,), jnp.int32),
        in_vmem(picked),
        *([coefs, head] if count else []),
        *[in_vmem(x) for x in blocks],
        *[in_vmem(x) for x in given],
        *([in_vmem(total)] if added else []),
        *parts,
    )


def put_kernel(pieces, where, part, whole, out, held, sems_in, sems_out):
    units, width = part.shape
    start = pl.multiple_of(where[0] * width, width)
    rows = [pl.ds(n * (units // pieces), units // pieces) for n in range(pieces)]
    fetch = [pltpu.make_async_copy(part.at[r, :], held.at[r, :], sems_in.at[n]) for n, r in enumerate(rows)]
    place = [
        pltpu.make_async_copy(held.at[r, :], out.at[r, pl.ds(start, width)], sems_out.at[n]) for n, r in enumerate(rows)
    ]
    for copy in fetch:
        copy.start()
    for n in range(pieces):
        fetch[n].wait()
        place[n].start()
    for copy in place:
        copy.wait()


def put(whole, part, where):
    units, width = part.shape
    pieces = pieces_of(units)
    return pl.pallas_call(
        functools.partial(put_kernel, pieces),
        grid_spec=pltpu.PrefetchScalarGridSpec(
            num_scalar_prefetch=1,
            grid=(),
            in_specs=[pl.BlockSpec(memory_space=pl.ANY)] * 2,
            out_specs=pl.BlockSpec(memory_space=pl.ANY),
            scratch_shapes=[
                pltpu.VMEM(part.shape, part.dtype),
                pltpu.SemaphoreType.DMA((pieces,)),
                pltpu.SemaphoreType.DMA((pieces,)),
            ],
        ),
        out_shape=jax.ShapeDtypeStruct(whole.shape, whole.dtype),
        input_output_aliases={2: 0},
        compiler_params=params(0),
        cost_estimate=cost(0, 0, 0, 4 * units * width),
    )(where, part, whole)


def all_returns(step_reward, resets):
    shards, tok = step_reward.shape
    position = jnp.arange(tok)
    earlier = position[None, :] < position[:, None]
    before = jnp.sum(jnp.where(earlier[None], resets[:, None, :], 0.0), axis=2)
    total = jnp.sum(resets, axis=1, keepdims=True)
    reach = (position[None, :] >= position[:, None])[None] & (before[:, None, :] == before[:, :, None])
    local = jnp.sum(jnp.where(reach, step_reward[:, None, :], 0.0), axis=2)
    passing = before == total
    blocked = jnp.where(passing[:, 0], 0.0, 1.0)
    ids = jnp.arange(shards)
    later = ids[None, :] > ids[:, None]
    between = later[:, None, :] & (ids[None, :] < ids[:, None])[None]
    open_path = later & (jnp.sum(jnp.where(between, blocked[None, None, :], 0.0), axis=2) == 0.0)
    incoming = jnp.sum(jnp.where(open_path, local[None, :, 0], 0.0), axis=1)
    return local + jnp.where(passing, incoming[:, None], 0.0)


def make_body(width, shards):
    paths = Paths(shards)

    def body(stream, hidden, final_gain, value_head, rewards, kl_terms, resets):
        tok, local = stream.shape
        half = local // 2
        me = lax.axis_index("seq")
        mine = me % 2
        gain = final_gain.astype(jnp.float32)
        head = gain * value_head.astype(jnp.float32)
        head_half = lax.dynamic_slice_in_dim(head, mine * half, half)[None]
        to_core = lambda x: lax.ppermute(x, "seq", paths.core)
        own = lambda a: lax.dynamic_index_in_dim(a, me, 0, keepdims=False)
        last, middle, early = block_groups(paths.m)
        table = paths.owners(last + middle + early)
        both = np.concatenate([table, table[np.arange(shards) ^ 1]], axis=1)
        owners = own(jnp.asarray(both))
        early_at = len(last + middle)

        def own_facts(stream):
            stream_f = stream.astype(jnp.float32)
            share = jnp.where(lax.axis_index("tp") == 0, 1.0, 0.0)
            return jnp.stack(
                [
                    jnp.sum(stream_f * stream_f, axis=-1),
                    jnp.sum(stream_f * head, axis=-1),
                    (rewards - 0.2 * kl_terms) * share,
                    resets.astype(jnp.float32) * share,
                ]
            )

        def early_own(have):
            sum_squares, along, step_reward, cut = (have["facts"][:, k] for k in range(4))
            scale = lax.rsqrt(sum_squares / width + EPSILON)
            values = scale * along
            returns = all_returns(step_reward, cut)
            error = values - returns
            pull = scale**3 * along / width
            coefs = jnp.stack([error * scale, error * pull]).reshape(2, shards * tok)
            coefs = jnp.pad(coefs, ((0, 6), (0, 0)))
            mask = jnp.arange(shards)[:, None] == have["me"]
            row = lambda a: jnp.sum(jnp.where(mask, a, 0.0), axis=0)
            have.update(values=row(values), returns=row(returns), coefs=coefs)
            have["early own"], have["early dstream"], have["early parts"] = product(
                have["owners"], early_at, have["own picks"], (coefs, head_half, [have[b] for b in early])
            )

        def early_other(have):
            have["other sum"], have["middle dstream"], have["middle parts"] = product(
                have["owners"],
                len(last),
                have["other picks"],
                (have["coefs"], head_half, [have[b] for b in middle]),
                [have["early dstream"]],
            )

        where = mine[None].astype(jnp.int32)
        scalars = {"core": mine, "me": me, "first core": mine == 0, "where": where, "elsewhere": 1 - where}
        for n in range(shards.bit_length() - 1):
            low = (me >> n) % 2 == 0
            scalars["low %d" % n] = low if n > 1 else (jnp.arange(2 << n) < 1 << n) == low
        scalars["owners"] = owners
        have = run_plan(stream, hidden, scalars, own_facts, paths, lambda hidden: pick(hidden, owners, tok), early_own, early_other)
        out, dstream, grad_head = product(
            have["owners"],
            0,
            have["other picks"],
            (have["coefs"], head_half, [have[b] for b in last]),
            (),
            have["other sum"],
            [have["early parts"], have["middle parts"]],
        )
        swapped = to_core(out)
        grad_head = grad_head[0]
        other_head = to_core(grad_head)
        grad_head = gain * jnp.where(
            have["first core"], jnp.concatenate([grad_head, other_head]), jnp.concatenate([other_head, grad_head])
        )
        (grad_down,) = product(
            have["owners"], 0, have["own picks"], None, [dstream, have["middle dstream"]], have["early own"], (), have["where"]
        )
        grad_down = put(grad_down, swapped, have["elsewhere"])
        return (have["values"], have["returns"], grad_head, grad_down)

    return body


def solution(mesh):
    placed = (P("seq", "tp"), P("seq", None), P("tp"), P("tp"), P("seq"), P("seq"), P("seq"))

    def run(stream, *rest):
        return jax.shard_map(
            make_body(stream.shape[1], mesh.shape["seq"]),
            mesh=mesh,
            in_specs=placed,
            out_specs=(P("seq"), P("seq"), P("tp"), P("seq", "tp")),
            check_vma=False,
        )(stream, *rest)

    return run
```

```python
import functools

import jax
import jax.numpy as jnp
import numpy as np
from jax import lax
from jax.experimental import pallas as pl
from jax.experimental.pallas import tpu as pltpu
from jax.sharding import PartitionSpec as P

EPSILON = 1e-05


def butterfly_sum(x, axis):
    count = lax.axis_size(axis)
    step = 1
    while step < count:
        x = x + lax.ppermute(x, axis, [(i, i ^ step) for i in range(count)])
        step *= 2
    return x


def butterfly_send(x, axis, bit):
    return lax.ppermute(x, axis, [(i, i ^ bit) for i in range(lax.axis_size(axis))])


def butterfly_merge(x, other, bit, low):
    low = low[bit]
    if bit == 1:
        return jnp.where(low[:, None, None], x, other)
    if bit == 4:
        return jnp.where(low[:, None, None, None], x[None], other[None])
    if bit == 2:
        both = jnp.stack([jnp.where(low, x, other), jnp.where(low, other, x)], axis=1)
        return both.reshape(-1, *x.shape[2:])
    return jnp.concatenate([jnp.where(low, x, other), jnp.where(low, other, x)])


class Paths:
    def __init__(self, count):
        self.count = count
        self.m = count // 4
        self.order = list(range(0, self.m, 2)) + list(range(self.m - 1 - self.m % 2, 0, -2))
        self.place = [self.order.index(z) for z in range(self.m)]
        self.across = [(i, i ^ 2) for i in range(count)]
        self.core = [(i, i ^ 1) for i in range(count)]
        self.ring = [self._ring(1), self._ring(-1)]

    def _ring(self, way):
        pairs = []
        for i in range(self.count):
            z, rest = divmod(i, 4)
            by = way if i % 2 == 0 else -way
            pairs.append((i, self.order[(self.place[z] + by) % self.m] * 4 + rest))
        return pairs

    def owners(self, blocks):
        table = np.zeros((self.count, len(blocks)), np.int32)
        for me in range(self.count):
            z, rest = divmod(me, 4)
            for b, (steps, across, kind) in enumerate(blocks):
                way = -1 if (me % 2 == 0) == (kind == 0) else 1
                table[me, b] = self.order[(self.place[z] + way * steps) % self.m] * 4 + (rest ^ (2 * across + kind))
        return table


class Flights:
    def __init__(self, **arrays):
        self.have = arrays

    def event(self, waits, sends=()):
        names = list(dict.fromkeys([*waits, *(source for _, source, _ in sends)]))
        self.have.update(zip(names, lax.optimization_barrier(tuple(self.have[n] for n in names))))
        for name, source, pairs in sends:
            self.have[name] = lax.ppermute(self.have[source], "seq", pairs)


def block_groups(m):
    last = [(m - 1, 1, 0), (m - 1, 1, 1)]
    middle = [(m - 2, 1, 0), (m - 2, 1, 1), (m - 1, 0, 0), (m - 1, 0, 1)]
    early = [(k, a, kind) for k in range(m - 1) for a in range(2) for kind in range(2) if k < m - 2 or a == 0]
    return last, middle, early


def run_plan(stream, hidden, scalars, own_facts, paths, pick_both, early_own, early_other):
    half = stream.shape[1] // 2
    m, ring, across, core = paths.m, paths.ring, paths.across, paths.core
    cut = lambda c: lax.dynamic_slice_in_dim(stream, c * half, half, 1)
    core_index = scalars["core"]
    f = Flights(stream=stream, hidden=hidden, away=cut(1 - core_index), **scalars)
    f.have[0, 0, 0] = cut(core_index)
    have = f.have
    names = list(scalars)
    low = lambda: {1 << n: have["low %d" % n] for n in range(paths.count.bit_length() - 1)}

    bits = [1, 4, 2] + [8 << n for n in range(paths.count.bit_length() - 4)]

    def facts_send():
        have["other facts"] = butterfly_send(have["facts"], "seq", bits[0])

    def facts_merge():
        have["facts"] = butterfly_merge(have["facts"], have["other facts"], bits.pop(0), low())

    def facts_step():
        if bits:
            facts_send()
            facts_merge()

    f.event([], [((1, 0, 0), (0, 0, 0), ring[0]), ((0, 1, 0), (0, 0, 0), across), ((0, 0, 1), "away", core)])
    f.event(
        [(0, 0, 1), "stream", *names],
        [((1, 0, 1), (0, 0, 1), ring[1]), ((0, 1, 1), (0, 0, 1), across)],
    )
    have["facts"] = butterfly_sum(own_facts(have["stream"]), "tp")[None]
    f.event(["facts", "hidden"])
    have["own picks"], have["away picks"] = pick_both(have["hidden"])
    f.event(
        [(1, 0, 0), (0, 1, 0), "facts", "own picks", "away picks"],
        [((2, 0, 0), (1, 0, 0), ring[0]), ((1, 1, 0), (1, 0, 0), across)],
    )
    facts_step()
    facts_send()
    f.event([(1, 0, 1), (0, 1, 1), "facts", "other facts"], [((2, 0, 1), (1, 0, 1), ring[1]), ((1, 1, 1), (1, 0, 1), across)])
    facts_merge()
    for k in range(2, m):
        for kind in range(2):
            facts_step()
            if k < m - 1:
                sends = [((k + 1, 0, kind), (k, 0, kind), ring[kind]), ((k, 1, kind), (k, 0, kind), across)]
            elif kind == 0:
                sends = []
            else:
                sends = [((k, 1, 0), (k - 1, 1, 0), ring[0]), ((k, 1, 1), (k, 0, 1), across)]
            waits = [(k, 0, kind), (k - 1, 1, kind), "facts"]
            if k == m - 2 and kind == 1:
                sends.append(("other picks", "away picks", core))
            if k == m - 1 and kind == 1:
                waits += ["other picks", "early own", "values", "returns"]
            f.event(waits, sends)
            if k == m - 2 and kind == 1:
                while bits:
                    facts_step()
                early_own(have)
    early_other(have)
    f.event([(m - 1, 1, 0), (m - 1, 1, 1), "other sum"])
    return have


def params(tokens):
    return pltpu.CompilerParams(vmem_limit_bytes=(9 if tokens <= 4096 else 40) * 1024 * 1024)


def cost(units, k, width, extra):
    return pl.CostEstimate(
        flops=2 * units * k * width, bytes_accessed=2 * (units * k + k * width) + extra, transcendentals=0
    )


def pieces_of(units):
    return next(n for n in (7, 4, 2, 1) if units % (16 * n) == 0)


def pick_kernel(tok, owners, hidden, own, away, held, turned, sems_in, sems_out):
    units, tokens = hidden.shape
    count = tokens // tok
    pieces = pieces_of(units)
    size = units // pieces
    rows = [pl.ds(n * size, size) for n in range(pieces)]
    fetch = [pltpu.make_async_copy(hidden.at[r, :], held.at[r, :], sems_in.at[n]) for n, r in enumerate(rows)]
    place = [pltpu.make_async_copy(turned.at[r, :], away.at[r, :], sems_out.at[n]) for n, r in enumerate(rows)]
    for copy in fetch:
        copy.start()
    for n, r in enumerate(rows):
        fetch[n].wait()
        for m, out in enumerate((own, turned)):
            for b in range(count):
                columns = pl.ds(pl.multiple_of(owners[m * count + b] * tok, tok), tok)
                out[r, b * tok : (b + 1) * tok] = held[r, columns]
        place[n].start()
    for copy in place:
        copy.wait()


def pick(hidden, owners, tok):
    inside = pl.BlockSpec(memory_space=pltpu.VMEM)
    anywhere = pl.BlockSpec(memory_space=pl.ANY)
    pieces = pieces_of(hidden.shape[0])
    return pl.pallas_call(
        functools.partial(pick_kernel, tok),
        grid_spec=pltpu.PrefetchScalarGridSpec(
            num_scalar_prefetch=1,
            grid=(),
            in_specs=[anywhere],
            out_specs=[inside, anywhere],
            scratch_shapes=[pltpu.VMEM(hidden.shape, hidden.dtype)] * 2 + [pltpu.SemaphoreType.DMA((pieces,))] * 2,
        ),
        out_shape=[pltpu.VMEM(hidden.shape, hidden.dtype), pltpu.HBM(hidden.shape, hidden.dtype)],
        compiler_params=params(hidden.shape[1]),
        cost_estimate=cost(0, 0, 0, 1),
    )(owners, pltpu.with_memory_space_constraint(hidden, pltpu.HBM))


def spread(tok, owners, first, coefs, weights, pulls):
    for b in range(weights.shape[0] // tok):
        coef = coefs[:, pl.ds(pl.multiple_of(owners[first + b] * tok, tok), tok)].T
        rows = slice(b * tok, (b + 1) * tok)
        weights[rows, :] = jnp.broadcast_to(coef[:, 0:1], (tok, 128))
        pulls[rows, :] = jnp.broadcast_to(coef[:, 1:2], (tok, 128))


def form(tok, owners, first, weights, pulls, head, blocks, dstream, parts, start, chunk):
    for b in range(len(blocks)):
        rows = slice(b * tok, (b + 1) * tok)
        for at in range(0, chunk, 128):
            lanes = slice(start + at, start + at + 128)
            stream_f = blocks[b][:, lanes].astype(jnp.float32)
            weight = weights[rows, :]
            dstream[rows, lanes] = (weight * head[:, lanes] - pulls[rows, :] * stream_f).astype(jnp.bfloat16)
            parts[owners[first + b], :, lanes] = jnp.sum(weight * stream_f, axis=0, keepdims=True)


def product_kernel(tok, count, first, given_count, added, parts_count, wide, chunk, owners, where, *refs):
    refs = list(refs)
    take = lambda n: [refs.pop(0) for _ in range(n)]
    (picked,) = take(1)
    coefs, head = take(2) if count else (None, None)
    blocks, given, total, other_parts = take(count), take(given_count), take(added), take(parts_count)
    (out,) = take(1)
    dstream, parts_out = take(2) if count else (None, None)
    weights, pulls, parts = take(3) if count else (None, None, None)
    out_v = take(1)[0] if wide else out
    (sem_out,) = take(1)
    half = out_v.shape[1]
    steps = half // chunk
    base = pl.multiple_of(where[0] * half, half)

    columns = lambda c: pl.ds(c * chunk, chunk)

    def put_out(c):
        there = pl.ds(pl.multiple_of(base + c * chunk, chunk), chunk)
        return pltpu.make_async_copy(out_v.at[:, columns(c)], out.at[:, there], sem_out.at[c])

    if count:
        parts[...] = jnp.zeros_like(parts)
        spread(tok, owners, first, coefs, weights, pulls)

    def form_chunk(c):
        if count and c < steps:
            form(tok, owners, first, weights, pulls, head, blocks, dstream, parts, c * chunk, chunk)

    factors = ([dstream] if count else []) + given
    form_chunk(0)
    for c in range(steps):
        form_chunk(c + 1)
        here = total[0][:, columns(c)] if added else None
        at = first * tok
        for factor in factors:
            depth = factor.shape[0]
            term = jnp.dot(picked[:, at : at + depth], factor[:, columns(c)], preferred_element_type=jnp.float32)
            here = term if here is None else here + term
            at += depth
        out_v[:, columns(c)] = here.astype(out_v.dtype)
        if wide:
            put_out(c).start()
    if count:
        if other_parts:
            parts_out[...] = sum([p[...] for p in other_parts], parts[...]).sum(axis=0)
        else:
            parts_out[...] = parts[...]
    if wide:
        for c in range(steps):
            put_out(c).wait()


def product(owners, first, picked, formed=None, given=(), total=None, parts=(), where=None):
    units, tokens = picked.shape
    coefs, head, blocks = formed or (None, None, [])
    half = blocks[0].shape[1] if blocks else given[0].shape[1]
    count = len(blocks)
    tok = tokens // owners.shape[0] * 2
    k = count * tok + sum(g.shape[0] for g in given)
    chunk = next(t for t in (512 if tokens <= 4096 else 256, 128, half) if half % t == 0)
    steps = half // chunk
    added, wide = total is not None, where is not None
    anywhere = pl.BlockSpec(memory_space=pl.ANY)
    inside = pl.BlockSpec(memory_space=pltpu.VMEM)
    in_vmem = lambda x: pltpu.with_memory_space_constraint(x, pltpu.VMEM)
    out_type = jnp.bfloat16 if added else jnp.float32
    if wide:
        out_specs = [anywhere]
        out_shape = [jax.ShapeDtypeStruct((units, 2 * half), out_type)]
    else:
        out_specs = [inside]
        out_shape = [pltpu.VMEM((units, half), out_type)]
    scratch = []
    parts_shape = (tokens // tok, 1, half)
    if count:
        out_specs += [inside, inside]
        out_shape += [
            pltpu.VMEM((count * tok, half), jnp.bfloat16),
            jax.ShapeDtypeStruct(parts_shape[1:] if parts else parts_shape, jnp.float32),
        ]
        scratch += [pltpu.VMEM((count * tok, 128), jnp.float32)] * 2 + [pltpu.VMEM(parts_shape, jnp.float32)]
    if wide:
        scratch += [pltpu.VMEM((units, half), out_type)]
    sems = [(steps,)]
    return pl.pallas_call(
        functools.partial(product_kernel, tok, count, first, len(given), int(added), len(parts), wide, chunk),
        grid_spec=pltpu.PrefetchScalarGridSpec(
            num_scalar_prefetch=2,
            grid=(),
            in_specs=[inside] * (1 + 2 * bool(count) + count + len(given) + added + len(parts)),
            out_specs=out_specs,
            scratch_shapes=scratch + [pltpu.SemaphoreType.DMA(shape) for shape in sems],
        ),
        out_shape=out_shape,
        compiler_params=params(tokens),
        cost_estimate=cost(units, k * (1 if added or given else 10), half, 6 * units * half),
    )(
        owners,
        where if wide else jnp.zeros((1,), jnp.int32),
        in_vmem(picked),
        *([coefs, head] if count else []),
        *[in_vmem(x) for x in blocks],
        *[in_vmem(x) for x in given],
        *([in_vmem(total)] if added else []),
        *parts,
    )


def put_kernel(pieces, where, part, whole, out, sems):
    units, width = part.shape
    start = pl.multiple_of(where[0] * width, width)
    rows = [pl.ds(n * (units // pieces), units // pieces) for n in range(pieces)]
    place = [
        pltpu.make_async_copy(part.at[r, :], out.at[r, pl.ds(start, width)], sems.at[n]) for n, r in enumerate(rows)
    ]
    for copy in place:
        copy.start()
    for copy in place:
        copy.wait()


def put(whole, part, where):
    units, width = part.shape
    pieces = pieces_of(units)
    anywhere = pl.BlockSpec(memory_space=pl.ANY)
    return pl.pallas_call(
        functools.partial(put_kernel, pieces),
        grid_spec=pltpu.PrefetchScalarGridSpec(
            num_scalar_prefetch=1,
            grid=(),
            in_specs=[pl.BlockSpec(memory_space=pltpu.VMEM), anywhere],
            out_specs=anywhere,
            scratch_shapes=[pltpu.SemaphoreType.DMA((pieces,))],
        ),
        out_shape=jax.ShapeDtypeStruct(whole.shape, whole.dtype),
        input_output_aliases={2: 0},
        compiler_params=params(0),
        cost_estimate=cost(0, 0, 0, 4 * units * width),
    )(where, pltpu.with_memory_space_constraint(part, pltpu.VMEM), whole)


def all_returns(step_reward, resets):
    shards, tok = step_reward.shape
    position = jnp.arange(tok)
    earlier = position[None, :] < position[:, None]
    before = jnp.sum(jnp.where(earlier[None], resets[:, None, :], 0.0), axis=2)
    total = jnp.sum(resets, axis=1, keepdims=True)
    reach = (position[None, :] >= position[:, None])[None] & (before[:, None, :] == before[:, :, None])
    local = jnp.sum(jnp.where(reach, step_reward[:, None, :], 0.0), axis=2)
    passing = before == total
    blocked = jnp.where(passing[:, 0], 0.0, 1.0)
    ids = jnp.arange(shards)
    later = ids[None, :] > ids[:, None]
    between = later[:, None, :] & (ids[None, :] < ids[:, None])[None]
    open_path = later & (jnp.sum(jnp.where(between, blocked[None, None, :], 0.0), axis=2) == 0.0)
    incoming = jnp.sum(jnp.where(open_path, local[None, :, 0], 0.0), axis=1)
    return local + jnp.where(passing, incoming[:, None], 0.0)


def make_body(width, shards):
    paths = Paths(shards)

    def body(stream, hidden, final_gain, value_head, rewards, kl_terms, resets):
        tok, local = stream.shape
        half = local // 2
        me = lax.axis_index("seq")
        mine = me % 2
        gain = final_gain.astype(jnp.float32)
        head = gain * value_head.astype(jnp.float32)
        head_half = lax.dynamic_slice_in_dim(head, mine * half, half)[None]
        to_core = lambda x: lax.ppermute(x, "seq", paths.core)
        own = lambda a: lax.dynamic_index_in_dim(a, me, 0, keepdims=False)
        last, middle, early = block_groups(paths.m)
        table = paths.owners(last + middle + early)
        both = np.concatenate([table, table[np.arange(shards) ^ 1]], axis=1)
        owners = own(jnp.asarray(both))
        early_at = len(last + middle)

        def own_facts(stream):
            stream_f = stream.astype(jnp.float32)
            share = jnp.where(lax.axis_index("tp") == 0, 1.0, 0.0)
            return jnp.stack(
                [
                    jnp.sum(stream_f * stream_f, axis=-1),
                    jnp.sum(stream_f * head, axis=-1),
                    (rewards - 0.2 * kl_terms) * share,
                    resets.astype(jnp.float32) * share,
                ]
            )

        def early_own(have):
            sum_squares, along, step_reward, cut = (have["facts"][:, k] for k in range(4))
            scale = lax.rsqrt(sum_squares / width + EPSILON)
            values = scale * along
            returns = all_returns(step_reward, cut)
            error = values - returns
            pull = scale**3 * along / width
            coefs = jnp.stack([error * scale, error * pull]).reshape(2, shards * tok)
            coefs = jnp.pad(coefs, ((0, 6), (0, 0)))
            mask = jnp.arange(shards)[:, None] == have["me"]
            row = lambda a: jnp.sum(jnp.where(mask, a, 0.0), axis=0)
            have.update(values=row(values), returns=row(returns), coefs=coefs)
            have["early own"], have["early dstream"], have["early parts"] = product(
                have["owners"], early_at, have["own picks"], (coefs, head_half, [have[b] for b in early])
            )

        def early_other(have):
            have["other sum"], have["middle dstream"], have["middle parts"] = product(
                have["owners"],
                len(last),
                have["other picks"],
                (have["coefs"], head_half, [have[b] for b in middle]),
                [have["early dstream"]],
            )

        where = mine[None].astype(jnp.int32)
        scalars = {"core": mine, "me": me, "first core": mine == 0, "where": where, "elsewhere": 1 - where}
        for n in range(shards.bit_length() - 1):
            low = (me >> n) % 2 == 0
            scalars["low %d" % n] = (jnp.arange(2) == 0) == low if n in (0, 2) else low
        scalars["owners"] = owners
        have = run_plan(stream, hidden, scalars, own_facts, paths, lambda hidden: pick(hidden, owners, tok), early_own, early_other)
        out, dstream, grad_head = product(
            have["owners"],
            0,
            have["other picks"],
            (have["coefs"], head_half, [have[b] for b in last]),
            (),
            have["other sum"],
            [have["early parts"], have["middle parts"]],
        )
        swapped = to_core(out)
        grad_head = grad_head[0]
        other_head = to_core(grad_head)
        grad_head = gain * jnp.where(
            have["first core"], jnp.concatenate([grad_head, other_head]), jnp.concatenate([other_head, grad_head])
        )
        (grad_down,) = product(
            have["owners"], 0, have["own picks"], None, [dstream, have["middle dstream"]], have["early own"], (), have["where"]
        )
        grad_down = put(grad_down, swapped, have["elsewhere"])
        return (have["values"], have["returns"], grad_head, grad_down)

    return body


def solution(mesh):
    placed = (P("seq", "tp"), P("seq", None), P("tp"), P("tp"), P("seq"), P("seq"), P("seq"))

    def run(stream, *rest):
        return jax.shard_map(
            make_body(stream.shape[1], mesh.shape["seq"]),
            mesh=mesh,
            in_specs=placed,
            out_specs=(P("seq"), P("seq"), P("tp"), P("seq", "tp")),
            check_vma=False,
        )(stream, *rest)

    return run
```

```python
import functools

import jax
import jax.numpy as jnp
import numpy as np
from jax import lax
from jax.experimental import pallas as pl
from jax.experimental.pallas import tpu as pltpu
from jax.sharding import PartitionSpec as P

EPSILON = 1e-05


def butterfly_sum(x, axis):
    count = lax.axis_size(axis)
    step = 1
    while step < count:
        x = x + lax.ppermute(x, axis, [(i, i ^ step) for i in range(count)])
        step *= 2
    return x


def butterfly_send(x, axis, bit):
    return lax.ppermute(x, axis, [(i, i ^ bit) for i in range(lax.axis_size(axis))])


def butterfly_merge(x, others, bit, low):
    if bit == 4:
        out = others[2][None]
        for mask, part in zip(low[4], (x, *others[:2])):
            out = jnp.where(mask[:, None, None, None], part[None], out)
        return out
    (other,) = others
    if bit == 1:
        return jnp.where(low[1][:, None, None], x, other)
    first, second = jnp.where(low[bit], x, other), jnp.where(low[bit], other, x)
    if bit == 2:
        return jnp.stack([first, second], axis=1).reshape(-1, *x.shape[2:])
    return jnp.concatenate([first, second])


def settle_kernel(x, out):
    out[...] = x[...]


def settle(x):
    inside = pl.BlockSpec(memory_space=pltpu.VMEM)
    return pl.pallas_call(
        settle_kernel,
        in_specs=[inside],
        out_specs=inside,
        out_shape=jax.ShapeDtypeStruct(x.shape, x.dtype),
        cost_estimate=pl.CostEstimate(flops=2 * 10**9, bytes_accessed=1, transcendentals=0),
    )(x)


class Paths:
    def __init__(self, count):
        self.count = count
        self.m = count // 4
        self.order = list(range(0, self.m, 2)) + list(range(self.m - 1 - self.m % 2, 0, -2))
        self.place = [self.order.index(z) for z in range(self.m)]
        self.across = [(i, i ^ 2) for i in range(count)]
        self.core = [(i, i ^ 1) for i in range(count)]
        self.ring = [self._ring(1), self._ring(-1)]

    def _ring(self, way):
        pairs = []
        for i in range(self.count):
            z, rest = divmod(i, 4)
            by = way if i % 2 == 0 else -way
            pairs.append((i, self.order[(self.place[z] + by) % self.m] * 4 + rest))
        return pairs

    def owners(self, blocks):
        table = np.zeros((self.count, len(blocks)), np.int32)
        for me in range(self.count):
            z, rest = divmod(me, 4)
            for b, (steps, across, kind) in enumerate(blocks):
                way = -1 if (me % 2 == 0) == (kind == 0) else 1
                table[me, b] = self.order[(self.place[z] + way * steps) % self.m] * 4 + (rest ^ (2 * across + kind))
        return table


class Flights:
    def __init__(self, **arrays):
        self.have = arrays

    def event(self, waits, sends=()):
        names = list(dict.fromkeys([*waits, *(source for _, source, _ in sends)]))
        self.have.update(zip(names, lax.optimization_barrier(tuple(self.have[n] for n in names))))
        for name, source, pairs in sends:
            self.have[name] = lax.ppermute(self.have[source], "seq", pairs)


def block_groups(m):
    last = [(m - 1, 1, 0), (m - 1, 1, 1)]
    middle = [(m - 2, 1, 0), (m - 2, 1, 1), (m - 1, 0, 0), (m - 1, 0, 1)]
    early = [(k, a, kind) for k in range(m - 1) for a in range(2) for kind in range(2) if k < m - 2 or a == 0]
    return last, middle, early


def run_plan(stream, hidden, scalars, own_facts, paths, pick_both, early_own, early_other):
    half = stream.shape[1] // 2
    m, ring, across, core = paths.m, paths.ring, paths.across, paths.core
    cut = lambda c: lax.dynamic_slice_in_dim(stream, c * half, half, 1)
    core_index = scalars["core"]
    f = Flights(stream=stream, hidden=hidden, away=cut(1 - core_index), **scalars)
    f.have[0, 0, 0] = cut(core_index)
    have = f.have
    names = list(scalars)
    bits = [1, 4, 2] + [16 << n for n in range(paths.count.bit_length() - 5)]

    def facts_send():
        steps = (4, 8, 12) if bits[0] == 4 else (bits[0],)
        for n, step in enumerate(steps):
            have["facts %d" % n] = butterfly_send(have["facts"], "seq", step)
        return ["facts %d" % n for n in range(len(steps))]

    def facts_merge(arrived):
        bit = bits.pop(0)
        low = {bit: [have["ring %d" % n] for n in range(3)] if bit == 4 else have["low %d" % bit]}
        have["facts"] = butterfly_merge(have["facts"], [have[name] for name in arrived], bit, low)

    def facts_step():
        if bits:
            facts_merge(facts_send())

    f.event([], [((1, 0, 0), (0, 0, 0), ring[0]), ((0, 1, 0), (0, 0, 0), across), ((0, 0, 1), "away", core)])
    f.event(
        [(0, 0, 1), "stream", *names],
        [((1, 0, 1), (0, 0, 1), ring[1]), ((0, 1, 1), (0, 0, 1), across)],
    )
    have["facts"] = butterfly_sum(own_facts(have["stream"]), "tp")[None]
    f.event(["facts", "hidden"])
    have["own picks"], have["away picks"] = pick_both(have["hidden"])
    f.event(
        [(1, 0, 0), (0, 1, 0), "facts", "own picks", "away picks"],
        [((2, 0, 0), (1, 0, 0), ring[0]), ((1, 1, 0), (1, 0, 0), across)],
    )
    facts_step()
    arriving = facts_send()
    f.event([(1, 0, 1), (0, 1, 1), "facts", *arriving], [((2, 0, 1), (1, 0, 1), ring[1]), ((1, 1, 1), (1, 0, 1), across)])
    facts_merge(arriving)
    for k in range(2, m):
        for kind in range(2):
            if bits:
                facts_step()
            elif k < m - 1:
                have["facts"] = settle(have["facts"])
            if k < m - 1:
                sends = [((k + 1, 0, kind), (k, 0, kind), ring[kind]), ((k, 1, kind), (k, 0, kind), across)]
            elif kind == 0:
                sends = []
            else:
                sends = [((k, 1, 0), (k - 1, 1, 0), ring[0]), ((k, 1, 1), (k, 0, 1), across)]
            waits = [(k, 0, kind), (k - 1, 1, kind), "facts"]
            if k == m - 2 and kind == 1:
                sends.append(("other picks", "away picks", core))
            if k == m - 1 and kind == 1:
                waits += ["other picks", "early own", "values", "returns"]
            f.event(waits, sends)
            if k == m - 2 and kind == 1:
                while bits:
                    facts_step()
                early_own(have)
    early_other(have)
    f.event([(m - 1, 1, 0), (m - 1, 1, 1), "other sum"])
    return have


def params(tokens):
    return pltpu.CompilerParams(vmem_limit_bytes=(9 if tokens <= 4096 else 40) * 1024 * 1024)


def cost(units, k, width, extra):
    return pl.CostEstimate(
        flops=2 * units * k * width, bytes_accessed=2 * (units * k + k * width) + extra, transcendentals=0
    )


def pieces_of(units):
    return next(n for n in (7, 4, 2, 1) if units % (16 * n) == 0)


def pick_kernel(tok, owners, hidden, own, away, held, turned, sems_in, sems_out):
    units, tokens = hidden.shape
    count = tokens // tok
    pieces = pieces_of(units)
    size = units // pieces
    rows = [pl.ds(n * size, size) for n in range(pieces)]
    fetch = [pltpu.make_async_copy(hidden.at[r, :], held.at[r, :], sems_in.at[n]) for n, r in enumerate(rows)]
    place = [pltpu.make_async_copy(turned.at[r, :], away.at[r, :], sems_out.at[n]) for n, r in enumerate(rows)]
    for copy in fetch:
        copy.start()
    for n, r in enumerate(rows):
        fetch[n].wait()
        for m, out in enumerate((own, turned)):
            for b in range(count):
                columns = pl.ds(pl.multiple_of(owners[m * count + b] * tok, tok), tok)
                out[r, b * tok : (b + 1) * tok] = held[r, columns]
        place[n].start()
    for copy in place:
        copy.wait()


def pick(hidden, owners, tok):
    inside = pl.BlockSpec(memory_space=pltpu.VMEM)
    anywhere = pl.BlockSpec(memory_space=pl.ANY)
    pieces = pieces_of(hidden.shape[0])
    return pl.pallas_call(
        functools.partial(pick_kernel, tok),
        grid_spec=pltpu.PrefetchScalarGridSpec(
            num_scalar_prefetch=1,
            grid=(),
            in_specs=[anywhere],
            out_specs=[inside, anywhere],
            scratch_shapes=[pltpu.VMEM(hidden.shape, hidden.dtype)] * 2 + [pltpu.SemaphoreType.DMA((pieces,))] * 2,
        ),
        out_shape=[pltpu.VMEM(hidden.shape, hidden.dtype), pltpu.HBM(hidden.shape, hidden.dtype)],
        compiler_params=params(hidden.shape[1]),
        cost_estimate=cost(0, 0, 0, 1),
    )(owners, pltpu.with_memory_space_constraint(hidden, pltpu.HBM))


def spread(tok, owners, first, coefs, weights, pulls):
    for b in range(weights.shape[0] // tok):
        coef = coefs[:, pl.ds(pl.multiple_of(owners[first + b] * tok, tok), tok)].T
        rows = slice(b * tok, (b + 1) * tok)
        weights[rows, :] = jnp.broadcast_to(coef[:, 0:1], (tok, 128))
        pulls[rows, :] = jnp.broadcast_to(coef[:, 1:2], (tok, 128))


def form(tok, owners, first, weights, pulls, head, blocks, dstream, parts, start, chunk):
    for b in range(len(blocks)):
        rows = slice(b * tok, (b + 1) * tok)
        for at in range(0, chunk, 128):
            lanes = slice(start + at, start + at + 128)
            stream_f = blocks[b][:, lanes].astype(jnp.float32)
            weight = weights[rows, :]
            dstream[rows, lanes] = (weight * head[:, lanes] - pulls[rows, :] * stream_f).astype(jnp.bfloat16)
            parts[owners[first + b], :, lanes] = jnp.sum(weight * stream_f, axis=0, keepdims=True)


def product_kernel(tok, count, first, given_count, added, parts_count, wide, chunk, owners, where, *refs):
    refs = list(refs)
    take = lambda n: [refs.pop(0) for _ in range(n)]
    (picked,) = take(1)
    coefs, head = take(2) if count else (None, None)
    blocks, given, total, other_parts = take(count), take(given_count), take(added), take(parts_count)
    (out,) = take(1)
    dstream, parts_out = take(2) if count else (None, None)
    weights, pulls, parts = take(3) if count else (None, None, None)
    out_v = take(1)[0] if wide else out
    (sem_out,) = take(1)
    half = out_v.shape[1]
    steps = half // chunk
    base = pl.multiple_of(where[0] * half, half)

    columns = lambda c: pl.ds(c * chunk, chunk)

    def put_out(c):
        there = pl.ds(pl.multiple_of(base + c * chunk, chunk), chunk)
        return pltpu.make_async_copy(out_v.at[:, columns(c)], out.at[:, there], sem_out.at[c])

    if count:
        parts[...] = jnp.zeros_like(parts)
        spread(tok, owners, first, coefs, weights, pulls)

    def form_chunk(c):
        if count and c < steps:
            form(tok, owners, first, weights, pulls, head, blocks, dstream, parts, c * chunk, chunk)

    factors = ([dstream] if count else []) + given
    form_chunk(0)
    for c in range(steps):
        form_chunk(c + 1)
        here = total[0][:, columns(c)] if added else None
        at = first * tok
        for factor in factors:
            depth = factor.shape[0]
            term = jnp.dot(picked[:, at : at + depth], factor[:, columns(c)], preferred_element_type=jnp.float32)
            here = term if here is None else here + term
            at += depth
        out_v[:, columns(c)] = here.astype(out_v.dtype)
        if wide:
            put_out(c).start()
    if count:
        if other_parts:
            parts_out[...] = sum([p[...] for p in other_parts], parts[...]).sum(axis=0)
        else:
            parts_out[...] = parts[...]
    if wide:
        for c in range(steps):
            put_out(c).wait()


def product(owners, first, picked, formed=None, given=(), total=None, parts=(), where=None):
    units, tokens = picked.shape
    coefs, head, blocks = formed or (None, None, [])
    half = blocks[0].shape[1] if blocks else given[0].shape[1]
    count = len(blocks)
    tok = tokens // owners.shape[0] * 2
    k = count * tok + sum(g.shape[0] for g in given)
    chunk = next(t for t in (512 if tokens <= 4096 else 256, 128, half) if half % t == 0)
    steps = half // chunk
    added, wide = total is not None, where is not None
    anywhere = pl.BlockSpec(memory_space=pl.ANY)
    inside = pl.BlockSpec(memory_space=pltpu.VMEM)
    in_vmem = lambda x: pltpu.with_memory_space_constraint(x, pltpu.VMEM)
    out_type = jnp.bfloat16 if added else jnp.float32
    if wide:
        out_specs = [anywhere]
        out_shape = [jax.ShapeDtypeStruct((units, 2 * half), out_type)]
    else:
        out_specs = [inside]
        out_shape = [pltpu.VMEM((units, half), out_type)]
    scratch = []
    parts_shape = (tokens // tok, 1, half)
    if count:
        out_specs += [inside, inside]
        out_shape += [
            pltpu.VMEM((count * tok, half), jnp.bfloat16),
            jax.ShapeDtypeStruct(parts_shape[1:] if parts else parts_shape, jnp.float32),
        ]
        scratch += [pltpu.VMEM((count * tok, 128), jnp.float32)] * 2 + [pltpu.VMEM(parts_shape, jnp.float32)]
    if wide:
        scratch += [pltpu.VMEM((units, half), out_type)]
    sems = [(steps,)]
    return pl.pallas_call(
        functools.partial(product_kernel, tok, count, first, len(given), int(added), len(parts), wide, chunk),
        grid_spec=pltpu.PrefetchScalarGridSpec(
            num_scalar_prefetch=2,
            grid=(),
            in_specs=[inside] * (1 + 2 * bool(count) + count + len(given) + added + len(parts)),
            out_specs=out_specs,
            scratch_shapes=scratch + [pltpu.SemaphoreType.DMA(shape) for shape in sems],
        ),
        out_shape=out_shape,
        compiler_params=params(tokens),
        cost_estimate=cost(units, k * (1 if added or given else 10), half, 6 * units * half),
    )(
        owners,
        where if wide else jnp.zeros((1,), jnp.int32),
        in_vmem(picked),
        *([coefs, head] if count else []),
        *[in_vmem(x) for x in blocks],
        *[in_vmem(x) for x in given],
        *([in_vmem(total)] if added else []),
        *parts,
    )


def put_kernel(pieces, where, part, whole, out, sems):
    units, width = part.shape
    start = pl.multiple_of(where[0] * width, width)
    rows = [pl.ds(n * (units // pieces), units // pieces) for n in range(pieces)]
    place = [
        pltpu.make_async_copy(part.at[r, :], out.at[r, pl.ds(start, width)], sems.at[n]) for n, r in enumerate(rows)
    ]
    for copy in place:
        copy.start()
    for copy in place:
        copy.wait()


def put(whole, part, where):
    units, width = part.shape
    pieces = pieces_of(units)
    anywhere = pl.BlockSpec(memory_space=pl.ANY)
    return pl.pallas_call(
        functools.partial(put_kernel, pieces),
        grid_spec=pltpu.PrefetchScalarGridSpec(
            num_scalar_prefetch=1,
            grid=(),
            in_specs=[pl.BlockSpec(memory_space=pltpu.VMEM), anywhere],
            out_specs=anywhere,
            scratch_shapes=[pltpu.SemaphoreType.DMA((pieces,))],
        ),
        out_shape=jax.ShapeDtypeStruct(whole.shape, whole.dtype),
        input_output_aliases={2: 0},
        compiler_params=params(0),
        cost_estimate=cost(0, 0, 0, 4 * units * width),
    )(where, pltpu.with_memory_space_constraint(part, pltpu.VMEM), whole)


def all_returns(step_reward, resets):
    shards, tok = step_reward.shape
    position = jnp.arange(tok)
    earlier = position[None, :] < position[:, None]
    before = jnp.sum(jnp.where(earlier[None], resets[:, None, :], 0.0), axis=2)
    total = jnp.sum(resets, axis=1, keepdims=True)
    reach = (position[None, :] >= position[:, None])[None] & (before[:, None, :] == before[:, :, None])
    local = jnp.sum(jnp.where(reach, step_reward[:, None, :], 0.0), axis=2)
    passing = before == total
    blocked = jnp.where(passing[:, 0], 0.0, 1.0)
    ids = jnp.arange(shards)
    later = ids[None, :] > ids[:, None]
    between = later[:, None, :] & (ids[None, :] < ids[:, None])[None]
    open_path = later & (jnp.sum(jnp.where(between, blocked[None, None, :], 0.0), axis=2) == 0.0)
    incoming = jnp.sum(jnp.where(open_path, local[None, :, 0], 0.0), axis=1)
    return local + jnp.where(passing, incoming[:, None], 0.0)


def make_body(width, shards):
    paths = Paths(shards)

    def body(stream, hidden, final_gain, value_head, rewards, kl_terms, resets):
        tok, local = stream.shape
        half = local // 2
        me = lax.axis_index("seq")
        mine = me % 2
        gain = final_gain.astype(jnp.float32)
        head = gain * value_head.astype(jnp.float32)
        head_half = lax.dynamic_slice_in_dim(head, mine * half, half)[None]
        to_core = lambda x: lax.ppermute(x, "seq", paths.core)
        own = lambda a: lax.dynamic_index_in_dim(a, me, 0, keepdims=False)
        last, middle, early = block_groups(paths.m)
        table = paths.owners(last + middle + early)
        both = np.concatenate([table, table[np.arange(shards) ^ 1]], axis=1)
        owners = own(jnp.asarray(both))
        early_at = len(last + middle)

        def own_facts(stream):
            stream_f = stream.astype(jnp.float32)
            share = jnp.where(lax.axis_index("tp") == 0, 1.0, 0.0)
            return jnp.stack(
                [
                    jnp.sum(stream_f * stream_f, axis=-1),
                    jnp.sum(stream_f * head, axis=-1),
                    (rewards - 0.2 * kl_terms) * share,
                    resets.astype(jnp.float32) * share,
                ]
            )

        def early_own(have):
            sum_squares, along, step_reward, cut = (have["facts"][:, k] for k in range(4))
            scale = lax.rsqrt(sum_squares / width + EPSILON)
            values = scale * along
            returns = all_returns(step_reward, cut)
            error = values - returns
            pull = scale**3 * along / width
            coefs = jnp.stack([error * scale, error * pull]).reshape(2, shards * tok)
            coefs = jnp.pad(coefs, ((0, 6), (0, 0)))
            mask = jnp.arange(shards)[:, None] == have["me"]
            row = lambda a: jnp.sum(jnp.where(mask, a, 0.0), axis=0)
            have.update(values=row(values), returns=row(returns), coefs=coefs)
            have["early own"], have["early dstream"], have["early parts"] = product(
                have["owners"], early_at, have["own picks"], (coefs, head_half, [have[b] for b in early])
            )

        def early_other(have):
            have["other sum"], have["middle dstream"], have["middle parts"] = product(
                have["owners"],
                len(last),
                have["other picks"],
                (have["coefs"], head_half, [have[b] for b in middle]),
                [have["early dstream"]],
            )

        where = mine[None].astype(jnp.int32)
        scalars = {"core": mine, "me": me, "first core": mine == 0, "where": where, "elsewhere": 1 - where}
        for n in range(shards.bit_length() - 1):
            low = (me >> n) % 2 == 0
            scalars["low %d" % (1 << n)] = (jnp.arange(2) == 0) == low if n == 0 else low
        for n in range(3):
            scalars["ring %d" % n] = (jnp.arange(4) ^ (me >> 2) % 4) == n
        scalars["owners"] = owners
        have = run_plan(stream, hidden, scalars, own_facts, paths, lambda hidden: pick(hidden, owners, tok), early_own, early_other)
        out, dstream, grad_head = product(
            have["owners"],
            0,
            have["other picks"],
            (have["coefs"], head_half, [have[b] for b in last]),
            (),
            have["other sum"],
            [have["early parts"], have["middle parts"]],
        )
        swapped = to_core(out)
        grad_head = grad_head[0]
        other_head = to_core(grad_head)
        grad_head = gain * jnp.where(
            have["first core"], jnp.concatenate([grad_head, other_head]), jnp.concatenate([other_head, grad_head])
        )
        (grad_down,) = product(
            have["owners"], 0, have["own picks"], None, [dstream, have["middle dstream"]], have["early own"], (), have["where"]
        )
        grad_down = put(grad_down, swapped, have["elsewhere"])
        return (have["values"], have["returns"], grad_head, grad_down)

    return body


def solution(mesh):
    placed = (P("seq", "tp"), P("seq", None), P("tp"), P("tp"), P("seq"), P("seq"), P("seq"))

    def run(stream, *rest):
        return jax.shard_map(
            make_body(stream.shape[1], mesh.shape["seq"]),
            mesh=mesh,
            in_specs=placed,
            out_specs=(P("seq"), P("seq"), P("tp"), P("seq", "tp")),
            check_vma=False,
        )(stream, *rest)

    return run
```

```python
import functools

import jax
import jax.numpy as jnp
import numpy as np
from jax import lax
from jax.experimental import pallas as pl
from jax.experimental.pallas import tpu as pltpu
from jax.sharding import PartitionSpec as P

EPSILON = 1e-05


def butterfly_sum(x, axis):
    count = lax.axis_size(axis)
    step = 1
    while step < count:
        x = x + lax.ppermute(x, axis, [(i, i ^ step) for i in range(count)])
        step *= 2
    return x


def butterfly_send(x, axis, bit):
    return lax.ppermute(x, axis, [(i, i ^ bit) for i in range(lax.axis_size(axis))])


def butterfly_merge(x, other, bit, low):
    low = low[bit]
    if bit == 1:
        return jnp.where(low[:, None, None], x, other)
    if bit == 4:
        return jnp.where(low[:, None, None, None], x[None], other[None])
    if bit == 2:
        both = jnp.stack([jnp.where(low, x, other), jnp.where(low, other, x)], axis=1)
        return both.reshape(-1, *x.shape[2:])
    return jnp.concatenate([jnp.where(low, x, other), jnp.where(low, other, x)])


class Paths:
    def __init__(self, count):
        self.count = count
        self.m = count // 4
        self.order = list(range(0, self.m, 2)) + list(range(self.m - 1 - self.m % 2, 0, -2))
        self.place = [self.order.index(z) for z in range(self.m)]
        self.across = [(i, i ^ 2) for i in range(count)]
        self.core = [(i, i ^ 1) for i in range(count)]
        self.ring = [self._ring(1), self._ring(-1)]

    def _ring(self, way):
        pairs = []
        for i in range(self.count):
            z, rest = divmod(i, 4)
            by = way if i % 2 == 0 else -way
            pairs.append((i, self.order[(self.place[z] + by) % self.m] * 4 + rest))
        return pairs

    def owners(self, blocks):
        table = np.zeros((self.count, len(blocks)), np.int32)
        for me in range(self.count):
            z, rest = divmod(me, 4)
            for b, (steps, across, kind) in enumerate(blocks):
                way = -1 if (me % 2 == 0) == (kind == 0) else 1
                table[me, b] = self.order[(self.place[z] + way * steps) % self.m] * 4 + (rest ^ (2 * across + kind))
        return table


class Flights:
    def __init__(self, **arrays):
        self.have = arrays

    def event(self, waits, sends=()):
        names = list(dict.fromkeys([*waits, *(source for _, source, _ in sends)]))
        self.have.update(zip(names, lax.optimization_barrier(tuple(self.have[n] for n in names))))
        for name, source, pairs in sends:
            self.have[name] = lax.ppermute(self.have[source], "seq", pairs)


def block_groups(m):
    last = [(m - 1, 1, 0), (m - 1, 1, 1)]
    middle = [(m - 2, 1, 0), (m - 2, 1, 1), (m - 1, 0, 0), (m - 1, 0, 1)]
    early = [(k, a, kind) for k in range(m - 1) for a in range(2) for kind in range(2) if k < m - 2 or a == 0]
    return last, middle, early


def run_plan(stream, hidden, scalars, own_facts, paths, pick_both, early_own, early_other):
    half = stream.shape[1] // 2
    m, ring, across, core = paths.m, paths.ring, paths.across, paths.core
    cut = lambda c: lax.dynamic_slice_in_dim(stream, c * half, half, 1)
    core_index = scalars["core"]
    f = Flights(stream=stream, hidden=hidden, away=cut(1 - core_index), **scalars)
    f.have[0, 0, 0] = cut(core_index)
    have = f.have
    names = list(scalars)
    low = lambda: {1 << n: have["low %d" % n] for n in range(paths.count.bit_length() - 1)}

    bits = [1, 4, 2] + [8 << n for n in range(paths.count.bit_length() - 4)]

    def facts_send():
        have["other facts"] = butterfly_send(have["facts"], "seq", bits[0])

    def facts_merge():
        have["facts"] = butterfly_merge(have["facts"], have["other facts"], bits.pop(0), low())

    def facts_step():
        if bits:
            facts_send()
            facts_merge()

    f.event([], [((1, 0, 0), (0, 0, 0), ring[0]), ((0, 1, 0), (0, 0, 0), across), ((0, 0, 1), "away", core)])
    f.event(
        [(0, 0, 1), "stream", *names],
        [((1, 0, 1), (0, 0, 1), ring[1]), ((0, 1, 1), (0, 0, 1), across)],
    )
    have["facts"] = butterfly_sum(own_facts(have["stream"]), "tp")[None]
    f.event(["facts", "hidden"])
    have["own picks"], have["away picks"] = pick_both(have["hidden"])
    f.event(
        [(1, 0, 0), (0, 1, 0), "facts", "own picks", "away picks"],
        [((2, 0, 0), (1, 0, 0), ring[0]), ((1, 1, 0), (1, 0, 0), across)],
    )
    facts_step()
    facts_send()
    f.event([(1, 0, 1), (0, 1, 1), "facts", "other facts"], [((2, 0, 1), (1, 0, 1), ring[1]), ((1, 1, 1), (1, 0, 1), across)])
    facts_merge()
    for k in range(2, m):
        for kind in range(2):
            facts_step()
            if k < m - 1:
                sends = [((k + 1, 0, kind), (k, 0, kind), ring[kind]), ((k, 1, kind), (k, 0, kind), across)]
            elif kind == 0:
                sends = [((k, 1, 0), (k, 0, 0), across)]
            else:
                sends = [((k, 1, 1), (k - 1, 1, 1), ring[1])]
            waits = [(k, 0, kind), (k - 1, 1, kind), "facts"]
            if k == m - 2 and kind == 1:
                sends.append(("other picks", "away picks", core))
            if k == m - 1 and kind == 1:
                waits = [(k - 1, 1, kind), "early own"]
            f.event(waits, sends)
            if k == m - 1 and kind == 1:
                f.event([(k, 0, kind), "other picks", "values", "returns"])
            if k == m - 2 and kind == 1:
                while bits:
                    facts_step()
                early_own(have)
    early_other(have)
    f.event([(m - 1, 1, 0), (m - 1, 1, 1), "other sum"])
    return have


def params(tokens):
    return pltpu.CompilerParams(vmem_limit_bytes=(9 if tokens <= 4096 else 40) * 1024 * 1024)


def cost(units, k, width, extra):
    return pl.CostEstimate(
        flops=2 * units * k * width, bytes_accessed=2 * (units * k + k * width) + extra, transcendentals=0
    )


def pieces_of(units):
    return next(n for n in (7, 4, 2, 1) if units % (16 * n) == 0)


def pick_kernel(tok, owners, hidden, own, away, held, turned, sems_in, sems_out):
    units, tokens = hidden.shape
    count = tokens // tok
    pieces = pieces_of(units)
    size = units // pieces
    rows = [pl.ds(n * size, size) for n in range(pieces)]
    fetch = [pltpu.make_async_copy(hidden.at[r, :], held.at[r, :], sems_in.at[n]) for n, r in enumerate(rows)]
    place = [pltpu.make_async_copy(turned.at[r, :], away.at[r, :], sems_out.at[n]) for n, r in enumerate(rows)]
    for copy in fetch:
        copy.start()
    for n, r in enumerate(rows):
        fetch[n].wait()
        for m, out in enumerate((own, turned)):
            for b in range(count):
                columns = pl.ds(pl.multiple_of(owners[m * count + b] * tok, tok), tok)
                out[r, b * tok : (b + 1) * tok] = held[r, columns]
        place[n].start()
    for copy in place:
        copy.wait()


def pick(hidden, owners, tok):
    inside = pl.BlockSpec(memory_space=pltpu.VMEM)
    anywhere = pl.BlockSpec(memory_space=pl.ANY)
    pieces = pieces_of(hidden.shape[0])
    return pl.pallas_call(
        functools.partial(pick_kernel, tok),
        grid_spec=pltpu.PrefetchScalarGridSpec(
            num_scalar_prefetch=1,
            grid=(),
            in_specs=[anywhere],
            out_specs=[inside, anywhere],
            scratch_shapes=[pltpu.VMEM(hidden.shape, hidden.dtype)] * 2 + [pltpu.SemaphoreType.DMA((pieces,))] * 2,
        ),
        out_shape=[pltpu.VMEM(hidden.shape, hidden.dtype), pltpu.HBM(hidden.shape, hidden.dtype)],
        compiler_params=params(hidden.shape[1]),
        cost_estimate=cost(0, 0, 0, 1),
    )(owners, pltpu.with_memory_space_constraint(hidden, pltpu.HBM))


def spread(tok, owners, first, coefs, weights, pulls):
    for b in range(weights.shape[0] // tok):
        coef = coefs[:, pl.ds(pl.multiple_of(owners[first + b] * tok, tok), tok)].T
        rows = slice(b * tok, (b + 1) * tok)
        weights[rows, :] = jnp.broadcast_to(coef[:, 0:1], (tok, 128))
        pulls[rows, :] = jnp.broadcast_to(coef[:, 1:2], (tok, 128))


def form(tok, owners, first, weights, pulls, head, blocks, dstream, parts, start, chunk):
    for b in range(len(blocks)):
        rows = slice(b * tok, (b + 1) * tok)
        for at in range(0, chunk, 128):
            lanes = slice(start + at, start + at + 128)
            stream_f = blocks[b][:, lanes].astype(jnp.float32)
            weight = weights[rows, :]
            dstream[rows, lanes] = (weight * head[:, lanes] - pulls[rows, :] * stream_f).astype(jnp.bfloat16)
            parts[owners[first + b], :, lanes] = jnp.sum(weight * stream_f, axis=0, keepdims=True)


def product_kernel(tok, count, first, given_count, added, parts_count, wide, chunk, owners, where, *refs):
    refs = list(refs)
    take = lambda n: [refs.pop(0) for _ in range(n)]
    (picked,) = take(1)
    coefs, head = take(2) if count else (None, None)
    blocks, given, total, other_parts = take(count), take(given_count), take(added), take(parts_count)
    (out,) = take(1)
    dstream, parts_out = take(2) if count else (None, None)
    weights, pulls, parts = take(3) if count else (None, None, None)
    out_v = take(1)[0] if wide else out
    (sem_out,) = take(1)
    half = out_v.shape[1]
    steps = half // chunk
    base = pl.multiple_of(where[0] * half, half)

    columns = lambda c: pl.ds(c * chunk, chunk)

    def put_out(c):
        there = pl.ds(pl.multiple_of(base + c * chunk, chunk), chunk)
        return pltpu.make_async_copy(out_v.at[:, columns(c)], out.at[:, there], sem_out.at[c])

    if count:
        parts[...] = jnp.zeros_like(parts)
        spread(tok, owners, first, coefs, weights, pulls)

    def form_chunk(c):
        if count and c < steps:
            form(tok, owners, first, weights, pulls, head, blocks, dstream, parts, c * chunk, chunk)

    factors = ([dstream] if count else []) + given
    form_chunk(0)
    for c in range(steps):
        form_chunk(c + 1)
        here = total[0][:, columns(c)] if added else None
        at = first * tok
        for factor in factors:
            depth = factor.shape[0]
            term = jnp.dot(picked[:, at : at + depth], factor[:, columns(c)], preferred_element_type=jnp.float32)
            here = term if here is None else here + term
            at += depth
        out_v[:, columns(c)] = here.astype(out_v.dtype)
        if wide:
            put_out(c).start()
    if count:
        if other_parts:
            parts_out[...] = sum([p[...] for p in other_parts], parts[...]).sum(axis=0)
        else:
            parts_out[...] = parts[...]
    if wide:
        for c in range(steps):
            put_out(c).wait()


def product(owners, first, picked, formed=None, given=(), total=None, parts=(), where=None):
    units, tokens = picked.shape
    coefs, head, blocks = formed or (None, None, [])
    half = blocks[0].shape[1] if blocks else given[0].shape[1]
    count = len(blocks)
    tok = tokens // owners.shape[0] * 2
    k = count * tok + sum(g.shape[0] for g in given)
    chunk = next(t for t in (512 if tokens <= 4096 else 256, 128, half) if half % t == 0)
    steps = half // chunk
    added, wide = total is not None, where is not None
    anywhere = pl.BlockSpec(memory_space=pl.ANY)
    inside = pl.BlockSpec(memory_space=pltpu.VMEM)
    in_vmem = lambda x: pltpu.with_memory_space_constraint(x, pltpu.VMEM)
    out_type = jnp.bfloat16 if added else jnp.float32
    if wide:
        out_specs = [anywhere]
        out_shape = [jax.ShapeDtypeStruct((units, 2 * half), out_type)]
    else:
        out_specs = [inside]
        out_shape = [pltpu.VMEM((units, half), out_type)]
    scratch = []
    parts_shape = (tokens // tok, 1, half)
    if count:
        out_specs += [inside, inside]
        out_shape += [
            pltpu.VMEM((count * tok, half), jnp.bfloat16),
            jax.ShapeDtypeStruct(parts_shape[1:] if parts else parts_shape, jnp.float32),
        ]
        scratch += [pltpu.VMEM((count * tok, 128), jnp.float32)] * 2 + [pltpu.VMEM(parts_shape, jnp.float32)]
    if wide:
        scratch += [pltpu.VMEM((units, half), out_type)]
    sems = [(steps,)]
    return pl.pallas_call(
        functools.partial(product_kernel, tok, count, first, len(given), int(added), len(parts), wide, chunk),
        grid_spec=pltpu.PrefetchScalarGridSpec(
            num_scalar_prefetch=2,
            grid=(),
            in_specs=[inside] * (1 + 2 * bool(count) + count + len(given) + added + len(parts)),
            out_specs=out_specs,
            scratch_shapes=scratch + [pltpu.SemaphoreType.DMA(shape) for shape in sems],
        ),
        out_shape=out_shape,
        compiler_params=params(tokens),
        cost_estimate=cost(units, k * (1 if added or given else 10), half, 6 * units * half),
    )(
        owners,
        where if wide else jnp.zeros((1,), jnp.int32),
        in_vmem(picked),
        *([coefs, head] if count else []),
        *[in_vmem(x) for x in blocks],
        *[in_vmem(x) for x in given],
        *([in_vmem(total)] if added else []),
        *parts,
    )


def put_kernel(pieces, where, part, whole, out, sems):
    units, width = part.shape
    start = pl.multiple_of(where[0] * width, width)
    rows = [pl.ds(n * (units // pieces), units // pieces) for n in range(pieces)]
    place = [
        pltpu.make_async_copy(part.at[r, :], out.at[r, pl.ds(start, width)], sems.at[n]) for n, r in enumerate(rows)
    ]
    for copy in place:
        copy.start()
    for copy in place:
        copy.wait()


def put(whole, part, where):
    units, width = part.shape
    pieces = pieces_of(units)
    anywhere = pl.BlockSpec(memory_space=pl.ANY)
    return pl.pallas_call(
        functools.partial(put_kernel, pieces),
        grid_spec=pltpu.PrefetchScalarGridSpec(
            num_scalar_prefetch=1,
            grid=(),
            in_specs=[pl.BlockSpec(memory_space=pltpu.VMEM), anywhere],
            out_specs=anywhere,
            scratch_shapes=[pltpu.SemaphoreType.DMA((pieces,))],
        ),
        out_shape=jax.ShapeDtypeStruct(whole.shape, whole.dtype),
        input_output_aliases={2: 0},
        compiler_params=params(0),
        cost_estimate=cost(0, 0, 0, 4 * units * width),
    )(where, pltpu.with_memory_space_constraint(part, pltpu.VMEM), whole)


def all_returns(step_reward, resets):
    shards, tok = step_reward.shape
    position = jnp.arange(tok)
    earlier = position[None, :] < position[:, None]
    before = jnp.sum(jnp.where(earlier[None], resets[:, None, :], 0.0), axis=2)
    total = jnp.sum(resets, axis=1, keepdims=True)
    reach = (position[None, :] >= position[:, None])[None] & (before[:, None, :] == before[:, :, None])
    local = jnp.sum(jnp.where(reach, step_reward[:, None, :], 0.0), axis=2)
    passing = before == total
    blocked = jnp.where(passing[:, 0], 0.0, 1.0)
    ids = jnp.arange(shards)
    later = ids[None, :] > ids[:, None]
    between = later[:, None, :] & (ids[None, :] < ids[:, None])[None]
    open_path = later & (jnp.sum(jnp.where(between, blocked[None, None, :], 0.0), axis=2) == 0.0)
    incoming = jnp.sum(jnp.where(open_path, local[None, :, 0], 0.0), axis=1)
    return local + jnp.where(passing, incoming[:, None], 0.0)


def make_body(width, shards):
    paths = Paths(shards)

    def body(stream, hidden, final_gain, value_head, rewards, kl_terms, resets):
        tok, local = stream.shape
        half = local // 2
        me = lax.axis_index("seq")
        mine = me % 2
        gain = final_gain.astype(jnp.float32)
        head = gain * value_head.astype(jnp.float32)
        head_half = lax.dynamic_slice_in_dim(head, mine * half, half)[None]
        to_core = lambda x: lax.ppermute(x, "seq", paths.core)
        own = lambda a: lax.dynamic_index_in_dim(a, me, 0, keepdims=False)
        last, middle, early = block_groups(paths.m)
        table = paths.owners(last + middle + early)
        both = np.concatenate([table, table[np.arange(shards) ^ 1]], axis=1)
        owners = own(jnp.asarray(both))
        early_at = len(last + middle)

        def own_facts(stream):
            stream_f = stream.astype(jnp.float32)
            share = jnp.where(lax.axis_index("tp") == 0, 1.0, 0.0)
            return jnp.stack(
                [
                    jnp.sum(stream_f * stream_f, axis=-1),
                    jnp.sum(stream_f * head, axis=-1),
                    (rewards - 0.2 * kl_terms) * share,
                    resets.astype(jnp.float32) * share,
                ]
            )

        def early_own(have):
            sum_squares, along, step_reward, cut = (have["facts"][:, k] for k in range(4))
            scale = lax.rsqrt(sum_squares / width + EPSILON)
            values = scale * along
            returns = all_returns(step_reward, cut)
            error = values - returns
            pull = scale**3 * along / width
            coefs = jnp.stack([error * scale, error * pull]).reshape(2, shards * tok)
            coefs = jnp.pad(coefs, ((0, 6), (0, 0)))
            mask = jnp.arange(shards)[:, None] == have["me"]
            row = lambda a: jnp.sum(jnp.where(mask, a, 0.0), axis=0)
            have.update(values=row(values), returns=row(returns), coefs=coefs)
            have["early own"], have["early dstream"], have["early parts"] = product(
                have["owners"], early_at, have["own picks"], (coefs, head_half, [have[b] for b in early])
            )

        def early_other(have):
            have["other sum"], have["middle dstream"], have["middle parts"] = product(
                have["owners"],
                len(last),
                have["other picks"],
                (have["coefs"], head_half, [have[b] for b in middle]),
                [have["early dstream"]],
            )

        where = mine[None].astype(jnp.int32)
        scalars = {"core": mine, "me": me, "first core": mine == 0, "where": where, "elsewhere": 1 - where}
        for n in range(shards.bit_length() - 1):
            low = (me >> n) % 2 == 0
            scalars["low %d" % n] = (jnp.arange(2) == 0) == low if n in (0, 2) else low
        scalars["owners"] = owners
        have = run_plan(stream, hidden, scalars, own_facts, paths, lambda hidden: pick(hidden, owners, tok), early_own, early_other)
        out, dstream, grad_head = product(
            have["owners"],
            0,
            have["other picks"],
            (have["coefs"], head_half, [have[b] for b in last]),
            (),
            have["other sum"],
            [have["early parts"], have["middle parts"]],
        )
        swapped = to_core(out)
        grad_head = grad_head[0]
        other_head = to_core(grad_head)
        grad_head = gain * jnp.where(
            have["first core"], jnp.concatenate([grad_head, other_head]), jnp.concatenate([other_head, grad_head])
        )
        (grad_down,) = product(
            have["owners"], 0, have["own picks"], None, [dstream, have["middle dstream"]], have["early own"], (), have["where"]
        )
        grad_down = put(grad_down, swapped, have["elsewhere"])
        return (have["values"], have["returns"], grad_head, grad_down)

    return body


def solution(mesh):
    placed = (P("seq", "tp"), P("seq", None), P("tp"), P("tp"), P("seq"), P("seq"), P("seq"))

    def run(stream, *rest):
        return jax.shard_map(
            make_body(stream.shape[1], mesh.shape["seq"]),
            mesh=mesh,
            in_specs=placed,
            out_specs=(P("seq"), P("seq"), P("tp"), P("seq", "tp")),
            check_vma=False,
        )(stream, *rest)

    return run
```

```python
import functools

import jax
import jax.numpy as jnp
import numpy as np
from jax import lax
from jax.experimental import pallas as pl
from jax.experimental.pallas import tpu as pltpu
from jax.sharding import PartitionSpec as P

EPSILON = 1e-05


def butterfly_sum(x, axis):
    count = lax.axis_size(axis)
    step = 1
    while step < count:
        x = x + lax.ppermute(x, axis, [(i, i ^ step) for i in range(count)])
        step *= 2
    return x


def butterfly_send(x, axis, bit):
    return lax.ppermute(x, axis, [(i, i ^ bit) for i in range(lax.axis_size(axis))])


def butterfly_merge(x, other, bit, low):
    low = low[bit]
    if bit == 1:
        return jnp.where(low[:, None, None], x, other)
    if bit == 4:
        return jnp.where(low[:, None, None, None], x[None], other[None])
    if bit == 2:
        both = jnp.stack([jnp.where(low, x, other), jnp.where(low, other, x)], axis=1)
        return both.reshape(-1, *x.shape[2:])
    return jnp.concatenate([jnp.where(low, x, other), jnp.where(low, other, x)])


class Paths:
    def __init__(self, count):
        self.count = count
        self.m = count // 4
        self.order = list(range(0, self.m, 2)) + list(range(self.m - 1 - self.m % 2, 0, -2))
        self.place = [self.order.index(z) for z in range(self.m)]
        self.across = [(i, i ^ 2) for i in range(count)]
        self.core = [(i, i ^ 1) for i in range(count)]
        self.ring = [self._ring(1), self._ring(-1)]

    def _ring(self, way):
        pairs = []
        for i in range(self.count):
            z, rest = divmod(i, 4)
            by = way if i % 2 == 0 else -way
            pairs.append((i, self.order[(self.place[z] + by) % self.m] * 4 + rest))
        return pairs

    def owners(self, blocks):
        table = np.zeros((self.count, len(blocks)), np.int32)
        for me in range(self.count):
            z, rest = divmod(me, 4)
            for b, (steps, across, kind) in enumerate(blocks):
                way = -1 if (me % 2 == 0) == (kind == 0) else 1
                table[me, b] = self.order[(self.place[z] + way * steps) % self.m] * 4 + (rest ^ (2 * across + kind))
        return table


class Flights:
    def __init__(self, **arrays):
        self.have = arrays

    def event(self, waits, sends=()):
        names = list(dict.fromkeys([*waits, *(source for _, source, _ in sends)]))
        self.have.update(zip(names, lax.optimization_barrier(tuple(self.have[n] for n in names))))
        for name, source, pairs in sends:
            self.have[name] = lax.ppermute(self.have[source], "seq", pairs)


def block_groups(m):
    last = [(m - 1, 1, 0), (m - 1, 1, 1)]
    middle = [(m - 2, 1, 0), (m - 2, 1, 1), (m - 1, 0, 0), (m - 1, 0, 1)]
    early = [(k, a, kind) for k in range(m - 1) for a in range(2) for kind in range(2) if k < m - 2 or a == 0]
    return last, middle, early


def run_plan(stream, hidden, scalars, own_facts, paths, pick_both, early_own, early_other):
    half = stream.shape[1] // 2
    m, ring, across, core = paths.m, paths.ring, paths.across, paths.core
    cut = lambda c: lax.dynamic_slice_in_dim(stream, c * half, half, 1)
    core_index = scalars["core"]
    f = Flights(stream=stream, hidden=hidden, away=cut(1 - core_index), **scalars)
    f.have[0, 0, 0] = cut(core_index)
    have = f.have
    names = list(scalars)
    low = lambda: {1 << n: have["low %d" % n] for n in range(paths.count.bit_length() - 1)}

    bits = [1, 4, 2] + [8 << n for n in range(paths.count.bit_length() - 4)]

    def facts_send():
        have["other facts"] = butterfly_send(have["facts"], "seq", bits[0])

    def facts_merge():
        have["facts"] = butterfly_merge(have["facts"], have["other facts"], bits.pop(0), low())

    def facts_step():
        if bits:
            facts_send()
            facts_merge()

    f.event([], [((1, 0, 0), (0, 0, 0), ring[0]), ((0, 1, 0), (0, 0, 0), across), ((0, 0, 1), "away", core)])
    f.event(
        [(0, 0, 1), "stream", *names],
        [((1, 0, 1), (0, 0, 1), ring[1]), ((0, 1, 1), (0, 0, 1), across)],
    )
    have["facts"] = butterfly_sum(own_facts(have["stream"]), "tp")[None]
    f.event(["facts", "hidden"])
    have["own picks"], have["away picks"] = pick_both(have["hidden"])
    f.event(
        [(1, 0, 0), (0, 1, 0), "facts", "own picks", "away picks"],
        [((2, 0, 0), (1, 0, 0), ring[0]), ((1, 1, 0), (1, 0, 0), across)],
    )
    facts_step()
    facts_send()
    f.event([(1, 0, 1), (0, 1, 1), "facts", "other facts"], [((2, 0, 1), (1, 0, 1), ring[1]), ((1, 1, 1), (1, 0, 1), across)])
    facts_merge()
    for k in range(2, m):
        for kind in range(2):
            pending = bits and (k, kind) == (m - 2, 1)
            if pending:
                facts_send()
            elif k < m - 1:
                facts_step()
            if k < m - 1:
                sends = [((k + 1, 0, kind), (k, 0, kind), ring[kind]), ((k, 1, kind), (k, 0, kind), across)]
            elif kind == 0:
                sends = []
            else:
                sends = [((k, 1, 0), (k - 1, 1, 0), ring[0]), ((k, 1, 1), (k, 0, 1), across)]
            waits = [(k, 0, kind), (k - 1, 1, kind)]
            if (k, kind) != (m - 2, 1):
                waits += ["facts"] + ["other facts"] * bool(bits)
            if k == m - 1 and kind == 0:
                sends.append(("other picks", "away picks", core))
            if k == m - 1 and kind == 1:
                waits += ["other picks", "early own", "values", "returns"]
            f.event(waits, sends)
            if k == m - 1 and kind == 0:
                if bits:
                    facts_merge()
                while bits:
                    facts_step()
                early_own(have)
    early_other(have)
    f.event([(m - 1, 1, 0), (m - 1, 1, 1), "other sum"])
    return have


def params(tokens):
    return pltpu.CompilerParams(vmem_limit_bytes=(9 if tokens <= 4096 else 40) * 1024 * 1024)


def cost(units, k, width, extra):
    return pl.CostEstimate(
        flops=2 * units * k * width, bytes_accessed=2 * (units * k + k * width) + extra, transcendentals=0
    )


def pieces_of(units):
    return next(n for n in (7, 4, 2, 1) if units % (16 * n) == 0)


def pick_kernel(tok, owners, hidden, own, away, held, turned, sems_in, sems_out):
    units, tokens = hidden.shape
    count = tokens // tok
    pieces = pieces_of(units)
    size = units // pieces
    rows = [pl.ds(n * size, size) for n in range(pieces)]
    fetch = [pltpu.make_async_copy(hidden.at[r, :], held.at[r, :], sems_in.at[n]) for n, r in enumerate(rows)]
    place = [pltpu.make_async_copy(turned.at[r, :], away.at[r, :], sems_out.at[n]) for n, r in enumerate(rows)]
    for copy in fetch:
        copy.start()
    for n, r in enumerate(rows):
        fetch[n].wait()
        for m, out in enumerate((own, turned)):
            for b in range(count):
                columns = pl.ds(pl.multiple_of(owners[m * count + b] * tok, tok), tok)
                out[r, b * tok : (b + 1) * tok] = held[r, columns]
        place[n].start()
    for copy in place:
        copy.wait()


def pick(hidden, owners, tok):
    inside = pl.BlockSpec(memory_space=pltpu.VMEM)
    anywhere = pl.BlockSpec(memory_space=pl.ANY)
    pieces = pieces_of(hidden.shape[0])
    return pl.pallas_call(
        functools.partial(pick_kernel, tok),
        grid_spec=pltpu.PrefetchScalarGridSpec(
            num_scalar_prefetch=1,
            grid=(),
            in_specs=[anywhere],
            out_specs=[inside, anywhere],
            scratch_shapes=[pltpu.VMEM(hidden.shape, hidden.dtype)] * 2 + [pltpu.SemaphoreType.DMA((pieces,))] * 2,
        ),
        out_shape=[pltpu.VMEM(hidden.shape, hidden.dtype), pltpu.HBM(hidden.shape, hidden.dtype)],
        compiler_params=params(hidden.shape[1]),
        cost_estimate=cost(0, 0, 0, 1),
    )(owners, pltpu.with_memory_space_constraint(hidden, pltpu.HBM))


def spread(tok, owners, first, coefs, weights, pulls):
    for b in range(weights.shape[0] // tok):
        coef = coefs[:, pl.ds(pl.multiple_of(owners[first + b] * tok, tok), tok)].T
        rows = slice(b * tok, (b + 1) * tok)
        weights[rows, :] = jnp.broadcast_to(coef[:, 0:1], (tok, 128))
        pulls[rows, :] = jnp.broadcast_to(coef[:, 1:2], (tok, 128))


def form(tok, owners, first, weights, pulls, head, blocks, dstream, parts, start, chunk):
    for b in range(len(blocks)):
        rows = slice(b * tok, (b + 1) * tok)
        for at in range(0, chunk, 128):
            lanes = slice(start + at, start + at + 128)
            stream_f = blocks[b][:, lanes].astype(jnp.float32)
            weight = weights[rows, :]
            dstream[rows, lanes] = (weight * head[:, lanes] - pulls[rows, :] * stream_f).astype(jnp.bfloat16)
            parts[owners[first + b], :, lanes] = jnp.sum(weight * stream_f, axis=0, keepdims=True)


def product_kernel(tok, count, first, given_count, added, parts_count, wide, chunk, owners, where, *refs):
    refs = list(refs)
    take = lambda n: [refs.pop(0) for _ in range(n)]
    (picked,) = take(1)
    coefs, head = take(2) if count else (None, None)
    blocks, given, total, other_parts = take(count), take(given_count), take(added), take(parts_count)
    (out,) = take(1)
    dstream, parts_out = take(2) if count else (None, None)
    weights, pulls, parts = take(3) if count else (None, None, None)
    out_v = take(1)[0] if wide else out
    (sem_out,) = take(1)
    half = out_v.shape[1]
    steps = half // chunk
    base = pl.multiple_of(where[0] * half, half)

    columns = lambda c: pl.ds(c * chunk, chunk)

    def put_out(c):
        there = pl.ds(pl.multiple_of(base + c * chunk, chunk), chunk)
        return pltpu.make_async_copy(out_v.at[:, columns(c)], out.at[:, there], sem_out.at[c])

    if count:
        parts[...] = jnp.zeros_like(parts)
        spread(tok, owners, first, coefs, weights, pulls)

    def form_chunk(c):
        if count and c < steps:
            form(tok, owners, first, weights, pulls, head, blocks, dstream, parts, c * chunk, chunk)

    factors = ([dstream] if count else []) + given
    form_chunk(0)
    for c in range(steps):
        form_chunk(c + 1)
        here = total[0][:, columns(c)] if added else None
        at = first * tok
        for factor in factors:
            depth = factor.shape[0]
            term = jnp.dot(picked[:, at : at + depth], factor[:, columns(c)], preferred_element_type=jnp.float32)
            here = term if here is None else here + term
            at += depth
        out_v[:, columns(c)] = here.astype(out_v.dtype)
        if wide:
            put_out(c).start()
    if count:
        if other_parts:
            parts_out[...] = sum([p[...] for p in other_parts], parts[...]).sum(axis=0)
        else:
            parts_out[...] = parts[...]
    if wide:
        for c in range(steps):
            put_out(c).wait()


def product(owners, first, picked, formed=None, given=(), total=None, parts=(), where=None):
    units, tokens = picked.shape
    coefs, head, blocks = formed or (None, None, [])
    half = blocks[0].shape[1] if blocks else given[0].shape[1]
    count = len(blocks)
    tok = tokens // owners.shape[0] * 2
    k = count * tok + sum(g.shape[0] for g in given)
    chunk = next(t for t in (512 if tokens <= 4096 else 256, 128, half) if half % t == 0)
    steps = half // chunk
    added, wide = total is not None, where is not None
    anywhere = pl.BlockSpec(memory_space=pl.ANY)
    inside = pl.BlockSpec(memory_space=pltpu.VMEM)
    in_vmem = lambda x: pltpu.with_memory_space_constraint(x, pltpu.VMEM)
    out_type = jnp.bfloat16 if added else jnp.float32
    if wide:
        out_specs = [anywhere]
        out_shape = [jax.ShapeDtypeStruct((units, 2 * half), out_type)]
    else:
        out_specs = [inside]
        out_shape = [pltpu.VMEM((units, half), out_type)]
    scratch = []
    parts_shape = (tokens // tok, 1, half)
    if count:
        out_specs += [inside, inside]
        out_shape += [
            pltpu.VMEM((count * tok, half), jnp.bfloat16),
            jax.ShapeDtypeStruct(parts_shape[1:] if parts else parts_shape, jnp.float32),
        ]
        scratch += [pltpu.VMEM((count * tok, 128), jnp.float32)] * 2 + [pltpu.VMEM(parts_shape, jnp.float32)]
    if wide:
        scratch += [pltpu.VMEM((units, half), out_type)]
    sems = [(steps,)]
    return pl.pallas_call(
        functools.partial(product_kernel, tok, count, first, len(given), int(added), len(parts), wide, chunk),
        grid_spec=pltpu.PrefetchScalarGridSpec(
            num_scalar_prefetch=2,
            grid=(),
            in_specs=[inside] * (1 + 2 * bool(count) + count + len(given) + added + len(parts)),
            out_specs=out_specs,
            scratch_shapes=scratch + [pltpu.SemaphoreType.DMA(shape) for shape in sems],
        ),
        out_shape=out_shape,
        compiler_params=params(tokens),
        cost_estimate=cost(units, k * (1 if added or given else 10), half, 6 * units * half),
    )(
        owners,
        where if wide else jnp.zeros((1,), jnp.int32),
        in_vmem(picked),
        *([coefs, head] if count else []),
        *[in_vmem(x) for x in blocks],
        *[in_vmem(x) for x in given],
        *([in_vmem(total)] if added else []),
        *parts,
    )


def put_kernel(pieces, where, part, whole, out, sems):
    units, width = part.shape
    start = pl.multiple_of(where[0] * width, width)
    rows = [pl.ds(n * (units // pieces), units // pieces) for n in range(pieces)]
    place = [
        pltpu.make_async_copy(part.at[r, :], out.at[r, pl.ds(start, width)], sems.at[n]) for n, r in enumerate(rows)
    ]
    for copy in place:
        copy.start()
    for copy in place:
        copy.wait()


def put(whole, part, where):
    units, width = part.shape
    pieces = pieces_of(units)
    anywhere = pl.BlockSpec(memory_space=pl.ANY)
    return pl.pallas_call(
        functools.partial(put_kernel, pieces),
        grid_spec=pltpu.PrefetchScalarGridSpec(
            num_scalar_prefetch=1,
            grid=(),
            in_specs=[pl.BlockSpec(memory_space=pltpu.VMEM), anywhere],
            out_specs=anywhere,
            scratch_shapes=[pltpu.SemaphoreType.DMA((pieces,))],
        ),
        out_shape=jax.ShapeDtypeStruct(whole.shape, whole.dtype),
        input_output_aliases={2: 0},
        compiler_params=params(0),
        cost_estimate=cost(0, 0, 0, 4 * units * width),
    )(where, pltpu.with_memory_space_constraint(part, pltpu.VMEM), whole)


def all_returns(step_reward, resets):
    shards, tok = step_reward.shape
    position = jnp.arange(tok)
    earlier = position[None, :] < position[:, None]
    before = jnp.sum(jnp.where(earlier[None], resets[:, None, :], 0.0), axis=2)
    total = jnp.sum(resets, axis=1, keepdims=True)
    reach = (position[None, :] >= position[:, None])[None] & (before[:, None, :] == before[:, :, None])
    local = jnp.sum(jnp.where(reach, step_reward[:, None, :], 0.0), axis=2)
    passing = before == total
    blocked = jnp.where(passing[:, 0], 0.0, 1.0)
    ids = jnp.arange(shards)
    later = ids[None, :] > ids[:, None]
    between = later[:, None, :] & (ids[None, :] < ids[:, None])[None]
    open_path = later & (jnp.sum(jnp.where(between, blocked[None, None, :], 0.0), axis=2) == 0.0)
    incoming = jnp.sum(jnp.where(open_path, local[None, :, 0], 0.0), axis=1)
    return local + jnp.where(passing, incoming[:, None], 0.0)


def make_body(width, shards):
    paths = Paths(shards)

    def body(stream, hidden, final_gain, value_head, rewards, kl_terms, resets):
        tok, local = stream.shape
        half = local // 2
        me = lax.axis_index("seq")
        mine = me % 2
        gain = final_gain.astype(jnp.float32)
        head = gain * value_head.astype(jnp.float32)
        head_half = lax.dynamic_slice_in_dim(head, mine * half, half)[None]
        to_core = lambda x: lax.ppermute(x, "seq", paths.core)
        own = lambda a: lax.dynamic_index_in_dim(a, me, 0, keepdims=False)
        last, middle, early = block_groups(paths.m)
        table = paths.owners(last + middle + early)
        both = np.concatenate([table, table[np.arange(shards) ^ 1]], axis=1)
        owners = own(jnp.asarray(both))
        early_at = len(last + middle)

        def own_facts(stream):
            stream_f = stream.astype(jnp.float32)
            share = jnp.where(lax.axis_index("tp") == 0, 1.0, 0.0)
            return jnp.stack(
                [
                    jnp.sum(stream_f * stream_f, axis=-1),
                    jnp.sum(stream_f * head, axis=-1),
                    (rewards - 0.2 * kl_terms) * share,
                    resets.astype(jnp.float32) * share,
                ]
            )

        def early_own(have):
            sum_squares, along, step_reward, cut = (have["facts"][:, k] for k in range(4))
            scale = lax.rsqrt(sum_squares / width + EPSILON)
            values = scale * along
            returns = all_returns(step_reward, cut)
            error = values - returns
            pull = scale**3 * along / width
            coefs = jnp.stack([error * scale, error * pull]).reshape(2, shards * tok)
            coefs = jnp.pad(coefs, ((0, 6), (0, 0)))
            mask = jnp.arange(shards)[:, None] == have["me"]
            row = lambda a: jnp.sum(jnp.where(mask, a, 0.0), axis=0)
            have.update(values=row(values), returns=row(returns), coefs=coefs)
            have["early own"], have["early dstream"], have["early parts"] = product(
                have["owners"], early_at, have["own picks"], (coefs, head_half, [have[b] for b in early])
            )

        def early_other(have):
            have["other sum"], have["middle dstream"], have["middle parts"] = product(
                have["owners"],
                len(last),
                have["other picks"],
                (have["coefs"], head_half, [have[b] for b in middle]),
                [have["early dstream"]],
            )

        where = mine[None].astype(jnp.int32)
        scalars = {"core": mine, "me": me, "first core": mine == 0, "where": where, "elsewhere": 1 - where}
        for n in range(shards.bit_length() - 1):
            low = (me >> n) % 2 == 0
            scalars["low %d" % n] = (jnp.arange(2) == 0) == low if n in (0, 2) else low
        scalars["owners"] = owners
        have = run_plan(stream, hidden, scalars, own_facts, paths, lambda hidden: pick(hidden, owners, tok), early_own, early_other)
        out, dstream, grad_head = product(
            have["owners"],
            0,
            have["other picks"],
            (have["coefs"], head_half, [have[b] for b in last]),
            (),
            have["other sum"],
            [have["early parts"], have["middle parts"]],
        )
        swapped = to_core(out)
        grad_head = grad_head[0]
        other_head = to_core(grad_head)
        grad_head = gain * jnp.where(
            have["first core"], jnp.concatenate([grad_head, other_head]), jnp.concatenate([other_head, grad_head])
        )
        (grad_down,) = product(
            have["owners"], 0, have["own picks"], None, [dstream, have["middle dstream"]], have["early own"], (), have["where"]
        )
        grad_down = put(grad_down, swapped, have["elsewhere"])
        return (have["values"], have["returns"], grad_head, grad_down)

    return body


def solution(mesh):
    placed = (P("seq", "tp"), P("seq", None), P("tp"), P("tp"), P("seq"), P("seq"), P("seq"))

    def run(stream, *rest):
        return jax.shard_map(
            make_body(stream.shape[1], mesh.shape["seq"]),
            mesh=mesh,
            in_specs=placed,
            out_specs=(P("seq"), P("seq"), P("tp"), P("seq", "tp")),
            check_vma=False,
        )(stream, *rest)

    return run
```

```python
import functools

import jax
import jax.numpy as jnp
import numpy as np
from jax import lax
from jax.experimental import pallas as pl
from jax.experimental.pallas import tpu as pltpu
from jax.sharding import PartitionSpec as P

EPSILON = 1e-05


def butterfly_sum(x, axis):
    count = lax.axis_size(axis)
    step = 1
    while step < count:
        x = x + lax.ppermute(x, axis, [(i, i ^ step) for i in range(count)])
        step *= 2
    return x


def butterfly_send(x, axis, bit):
    return lax.ppermute(x, axis, [(i, i ^ bit) for i in range(lax.axis_size(axis))])


def butterfly_merge(x, other, bit, low):
    low = low[bit]
    if bit == 1:
        return jnp.where(low[:, None, None], x, other)
    if bit == 4:
        return jnp.where(low[:, None, None, None], x[None], other[None])
    if bit == 2:
        both = jnp.stack([jnp.where(low, x, other), jnp.where(low, other, x)], axis=1)
        return both.reshape(-1, *x.shape[2:])
    return jnp.concatenate([jnp.where(low, x, other), jnp.where(low, other, x)])


class Paths:
    def __init__(self, count):
        self.count = count
        self.m = count // 4
        self.order = list(range(0, self.m, 2)) + list(range(self.m - 1 - self.m % 2, 0, -2))
        self.place = [self.order.index(z) for z in range(self.m)]
        self.across = [(i, i ^ 2) for i in range(count)]
        self.core = [(i, i ^ 1) for i in range(count)]
        self.ring = [self._ring(1), self._ring(-1)]

    def _ring(self, way):
        pairs = []
        for i in range(self.count):
            z, rest = divmod(i, 4)
            by = way if i % 2 == 0 else -way
            pairs.append((i, self.order[(self.place[z] + by) % self.m] * 4 + rest))
        return pairs

    def owners(self, blocks):
        table = np.zeros((self.count, len(blocks)), np.int32)
        for me in range(self.count):
            z, rest = divmod(me, 4)
            for b, (steps, across, kind) in enumerate(blocks):
                way = -1 if (me % 2 == 0) == (kind == 0) else 1
                table[me, b] = self.order[(self.place[z] + way * steps) % self.m] * 4 + (rest ^ (2 * across + kind))
        return table


class Flights:
    def __init__(self, **arrays):
        self.have = arrays

    def event(self, waits, sends=()):
        names = list(dict.fromkeys([*waits, *(source for _, source, _ in sends)]))
        self.have.update(zip(names, lax.optimization_barrier(tuple(self.have[n] for n in names))))
        for name, source, pairs in sends:
            self.have[name] = lax.ppermute(self.have[source], "seq", pairs)


def block_groups(m):
    last = [(m - 1, 1, 0), (m - 1, 1, 1)]
    middle = [(m - 2, 1, 0), (m - 2, 1, 1), (m - 1, 0, 0), (m - 1, 0, 1)]
    early = [(k, a, kind) for k in range(m - 1) for a in range(2) for kind in range(2) if k < m - 2 or a == 0]
    return last, middle, early


def run_plan(stream, hidden, scalars, own_facts, paths, pick_both, early_own, early_other):
    half = stream.shape[1] // 2
    m, ring, across, core = paths.m, paths.ring, paths.across, paths.core
    cut = lambda c: lax.dynamic_slice_in_dim(stream, c * half, half, 1)
    core_index = scalars["core"]
    f = Flights(stream=stream, hidden=hidden, away=cut(1 - core_index), **scalars)
    f.have[0, 0, 0] = cut(core_index)
    have = f.have
    names = list(scalars)
    low = lambda: {1 << n: have["low %d" % n] for n in range(paths.count.bit_length() - 1)}

    bits = [1, 4, 2] + [8 << n for n in range(paths.count.bit_length() - 4)]

    def facts_send():
        have["other facts"] = butterfly_send(have["facts"], "seq", bits[0])

    def facts_merge():
        have["facts"] = butterfly_merge(have["facts"], have["other facts"], bits.pop(0), low())

    def facts_step():
        if bits:
            facts_send()
            facts_merge()

    f.event([], [((1, 0, 0), (0, 0, 0), ring[0]), ((0, 1, 0), (0, 0, 0), across), ((0, 0, 1), "away", core)])
    f.event(
        [(0, 0, 1), "stream", *names],
        [((1, 0, 1), (0, 0, 1), ring[1]), ((0, 1, 1), (0, 0, 1), across)],
    )
    have["facts"] = butterfly_sum(own_facts(have["stream"]), "tp")[None]
    f.event(["facts", "hidden"])
    have["own picks"], have["away picks"] = pick_both(have["hidden"])
    f.event(
        [(1, 0, 0), (0, 1, 0), "facts", "own picks", "away picks"],
        [((2, 0, 0), (1, 0, 0), ring[0]), ((1, 1, 0), (1, 0, 0), across)],
    )
    facts_step()
    facts_send()
    f.event([(1, 0, 1), (0, 1, 1), "facts", "other facts"], [((2, 0, 1), (1, 0, 1), ring[1]), ((1, 1, 1), (1, 0, 1), across)])
    facts_merge()
    for k in range(2, m):
        for kind in range(2):
            facts_step()
            if k < m - 1:
                sends = [((k + 1, 0, kind), (k, 0, kind), ring[kind]), ((k, 1, kind), (k, 0, kind), across)]
            elif kind == 0:
                sends = []
            else:
                sends = [((k, 1, 0), (k - 1, 1, 0), ring[0]), ((k, 1, 1), (k, 0, 1), across)]
            waits = [(k, 0, kind), (k - 1, 1, kind), "facts"]
            if k == m - 2 and kind == 1:
                sends.append(("other picks", "away picks", core))
            if k == m - 1 and kind == 1:
                waits += ["other picks", "early own", "values", "returns"]
            f.event(waits, sends)
            if k == m - 2 and kind == 1:
                while bits:
                    facts_step()
                early_own(have)
    early_other(have)
    f.event([(m - 1, 1, 0), (m - 1, 1, 1), "other sum"])
    return have


def params(tokens):
    return pltpu.CompilerParams(vmem_limit_bytes=(9 if tokens <= 4096 else 40) * 1024 * 1024)


def cost(units, k, width, extra):
    return pl.CostEstimate(
        flops=2 * units * k * width, bytes_accessed=2 * (units * k + k * width) + extra, transcendentals=0
    )


def pieces_of(units):
    return next(n for n in (7, 4, 2, 1) if units % (16 * n) == 0)


def pick_kernel(tok, owners, hidden, own, away, held, turned, sems_in, sems_out):
    units, tokens = hidden.shape
    count = tokens // tok
    pieces = pieces_of(units)
    size = units // pieces
    rows = [pl.ds(n * size, size) for n in range(pieces)]
    fetch = [pltpu.make_async_copy(hidden.at[r, :], held.at[r, :], sems_in.at[n]) for n, r in enumerate(rows)]
    place = [pltpu.make_async_copy(turned.at[r, :], away.at[r, :], sems_out.at[n]) for n, r in enumerate(rows)]
    for copy in fetch:
        copy.start()
    for n, r in enumerate(rows):
        fetch[n].wait()
        for m, out in enumerate((own, turned)):
            for b in range(count):
                columns = pl.ds(pl.multiple_of(owners[m * count + b] * tok, tok), tok)
                out[r, b * tok : (b + 1) * tok] = held[r, columns]
        place[n].start()
    for copy in place:
        copy.wait()


def pick(hidden, owners, tok):
    inside = pl.BlockSpec(memory_space=pltpu.VMEM)
    anywhere = pl.BlockSpec(memory_space=pl.ANY)
    pieces = pieces_of(hidden.shape[0])
    return pl.pallas_call(
        functools.partial(pick_kernel, tok),
        grid_spec=pltpu.PrefetchScalarGridSpec(
            num_scalar_prefetch=1,
            grid=(),
            in_specs=[anywhere],
            out_specs=[inside, anywhere],
            scratch_shapes=[pltpu.VMEM(hidden.shape, hidden.dtype)] * 2 + [pltpu.SemaphoreType.DMA((pieces,))] * 2,
        ),
        out_shape=[pltpu.VMEM(hidden.shape, hidden.dtype), pltpu.HBM(hidden.shape, hidden.dtype)],
        compiler_params=params(hidden.shape[1]),
        cost_estimate=cost(0, 0, 0, 1),
    )(owners, pltpu.with_memory_space_constraint(hidden, pltpu.HBM))


def spread(tok, owners, first, coefs, weights, pulls):
    for b in range(weights.shape[0] // tok):
        coef = coefs[:, pl.ds(pl.multiple_of(owners[first + b] * tok, tok), tok)].T
        rows = slice(b * tok, (b + 1) * tok)
        weights[rows, :] = jnp.broadcast_to(coef[:, 0:1], (tok, 128))
        pulls[rows, :] = jnp.broadcast_to(coef[:, 1:2], (tok, 128))


def form(tok, owners, first, weights, pulls, head, blocks, dstream, parts, start, chunk):
    for b in range(len(blocks)):
        rows = slice(b * tok, (b + 1) * tok)
        for at in range(0, chunk, 128):
            lanes = slice(start + at, start + at + 128)
            stream_f = blocks[b][:, lanes].astype(jnp.float32)
            weight = weights[rows, :]
            dstream[rows, lanes] = (weight * head[:, lanes] - pulls[rows, :] * stream_f).astype(jnp.bfloat16)
            parts[owners[first + b], :, lanes] = jnp.sum(weight * stream_f, axis=0, keepdims=True)


def product_kernel(tok, count, first, given_count, added, parts_count, wide, chunk, owners, where, *refs):
    refs = list(refs)
    take = lambda n: [refs.pop(0) for _ in range(n)]
    (picked,) = take(1)
    coefs, head = take(2) if count else (None, None)
    blocks, given, total, other_parts = take(count), take(given_count), take(added), take(parts_count)
    (out,) = take(1)
    dstream, parts_out = take(2) if count else (None, None)
    weights, pulls, parts = take(3) if count else (None, None, None)
    out_v = take(1)[0] if wide else out
    (sem_out,) = take(1)
    half = out_v.shape[1]
    steps = half // chunk
    base = pl.multiple_of(where[0] * half, half)

    columns = lambda c: pl.ds(c * chunk, chunk)

    def put_out(c):
        there = pl.ds(pl.multiple_of(base + c * chunk, chunk), chunk)
        return pltpu.make_async_copy(out_v.at[:, columns(c)], out.at[:, there], sem_out.at[c])

    if count:
        parts[...] = jnp.zeros_like(parts)
        spread(tok, owners, first, coefs, weights, pulls)

    def form_chunk(c):
        if count and c < steps:
            form(tok, owners, first, weights, pulls, head, blocks, dstream, parts, c * chunk, chunk)

    factors = ([dstream] if count else []) + given
    form_chunk(0)
    for c in range(steps):
        form_chunk(c + 1)
        here = total[0][:, columns(c)] if added else None
        at = first * tok
        for factor in factors:
            depth = factor.shape[0]
            term = jnp.dot(picked[:, at : at + depth], factor[:, columns(c)], preferred_element_type=jnp.float32)
            here = term if here is None else here + term
            at += depth
        out_v[:, columns(c)] = here.astype(out_v.dtype)
        if wide:
            put_out(c).start()
    if count:
        if other_parts:
            parts_out[...] = sum([p[...] for p in other_parts], parts[...]).sum(axis=0)
        else:
            parts_out[...] = parts[...]
    if wide:
        for c in range(steps):
            put_out(c).wait()


def product(owners, first, picked, formed=None, given=(), total=None, parts=(), where=None):
    units, tokens = picked.shape
    coefs, head, blocks = formed or (None, None, [])
    half = blocks[0].shape[1] if blocks else given[0].shape[1]
    count = len(blocks)
    tok = tokens // owners.shape[0] * 2
    k = count * tok + sum(g.shape[0] for g in given)
    chunk = next(t for t in (512 if tokens <= 4096 else 256, 128, half) if half % t == 0)
    steps = half // chunk
    added, wide = total is not None, where is not None
    anywhere = pl.BlockSpec(memory_space=pl.ANY)
    inside = pl.BlockSpec(memory_space=pltpu.VMEM)
    in_vmem = lambda x: pltpu.with_memory_space_constraint(x, pltpu.VMEM)
    out_type = jnp.bfloat16 if added else jnp.float32
    if wide:
        out_specs = [anywhere]
        out_shape = [jax.ShapeDtypeStruct((units, 2 * half), out_type)]
    else:
        out_specs = [inside]
        out_shape = [pltpu.VMEM((units, half), out_type)]
    scratch = []
    parts_shape = (tokens // tok, 1, half)
    if count:
        out_specs += [inside, inside]
        out_shape += [
            pltpu.VMEM((count * tok, half), jnp.bfloat16),
            jax.ShapeDtypeStruct(parts_shape[1:] if parts else parts_shape, jnp.float32),
        ]
        scratch += [pltpu.VMEM((count * tok, 128), jnp.float32)] * 2 + [pltpu.VMEM(parts_shape, jnp.float32)]
    if wide:
        scratch += [pltpu.VMEM((units, half), out_type)]
    sems = [(steps,)]
    return pl.pallas_call(
        functools.partial(product_kernel, tok, count, first, len(given), int(added), len(parts), wide, chunk),
        grid_spec=pltpu.PrefetchScalarGridSpec(
            num_scalar_prefetch=2,
            grid=(),
            in_specs=[inside] * (1 + 2 * bool(count) + count + len(given) + added + len(parts)),
            out_specs=out_specs,
            scratch_shapes=scratch + [pltpu.SemaphoreType.DMA(shape) for shape in sems],
        ),
        out_shape=out_shape,
        compiler_params=params(tokens),
        cost_estimate=cost(units, k * (1 if added or given else 10), half, 6 * units * half),
    )(
        owners,
        where if wide else jnp.zeros((1,), jnp.int32),
        in_vmem(picked),
        *([coefs, head] if count else []),
        *[in_vmem(x) for x in blocks],
        *[in_vmem(x) for x in given],
        *([in_vmem(total)] if added else []),
        *parts,
    )


def put_kernel(pieces, where, part, head, other_head, gain, whole, out, grad, sems):
    units, width = part.shape
    start = pl.multiple_of(where[0] * width, width)
    rows = [pl.ds(n * (units // pieces), units // pieces) for n in range(pieces)]
    place = [
        pltpu.make_async_copy(part.at[r, :], out.at[r, pl.ds(start, width)], sems.at[n]) for n, r in enumerate(rows)
    ]
    for copy in place:
        copy.start()
    there = pl.ds(start, width)
    here = pl.ds(pl.multiple_of((1 - where[0]) * width, width), width)
    grad[:, there] = gain[:, there] * other_head[...]
    grad[:, here] = gain[:, here] * head[...]
    for copy in place:
        copy.wait()


def put(whole, part, where, head, other_head, gain):
    units, width = part.shape
    pieces = pieces_of(units)
    anywhere = pl.BlockSpec(memory_space=pl.ANY)
    inside = pl.BlockSpec(memory_space=pltpu.VMEM)
    return pl.pallas_call(
        functools.partial(put_kernel, pieces),
        grid_spec=pltpu.PrefetchScalarGridSpec(
            num_scalar_prefetch=1,
            grid=(),
            in_specs=[inside] * 4 + [anywhere],
            out_specs=[anywhere, inside],
            scratch_shapes=[pltpu.SemaphoreType.DMA((pieces,))],
        ),
        out_shape=[
            jax.ShapeDtypeStruct(whole.shape, whole.dtype),
            jax.ShapeDtypeStruct(gain.shape, jnp.float32),
        ],
        input_output_aliases={5: 0},
        compiler_params=params(0),
        cost_estimate=cost(0, 0, 0, 4 * units * width),
    )(where, pltpu.with_memory_space_constraint(part, pltpu.VMEM), head, other_head, gain, whole)


def all_returns(step_reward, resets):
    shards, tok = step_reward.shape
    position = jnp.arange(tok)
    earlier = position[None, :] < position[:, None]
    before = jnp.sum(jnp.where(earlier[None], resets[:, None, :], 0.0), axis=2)
    total = jnp.sum(resets, axis=1, keepdims=True)
    reach = (position[None, :] >= position[:, None])[None] & (before[:, None, :] == before[:, :, None])
    local = jnp.sum(jnp.where(reach, step_reward[:, None, :], 0.0), axis=2)
    passing = before == total
    blocked = jnp.where(passing[:, 0], 0.0, 1.0)
    ids = jnp.arange(shards)
    later = ids[None, :] > ids[:, None]
    between = later[:, None, :] & (ids[None, :] < ids[:, None])[None]
    open_path = later & (jnp.sum(jnp.where(between, blocked[None, None, :], 0.0), axis=2) == 0.0)
    incoming = jnp.sum(jnp.where(open_path, local[None, :, 0], 0.0), axis=1)
    return local + jnp.where(passing, incoming[:, None], 0.0)


def make_body(width, shards):
    paths = Paths(shards)

    def body(stream, hidden, final_gain, value_head, rewards, kl_terms, resets):
        tok, local = stream.shape
        half = local // 2
        me = lax.axis_index("seq")
        mine = me % 2
        gain = final_gain.astype(jnp.float32)
        head = gain * value_head.astype(jnp.float32)
        head_half = lax.dynamic_slice_in_dim(head, mine * half, half)[None]
        to_core = lambda x: lax.ppermute(x, "seq", paths.core)
        own = lambda a: lax.dynamic_index_in_dim(a, me, 0, keepdims=False)
        last, middle, early = block_groups(paths.m)
        table = paths.owners(last + middle + early)
        both = np.concatenate([table, table[np.arange(shards) ^ 1]], axis=1)
        owners = own(jnp.asarray(both))
        early_at = len(last + middle)

        def own_facts(stream):
            stream_f = stream.astype(jnp.float32)
            share = jnp.where(lax.axis_index("tp") == 0, 1.0, 0.0)
            return jnp.stack(
                [
                    jnp.sum(stream_f * stream_f, axis=-1),
                    jnp.sum(stream_f * head, axis=-1),
                    (rewards - 0.2 * kl_terms) * share,
                    resets.astype(jnp.float32) * share,
                ]
            )

        def early_own(have):
            sum_squares, along, step_reward, cut = (have["facts"][:, k] for k in range(4))
            scale = lax.rsqrt(sum_squares / width + EPSILON)
            values = scale * along
            returns = all_returns(step_reward, cut)
            error = values - returns
            pull = scale**3 * along / width
            coefs = jnp.stack([error * scale, error * pull]).reshape(2, shards * tok)
            coefs = jnp.pad(coefs, ((0, 6), (0, 0)))
            mask = jnp.arange(shards)[:, None] == have["me"]
            row = lambda a: jnp.sum(jnp.where(mask, a, 0.0), axis=0)
            have.update(values=row(values), returns=row(returns), coefs=coefs)
            have["early own"], have["early dstream"], have["early parts"] = product(
                have["owners"], early_at, have["own picks"], (coefs, head_half, [have[b] for b in early])
            )

        def early_other(have):
            have["other sum"], have["middle dstream"], have["middle parts"] = product(
                have["owners"],
                len(last),
                have["other picks"],
                (have["coefs"], head_half, [have[b] for b in middle]),
                [have["early dstream"]],
            )

        where = mine[None].astype(jnp.int32)
        scalars = {"core": mine, "me": me, "first core": mine == 0, "where": where, "elsewhere": 1 - where}
        for n in range(shards.bit_length() - 1):
            low = (me >> n) % 2 == 0
            scalars["low %d" % n] = (jnp.arange(2) == 0) == low if n in (0, 2) else low
        scalars["owners"] = owners
        have = run_plan(stream, hidden, scalars, own_facts, paths, lambda hidden: pick(hidden, owners, tok), early_own, early_other)
        out, dstream, grad_head = product(
            have["owners"],
            0,
            have["other picks"],
            (have["coefs"], head_half, [have[b] for b in last]),
            (),
            have["other sum"],
            [have["early parts"], have["middle parts"]],
        )
        swapped = to_core(out)
        other_head = to_core(grad_head[0])[None]
        (grad_down,) = product(
            have["owners"], 0, have["own picks"], None, [dstream, have["middle dstream"]], have["early own"], (), have["where"]
        )
        grad_down, grad_head = put(grad_down, swapped, have["elsewhere"], grad_head, other_head, gain[None])
        return (have["values"], have["returns"], grad_head[0], grad_down)

    return body


def solution(mesh):
    placed = (P("seq", "tp"), P("seq", None), P("tp"), P("tp"), P("seq"), P("seq"), P("seq"))

    def run(stream, *rest):
        return jax.shard_map(
            make_body(stream.shape[1], mesh.shape["seq"]),
            mesh=mesh,
            in_specs=placed,
            out_specs=(P("seq"), P("seq"), P("tp"), P("seq", "tp")),
            check_vma=False,
        )(stream, *rest)

    return run
```

```python
import functools

import jax
import jax.numpy as jnp
import numpy as np
from jax import lax
from jax.experimental import pallas as pl
from jax.experimental.pallas import tpu as pltpu
from jax.sharding import PartitionSpec as P

EPSILON = 1e-05


def butterfly_sum(x, axis):
    count = lax.axis_size(axis)
    step = 1
    while step < count:
        x = x + lax.ppermute(x, axis, [(i, i ^ step) for i in range(count)])
        step *= 2
    return x


def butterfly_send(x, axis, bit):
    return lax.ppermute(x, axis, [(i, i ^ bit) for i in range(lax.axis_size(axis))])


def butterfly_merge(x, other, bit, low):
    low = low[bit]
    if bit == 1:
        return jnp.where(low[:, None, None], x, other)
    if bit == 4:
        return jnp.where(low[:, None, None, None], x[None], other[None])
    if bit == 2:
        both = jnp.stack([jnp.where(low, x, other), jnp.where(low, other, x)], axis=1)
        return both.reshape(-1, *x.shape[2:])
    return jnp.concatenate([jnp.where(low, x, other), jnp.where(low, other, x)])


class Paths:
    def __init__(self, count):
        self.count = count
        self.m = count // 4
        self.order = list(range(0, self.m, 2)) + list(range(self.m - 1 - self.m % 2, 0, -2))
        self.place = [self.order.index(z) for z in range(self.m)]
        self.across = [(i, i ^ 2) for i in range(count)]
        self.core = [(i, i ^ 1) for i in range(count)]
        self.ring = [self._ring(1), self._ring(-1)]

    def _ring(self, way):
        pairs = []
        for i in range(self.count):
            z, rest = divmod(i, 4)
            by = way if i % 2 == 0 else -way
            pairs.append((i, self.order[(self.place[z] + by) % self.m] * 4 + rest))
        return pairs

    def owners(self, blocks):
        table = np.zeros((self.count, len(blocks)), np.int32)
        for me in range(self.count):
            z, rest = divmod(me, 4)
            for b, (steps, across, kind) in enumerate(blocks):
                way = -1 if (me % 2 == 0) == (kind == 0) else 1
                table[me, b] = self.order[(self.place[z] + way * steps) % self.m] * 4 + (rest ^ (2 * across + kind))
        return table


class Flights:
    def __init__(self, **arrays):
        self.have = arrays

    def event(self, waits, sends=()):
        names = list(dict.fromkeys([*waits, *(source for _, source, _ in sends)]))
        self.have.update(zip(names, lax.optimization_barrier(tuple(self.have[n] for n in names))))
        for name, source, pairs in sends:
            self.have[name] = lax.ppermute(self.have[source], "seq", pairs)


def block_groups(m):
    last = [(m - 1, 1, 0), (m - 1, 1, 1)]
    middle = [(m - 2, 1, 0), (m - 2, 1, 1), (m - 1, 0, 0), (m - 1, 0, 1)]
    early = [(k, a, kind) for k in range(m - 1) for a in range(2) for kind in range(2) if k < m - 2 or a == 0]
    return last, middle, early


def run_plan(stream, hidden, scalars, own_facts, paths, pick_both, early_own, early_other):
    half = stream.shape[1] // 2
    m, ring, across, core = paths.m, paths.ring, paths.across, paths.core
    cut = lambda c: lax.dynamic_slice_in_dim(stream, c * half, half, 1)
    core_index = scalars["core"]
    f = Flights(stream=stream, hidden=hidden, away=cut(1 - core_index), **scalars)
    f.have[0, 0, 0] = cut(core_index)
    have = f.have
    names = list(scalars)
    low = lambda: {1 << n: have["low %d" % n] for n in range(paths.count.bit_length() - 1)}

    bits = [1, 4, 2] + [8 << n for n in range(paths.count.bit_length() - 4)]

    def facts_send():
        have["other facts"] = butterfly_send(have["facts"], "seq", bits[0])

    def facts_merge():
        have["facts"] = butterfly_merge(have["facts"], have["other facts"], bits.pop(0), low())

    def facts_step():
        if bits:
            facts_send()
            facts_merge()

    f.event([], [((1, 0, 0), (0, 0, 0), ring[0]), ((0, 1, 0), (0, 0, 0), across), ((0, 0, 1), "away", core)])
    f.event(
        [(0, 0, 1), "stream", *names],
        [((1, 0, 1), (0, 0, 1), ring[1]), ((0, 1, 1), (0, 0, 1), across)],
    )
    have["facts"] = butterfly_sum(own_facts(have["stream"]), "tp")[None]
    f.event(["facts", "hidden"])
    have["own picks"], have["away picks"] = pick_both(have["hidden"])
    f.event(
        [(1, 0, 0), (0, 1, 0), "facts", "own picks", "away picks"],
        [((2, 0, 0), (1, 0, 0), ring[0]), ((1, 1, 0), (1, 0, 0), across)],
    )
    facts_step()
    facts_send()
    f.event([(1, 0, 1), (0, 1, 1), "facts", "other facts"], [((2, 0, 1), (1, 0, 1), ring[1]), ((1, 1, 1), (1, 0, 1), across)])
    facts_merge()
    for k in range(2, m):
        for kind in range(2):
            facts_step()
            if k < m - 1:
                sends = [((k + 1, 0, kind), (k, 0, kind), ring[kind]), ((k, 1, kind), (k, 0, kind), across)]
            elif kind == 0:
                sends = []
            else:
                sends = [((k, 1, 0), (k - 1, 1, 0), ring[0]), ((k, 1, 1), (k, 0, 1), across)]
            waits = [(k, 0, kind), (k - 1, 1, kind), "facts"]
            if k == m - 2 and kind == 1:
                sends.append(("other picks", "away picks", core))
            if k == m - 1 and kind == 1:
                waits += ["other picks", "early own", "values", "returns"]
            f.event(waits, sends)
            if k == m - 2 and kind == 1:
                while bits:
                    facts_step()
                early_own(have)
    early_other(have)
    f.event([(m - 1, 1, 0), (m - 1, 1, 1), "other sum"])
    return have


def params(tokens):
    return pltpu.CompilerParams(vmem_limit_bytes=(9 if tokens <= 4096 else 40) * 1024 * 1024)


def cost(units, k, width, extra):
    return pl.CostEstimate(
        flops=2 * units * k * width, bytes_accessed=2 * (units * k + k * width) + extra, transcendentals=0
    )


def pieces_of(units):
    return next(n for n in (7, 4, 2, 1) if units % (16 * n) == 0)


def pick_kernel(tok, owners, hidden, own, away, held, turned, sems_in, sems_out):
    units, tokens = hidden.shape
    count = tokens // tok
    pieces = pieces_of(units)
    size = units // pieces
    rows = [pl.ds(n * size, size) for n in range(pieces)]
    fetch = [pltpu.make_async_copy(hidden.at[r, :], held.at[r, :], sems_in.at[n]) for n, r in enumerate(rows)]
    place = [pltpu.make_async_copy(turned.at[r, :], away.at[r, :], sems_out.at[n]) for n, r in enumerate(rows)]
    for copy in fetch:
        copy.start()
    for n, r in enumerate(rows):
        fetch[n].wait()
        for m, out in enumerate((own, turned)):
            for b in range(count):
                columns = pl.ds(pl.multiple_of(owners[m * count + b] * tok, tok), tok)
                out[r, b * tok : (b + 1) * tok] = held[r, columns]
        place[n].start()
    for copy in place:
        copy.wait()


def pick(hidden, owners, tok):
    inside = pl.BlockSpec(memory_space=pltpu.VMEM)
    anywhere = pl.BlockSpec(memory_space=pl.ANY)
    pieces = pieces_of(hidden.shape[0])
    return pl.pallas_call(
        functools.partial(pick_kernel, tok),
        grid_spec=pltpu.PrefetchScalarGridSpec(
            num_scalar_prefetch=1,
            grid=(),
            in_specs=[anywhere],
            out_specs=[inside, anywhere],
            scratch_shapes=[pltpu.VMEM(hidden.shape, hidden.dtype)] * 2 + [pltpu.SemaphoreType.DMA((pieces,))] * 2,
        ),
        out_shape=[pltpu.VMEM(hidden.shape, hidden.dtype), pltpu.HBM(hidden.shape, hidden.dtype)],
        compiler_params=params(hidden.shape[1]),
        cost_estimate=cost(0, 0, 0, 1),
    )(owners, pltpu.with_memory_space_constraint(hidden, pltpu.HBM))


def spread(tok, owners, first, coefs, weights, pulls):
    for b in range(weights.shape[0] // tok):
        coef = coefs[:, pl.ds(pl.multiple_of(owners[first + b] * tok, tok), tok)].T
        rows = slice(b * tok, (b + 1) * tok)
        weights[rows, :] = jnp.broadcast_to(coef[:, 0:1], (tok, 128))
        pulls[rows, :] = jnp.broadcast_to(coef[:, 1:2], (tok, 128))


def form(tok, owners, first, weights, pulls, head, blocks, dstream, parts, start, chunk):
    for b in range(len(blocks)):
        rows = slice(b * tok, (b + 1) * tok)
        for at in range(0, chunk, 128):
            lanes = slice(start + at, start + at + 128)
            stream_f = blocks[b][:, lanes].astype(jnp.float32)
            weight = weights[rows, :]
            dstream[rows, lanes] = (weight * head[:, lanes] - pulls[rows, :] * stream_f).astype(jnp.bfloat16)
            parts[owners[first + b], :, lanes] = jnp.sum(weight * stream_f, axis=0, keepdims=True)


def product_kernel(tok, count, first, given_count, added, parts_count, wide, chunk, owners, where, *refs):
    refs = list(refs)
    take = lambda n: [refs.pop(0) for _ in range(n)]
    (picked,) = take(1)
    coefs, head = take(2) if count else (None, None)
    blocks, given, total, other_parts = take(count), take(given_count), take(added), take(parts_count)
    (out,) = take(1)
    dstream, parts_out = take(2) if count else (None, None)
    weights, pulls, parts = take(3) if count else (None, None, None)
    out_v = take(1)[0] if wide else out
    (sem_out,) = take(1)
    half = out_v.shape[1]
    steps = half // chunk
    base = pl.multiple_of(where[0] * half, half)

    columns = lambda c: pl.ds(c * chunk, chunk)

    def put_out(c):
        there = pl.ds(pl.multiple_of(base + c * chunk, chunk), chunk)
        return pltpu.make_async_copy(out_v.at[:, columns(c)], out.at[:, there], sem_out.at[c])

    if count:
        parts[...] = jnp.zeros_like(parts)
        spread(tok, owners, first, coefs, weights, pulls)

    def form_chunk(c):
        if count and c < steps:
            form(tok, owners, first, weights, pulls, head, blocks, dstream, parts, c * chunk, chunk)

    factors = ([dstream] if count else []) + given
    form_chunk(0)
    for c in range(steps):
        form_chunk(c + 1)
        here = total[0][:, columns(c)] if added else None
        at = first * tok
        for factor in factors:
            depth = factor.shape[0]
            term = jnp.dot(picked[:, at : at + depth], factor[:, columns(c)], preferred_element_type=jnp.float32)
            here = term if here is None else here + term
            at += depth
        out_v[:, columns(c)] = here.astype(out_v.dtype)
        if wide:
            put_out(c).start()
    if count:
        if other_parts:
            parts_out[...] = sum([p[...] for p in other_parts], parts[...]).sum(axis=0)
        else:
            parts_out[...] = parts[...]
    if wide:
        for c in range(steps):
            put_out(c).wait()


def product(owners, first, picked, formed=None, given=(), total=None, parts=(), where=None):
    units, tokens = picked.shape
    coefs, head, blocks = formed or (None, None, [])
    half = blocks[0].shape[1] if blocks else given[0].shape[1]
    count = len(blocks)
    tok = tokens // owners.shape[0] * 2
    k = count * tok + sum(g.shape[0] for g in given)
    chunk = next(t for t in (1024 if tokens <= 4096 else 256, 512, 128, half) if half % t == 0)
    steps = half // chunk
    added, wide = total is not None, where is not None
    anywhere = pl.BlockSpec(memory_space=pl.ANY)
    inside = pl.BlockSpec(memory_space=pltpu.VMEM)
    in_vmem = lambda x: pltpu.with_memory_space_constraint(x, pltpu.VMEM)
    out_type = jnp.bfloat16 if added else jnp.float32
    if wide:
        out_specs = [anywhere]
        out_shape = [jax.ShapeDtypeStruct((units, 2 * half), out_type)]
    else:
        out_specs = [inside]
        out_shape = [pltpu.VMEM((units, half), out_type)]
    scratch = []
    parts_shape = (tokens // tok, 1, half)
    if count:
        out_specs += [inside, inside]
        out_shape += [
            pltpu.VMEM((count * tok, half), jnp.bfloat16),
            jax.ShapeDtypeStruct(parts_shape[1:] if parts else parts_shape, jnp.float32),
        ]
        scratch += [pltpu.VMEM((count * tok, 128), jnp.float32)] * 2 + [pltpu.VMEM(parts_shape, jnp.float32)]
    if wide:
        scratch += [pltpu.VMEM((units, half), out_type)]
    sems = [(steps,)]
    return pl.pallas_call(
        functools.partial(product_kernel, tok, count, first, len(given), int(added), len(parts), wide, chunk),
        grid_spec=pltpu.PrefetchScalarGridSpec(
            num_scalar_prefetch=2,
            grid=(),
            in_specs=[inside] * (1 + 2 * bool(count) + count + len(given) + added + len(parts)),
            out_specs=out_specs,
            scratch_shapes=scratch + [pltpu.SemaphoreType.DMA(shape) for shape in sems],
        ),
        out_shape=out_shape,
        compiler_params=params(tokens),
        cost_estimate=cost(units, k * (1 if added or given else 10), half, 6 * units * half),
    )(
        owners,
        where if wide else jnp.zeros((1,), jnp.int32),
        in_vmem(picked),
        *([coefs, head] if count else []),
        *[in_vmem(x) for x in blocks],
        *[in_vmem(x) for x in given],
        *([in_vmem(total)] if added else []),
        *parts,
    )


def put_kernel(pieces, where, part, whole, out, sems):
    units, width = part.shape
    start = pl.multiple_of(where[0] * width, width)
    rows = [pl.ds(n * (units // pieces), units // pieces) for n in range(pieces)]
    place = [
        pltpu.make_async_copy(part.at[r, :], out.at[r, pl.ds(start, width)], sems.at[n]) for n, r in enumerate(rows)
    ]
    for copy in place:
        copy.start()
    for copy in place:
        copy.wait()


def put(whole, part, where):
    units, width = part.shape
    pieces = pieces_of(units)
    anywhere = pl.BlockSpec(memory_space=pl.ANY)
    return pl.pallas_call(
        functools.partial(put_kernel, pieces),
        grid_spec=pltpu.PrefetchScalarGridSpec(
            num_scalar_prefetch=1,
            grid=(),
            in_specs=[pl.BlockSpec(memory_space=pltpu.VMEM), anywhere],
            out_specs=anywhere,
            scratch_shapes=[pltpu.SemaphoreType.DMA((pieces,))],
        ),
        out_shape=jax.ShapeDtypeStruct(whole.shape, whole.dtype),
        input_output_aliases={2: 0},
        compiler_params=params(0),
        cost_estimate=cost(0, 0, 0, 4 * units * width),
    )(where, pltpu.with_memory_space_constraint(part, pltpu.VMEM), whole)


def all_returns(step_reward, resets):
    shards, tok = step_reward.shape
    position = jnp.arange(tok)
    earlier = position[None, :] < position[:, None]
    before = jnp.sum(jnp.where(earlier[None], resets[:, None, :], 0.0), axis=2)
    total = jnp.sum(resets, axis=1, keepdims=True)
    reach = (position[None, :] >= position[:, None])[None] & (before[:, None, :] == before[:, :, None])
    local = jnp.sum(jnp.where(reach, step_reward[:, None, :], 0.0), axis=2)
    passing = before == total
    blocked = jnp.where(passing[:, 0], 0.0, 1.0)
    ids = jnp.arange(shards)
    later = ids[None, :] > ids[:, None]
    between = later[:, None, :] & (ids[None, :] < ids[:, None])[None]
    open_path = later & (jnp.sum(jnp.where(between, blocked[None, None, :], 0.0), axis=2) == 0.0)
    incoming = jnp.sum(jnp.where(open_path, local[None, :, 0], 0.0), axis=1)
    return local + jnp.where(passing, incoming[:, None], 0.0)


def make_body(width, shards):
    paths = Paths(shards)

    def body(stream, hidden, final_gain, value_head, rewards, kl_terms, resets):
        tok, local = stream.shape
        half = local // 2
        me = lax.axis_index("seq")
        mine = me % 2
        gain = final_gain.astype(jnp.float32)
        head = gain * value_head.astype(jnp.float32)
        head_half = lax.dynamic_slice_in_dim(head, mine * half, half)[None]
        to_core = lambda x: lax.ppermute(x, "seq", paths.core)
        own = lambda a: lax.dynamic_index_in_dim(a, me, 0, keepdims=False)
        last, middle, early = block_groups(paths.m)
        table = paths.owners(last + middle + early)
        both = np.concatenate([table, table[np.arange(shards) ^ 1]], axis=1)
        owners = own(jnp.asarray(both))
        early_at = len(last + middle)

        def own_facts(stream):
            stream_f = stream.astype(jnp.float32)
            share = jnp.where(lax.axis_index("tp") == 0, 1.0, 0.0)
            return jnp.stack(
                [
                    jnp.sum(stream_f * stream_f, axis=-1),
                    jnp.sum(stream_f * head, axis=-1),
                    (rewards - 0.2 * kl_terms) * share,
                    resets.astype(jnp.float32) * share,
                ]
            )

        def early_own(have):
            sum_squares, along, step_reward, cut = (have["facts"][:, k] for k in range(4))
            scale = lax.rsqrt(sum_squares / width + EPSILON)
            values = scale * along
            returns = all_returns(step_reward, cut)
            error = values - returns
            pull = scale**3 * along / width
            coefs = jnp.stack([error * scale, error * pull]).reshape(2, shards * tok)
            coefs = jnp.pad(coefs, ((0, 6), (0, 0)))
            mask = jnp.arange(shards)[:, None] == have["me"]
            row = lambda a: jnp.sum(jnp.where(mask, a, 0.0), axis=0)
            have.update(values=row(values), returns=row(returns), coefs=coefs)
            have["early own"], have["early dstream"], have["early parts"] = product(
                have["owners"], early_at, have["own picks"], (coefs, head_half, [have[b] for b in early])
            )

        def early_other(have):
            have["other sum"], have["middle dstream"], have["middle parts"] = product(
                have["owners"],
                len(last),
                have["other picks"],
                (have["coefs"], head_half, [have[b] for b in middle]),
                [have["early dstream"]],
            )

        where = mine[None].astype(jnp.int32)
        scalars = {"core": mine, "me": me, "first core": mine == 0, "where": where, "elsewhere": 1 - where}
        for n in range(shards.bit_length() - 1):
            low = (me >> n) % 2 == 0
            scalars["low %d" % n] = (jnp.arange(2) == 0) == low if n in (0, 2) else low
        scalars["owners"] = owners
        have = run_plan(stream, hidden, scalars, own_facts, paths, lambda hidden: pick(hidden, owners, tok), early_own, early_other)
        out, dstream, grad_head = product(
            have["owners"],
            0,
            have["other picks"],
            (have["coefs"], head_half, [have[b] for b in last]),
            (),
            have["other sum"],
            [have["early parts"], have["middle parts"]],
        )
        swapped = to_core(out)
        grad_head = grad_head[0]
        other_head = to_core(grad_head)
        grad_head = gain * jnp.where(
            have["first core"], jnp.concatenate([grad_head, other_head]), jnp.concatenate([other_head, grad_head])
        )
        (grad_down,) = product(
            have["owners"], 0, have["own picks"], None, [dstream, have["middle dstream"]], have["early own"], (), have["where"]
        )
        grad_down = put(grad_down, swapped, have["elsewhere"])
        return (have["values"], have["returns"], grad_head, grad_down)

    return body


def solution(mesh):
    placed = (P("seq", "tp"), P("seq", None), P("tp"), P("tp"), P("seq"), P("seq"), P("seq"))

    def run(stream, *rest):
        return jax.shard_map(
            make_body(stream.shape[1], mesh.shape["seq"]),
            mesh=mesh,
            in_specs=placed,
            out_specs=(P("seq"), P("seq"), P("tp"), P("seq", "tp")),
            check_vma=False,
        )(stream, *rest)

    return run
```
